32 devices in a mesh: rep: 2 (over core), sq: 16 (over z, y, x).
Axes of the slice: x: 2, y: 2, z: 4, core: 2. Of those that a mesh axis runs over, the one named last changes fastest.
Arguments:
- inputs: bfloat16 [4, 1024, 768], P('rep', 'sq'), may hold values from -6 to 6
- w_query: bfloat16 [768, 768], P('sq'), may hold values from -0.21875 to 0.21875
- w_key: bfloat16 [768, 768], P('sq'), may hold values from -0.21875 to 0.21875
- w_value: bfloat16 [768, 768], P('sq'), may hold values from -0.21875 to 0.21875
- w_out: bfloat16 [768, 768], P('sq'), may hold values from -1.75 to 1.75
- table: bfloat16 [32, 12], P('sq'), may hold values from -4 to 4
- gain_one: bfloat16 [768], P('sq'), may hold values from 0.5 to 1.5
- gain_two: bfloat16 [768], P('sq'), may hold values from 0.5 to 1.5
- w_router: bfloat16 [768, 8], P('sq'), may hold values from -0.109375 to 0.109375
- w_up: bfloat16 [768, 24576], P(None, 'sq'), may hold values from -0.21875 to 0.21875
- w_down: bfloat16 [24576, 768], P('sq'), may hold values from -1.25 to 1.25
- routes: int32 [4, 1024, 1], P('rep', 'sq'), may hold values from 0 to 7; in each aligned block of 64 rows (0 to 63, 64 to 127, ..., all dimensions but the last counted through in order) at most 16 rows name the same one
- segments: int32 [4, 1024], P('rep', 'sq'), may hold values from 0 to 1, as said below
- cotangent: bfloat16 [4, 1024, 768], P('rep', 'sq'), may hold values from -6 to 6
Outputs:
- output: bfloat16 [4, 1024, 768], P('rep', 'sq')
- input_grad: float32 [4, 1024, 768], P('rep', 'sq')
- query_grad: float32 [768, 768], P('sq')
- key_grad: float32 [768, 768], P('sq')
- value_grad: float32 [768, 768], P('sq')
- out_grad: float32 [768, 768], P('sq')
- table_grad: float32 [32, 12], P('sq')
- gain_one_grad: float32 [768], P('sq')
- gain_two_grad: float32 [768], P('sq')
- router_grad: float32 [768, 8], P('sq')
- up_grad: float32 [768, 24576], P(None, 'sq')
- down_grad: float32 [24576, 768], P('sq')
The draws below stay inside these ranges and needn't reach their ends.
Inputs may be any that keep to these rules, and one draw needn't show every extreme that they name: `routes`: in each aligned block of 64 rows (one sequence's positions on one device), at most 16 tokens name the same expert. `segments`: segment numbers count a sequence's documents from 0 and never fall along it. Of sequences 2 k and 2 k + 1, one is a single document and the other holds 2 documents.
All inputs are finite; a program needn't handle non-finite values.
Results may differ from the reference program's by a relative error of at most 0.03.
Values may be sent and summed in bfloat16 or wider, within the bound.
No kernel may reach another device: no remote copies, remote signals or barrier semaphores. Data moves between devices by JAX's collectives and lax.ppermute only.
A program may use at most 192 MiB of HBM per device.

```python
import math
import jax
import jax.numpy as jnp
import numpy as np
from jax import lax

D = 768
HEADS = 12
HEAD_DIM = 64
FF = 3072
BUCKETS = 32
EXPERTS = 8
SEQ_DEV = 64
MOST = 16
SEQS = 4
LEN = 1024
DOCS = 2


def draw_segments(key, part):
    key = jax.random.fold_in(key, 7)
    pick_key, cut_key = jax.random.split(key)
    single = jax.random.randint(pick_key, (SEQS // 2,), 0, 2)
    span = LEN // DOCS
    jitter = span // 4
    offsets = jax.random.randint(cut_key, (SEQS, DOCS - 1), -jitter, jitter + 1)
    cuts = jnp.arange(1, DOCS, dtype=jnp.int32)[None, :] * span + offsets
    positions = jnp.arange(LEN, dtype=jnp.int32)
    counted = jnp.sum((positions[None, :, None] >= cuts[:, None, :]).astype(jnp.int32), axis=-1)
    whole = jnp.arange(SEQS, dtype=jnp.int32) % 2 == jnp.repeat(single, 2)
    return jnp.where(whole[:, None], 0, counted).astype(jnp.int32)


def levels(rng, shape, cuts, low, top_value):
    factor_of = 1.0
    for axis_at, parts in cuts:
        heights = jax.random.uniform(jax.random.fold_in(jax.random.fold_in(rng, 6), axis_at), (parts,), jnp.float32, low / len(cuts), top_value / len(cuts))
        factor_of = factor_of * jnp.repeat(jnp.exp(heights), shape[axis_at] // parts).reshape((-1,) + (1,) * (len(shape) - 1 - axis_at))
    return factor_of


def deal_out(rng, own, number, rows, amount, top, reach, lean):
    ranking = jax.random.permutation(rng, amount)
    heavy_load, ordinary = load_shares(amount, rows * top, reach, lean, True), load_shares(amount, rows * top, reach, lean, False)
    places = jnp.arange(amount)

    def named(lengths, offset_by):
        used = int((lengths > 0).sum())
        fixed = max(1, used // 4)
        passed = fixed + (places - fixed + offset_by * (used - fixed)) % max(1, amount - fixed)
        return jnp.zeros((amount,), jnp.int32).at[ranking[jnp.where(places < fixed, places, passed)]].set(jnp.asarray(lengths, jnp.int32))

    lengths = jnp.where(number % 4 == 0, named(heavy_load, number // 4), named(ordinary, number - number // 4 - 1))
    mixed = jax.random.permutation(jax.random.fold_in(own, 3), amount)
    donor, sink = mixed[0:amount // 2 * 2:2], mixed[1:amount // 2 * 2:2]
    margin = jnp.minimum(lengths[donor] - 1, reach - lengths[sink]) // 2
    margin = jnp.where((donor == ranking[0]) | (sink == ranking[0]) | (lengths[sink] == 0), 0, jnp.maximum(margin, 0))
    passed = jax.random.randint(jax.random.fold_in(own, 4), (amount // 2,), 0, 1 << 20) % (margin + 1)
    lengths = lengths.at[donor].add(-passed).at[sink].add(passed)
    labels = jnp.searchsorted(jnp.cumsum(lengths), jnp.arange(rows * top), side="right").astype(jnp.int32)
    grid = labels.reshape(top, rows).T
    grid = grid[jax.random.permutation(jax.random.fold_in(own, 1), rows)]
    offset_by = jax.random.randint(jax.random.fold_in(own, 2), (rows, 1), 0, top)
    return jnp.take_along_axis(grid, (jnp.arange(top)[None, :] + offset_by) % top, axis=1)


def load_shares(count, total, bound, lean, full):
    portions = [(1 << 20) // math.isqrt(standing ** lean) + 1 for standing in range(1, count + 1)]
    largest = bound if full else min(bound, max(-(-total // count), total * portions[0] // sum(portions)))
    least = 1 if total - largest >= count - 1 else 0
    given, surplus = [largest] + [least] * (count - 1), total - largest - least * (count - 1)
    while surplus > 0:
        free = [i for i in range(1, count) if given[i] < largest] or [i for i in range(1, count) if given[i] < bound]
        whole, remaining = sum([portions[i] for i in free]), surplus
        for i in free:
            addition = min(bound - given[i], max(1, remaining * portions[i] // whole), surplus)
            given[i] = given[i] + addition
            surplus = surplus - addition
    return np.array(given)


def noise(rng, extent, deviation, limit, cuts=(), kind=jnp.bfloat16):
    loudness = levels(rng, extent, cuts, -0.22, 0.18) if cuts else 1.0
    values = jax.random.normal(rng, extent, jnp.float32) * deviation * loudness
    return jnp.minimum(jnp.maximum(values, -limit), limit).astype(kind)


def setup_inputs(seed: int = 0) -> dict:
    key_list = jax.random.split(jax.random.key(seed), 15)
    inputs = noise(key_list[0], (SEQS, LEN, D), 1.0, 6.0, ((0, 2), (1, 16)))
    w_query = noise(key_list[1], (D, D), D ** -0.5, 0.21875, ((0, 16),))
    w_key = noise(key_list[2], (D, D), D ** -0.5, 0.21875, ((0, 16),))
    w_value = noise(key_list[3], (D, D), D ** -0.5, 0.21875, ((0, 16),))
    w_out = noise(key_list[4], (D, D), (D // 64) ** -0.5, 1.75, ((0, 16),))
    table = noise(key_list[5], (BUCKETS, HEADS), 1.0, 4.0, ((0, 16),))
    gain_one = jnp.clip(1.0 + 0.1 * jax.random.normal(key_list[6], (D,), jnp.float32), 0.5, 1.5).astype(jnp.bfloat16)
    gain_two = jnp.clip(1.0 + 0.1 * jax.random.normal(key_list[7], (D,), jnp.float32), 0.5, 1.5).astype(jnp.bfloat16)
    w_router = noise(key_list[8], (D, EXPERTS), (4 * D) ** -0.5, 0.109375, ((0, 16),))
    w_up = noise(key_list[9], (D, EXPERTS * FF), D ** -0.5, 0.21875, ((1, 16),))
    w_down = noise(key_list[10], (EXPERTS * FF, D), (max(FF // 128, 1)) ** -0.5, 1.25, ((0, 16),))
    routes_keys = jax.random.split(jax.random.fold_in(key_list[11], 1), SEQS * LEN // SEQ_DEV)
    routes_turns = jax.random.permutation(jax.random.fold_in(key_list[11], 3), SEQS * LEN // SEQ_DEV)
    routes = jax.vmap(lambda own, number: deal_out(jax.random.fold_in(key_list[11], 2), own, number, SEQ_DEV, EXPERTS, 1, MOST, 1))(routes_keys, routes_turns).reshape((SEQS, LEN, 1))
    segments = draw_segments(jax.random.fold_in(key_list[14], 71), 0)
    cotangent = noise(key_list[13], (SEQS, LEN, D), 1.0, 6.0, ((0, 2), (1, 16)))
    return dict(inputs=inputs, w_query=w_query, w_key=w_key, w_value=w_value, w_out=w_out, table=table, gain_one=gain_one, gain_two=gain_two, w_router=w_router, w_up=w_up, w_down=w_down, routes=routes, segments=segments, cotangent=cotangent)


@jax.custom_vjp
def low(v):
    return lax.optimization_barrier(v.astype(jnp.bfloat16)).astype(jnp.float32)

@jax.custom_vjp
def low_back(v):
    return v

def low_keep(v):
    return (low(v), None)

def low_pass(kept, grad):
    return (grad,)

def back_keep(v):
    return (v, None)

def back_low(kept, grad):
    return (low(grad),)
low.defvjp(low_keep, low_pass)
low_back.defvjp(back_keep, back_low)
EPS = 1e-06
NEGATIVE = -1e+30
LIMITS = (1, 2, 3, 4, 5, 6, 7, 8, 12, 16, 23, 32, 46, 64, 91)
HIGH = lax.Precision.HIGHEST

def buckets(relative):
    magnitude = jnp.abs(relative)
    counted = (relative > 0).astype(jnp.int32) * 16
    for threshold in LIMITS:
        counted = counted + (magnitude >= threshold).astype(jnp.int32)
    return counted

def rms_norm(values, gain):
    return values * lax.rsqrt(lax.optimization_barrier(jnp.mean(values * values, axis=-1, keepdims=True)) + EPS) * gain

def sequence_forward(params, inputs, routes, segments):
    w_query, w_key, w_value, w_out, table, gain_one, gain_two, w_router, w_up, w_down = params
    normed = low(rms_norm(inputs, gain_one))

    def project(weight):
        return low(low_back(jnp.dot(normed, weight, precision=HIGH))).reshape(LEN, HEADS, HEAD_DIM)
    queries = project(w_query)
    keys = project(w_key)
    values = project(w_value)
    positions = jnp.arange(LEN, dtype=jnp.int32)
    block = min(512, LEN)

    def attend(start):
        rows = lax.dynamic_slice_in_dim(queries, start, block, 0)
        row_pos = start + jnp.arange(block, dtype=jnp.int32)
        row_seg = lax.dynamic_slice_in_dim(segments, start, block, 0)
        bias = jnp.take(table, buckets(positions[None, :] - row_pos[:, None]), axis=0)
        scores = jnp.einsum('qhd,khd->hqk', rows, keys, precision=HIGH) * HEAD_DIM ** (-0.5)
        scores = low_back(scores + jnp.transpose(bias, (2, 0, 1)))
        same = row_seg[:, None] == segments[None, :]
        scores = jnp.where(same[None], scores, NEGATIVE)
        weights = low(jax.nn.softmax(scores, axis=-1))
        return jnp.einsum('hqk,khd->qhd', weights, values, precision=HIGH)
    starts = jnp.arange(LEN // block, dtype=jnp.int32) * block
    mixed = lax.map(jax.checkpoint(attend), starts).reshape(LEN, D)
    attended = low(low_back(mixed))
    hidden = inputs + low_back(jnp.dot(attended, w_out, precision=HIGH))
    normed_two = low(rms_norm(hidden, gain_two))
    router_probs = jax.nn.softmax(jnp.dot(normed_two, w_router, precision=HIGH), axis=-1)
    chosen = routes[:, 0]
    picked = (chosen[:, None] == jnp.arange(EXPERTS, dtype=jnp.int32)[None, :]).astype(jnp.float32)
    gate = lax.optimization_barrier(jnp.sum(router_probs * picked, axis=-1))
    sorting = jnp.argsort(chosen)
    inverse = jnp.argsort(sorting)
    group_sizes = lax.optimization_barrier(jnp.sum(picked, axis=0)).astype(jnp.int32)
    up_stack = jnp.transpose(w_up.reshape(D, EXPERTS, FF), (1, 0, 2))
    down_stack = w_down.reshape(EXPERTS, FF, D)
    pre = low_back(lax.ragged_dot(normed_two[sorting], up_stack, group_sizes, precision=HIGH))
    act = low(jax.nn.gelu(pre, approximate=True))
    expert_out = low_back(lax.ragged_dot(act, down_stack, group_sizes, precision=HIGH)[inverse])
    return hidden + gate[:, None] * expert_out

def reference(inputs, w_query, w_key, w_value, w_out, table, gain_one, gain_two, w_router, w_up, w_down, routes, segments, cotangent):
    params = tuple((weight.astype(jnp.float32) for weight in (w_query, w_key, w_value, w_out, table, gain_one, gain_two, w_router, w_up, w_down)))

    def forward(values, weights):

        def per_sequence(carry, pieces):
            return (carry, jax.checkpoint(sequence_forward)(weights, pieces[0], pieces[1], pieces[2]))
        _, result = lax.scan(per_sequence, jnp.zeros((), jnp.float32), (values, routes, segments))
        return result
    output, pull = jax.vjp(forward, inputs.astype(jnp.float32), params)
    input_grad, weight_grads = pull(cotangent.astype(jnp.float32))
    return (output.astype(jnp.bfloat16), input_grad, weight_grads[0], weight_grads[1], weight_grads[2], weight_grads[3], weight_grads[4], weight_grads[5], weight_grads[6], weight_grads[7], weight_grads[8], weight_grads[9])
```

```python
from functools import partial

import jax
import jax.numpy as jnp
from jax import lax
from jax.experimental import pallas as pl
from jax.experimental.pallas import tpu as pltpu
from jax.sharding import PartitionSpec as P

EXPERTS = 8
CAP = 32
HEAD_GROUPS = 4
EPS = 1e-06
NEGATIVE = -1e30
LIMITS = (1, 2, 3, 4, 5, 6, 7, 8, 12, 16, 23, 32, 46, 64, 91)
LANES = 128
f32 = jnp.float32
bf16 = jnp.bfloat16


def dot(a, b, dims=((1,), (0,))):
    return lax.dot_general(a, b, (dims, ((), ())), preferred_element_type=f32)


def relative_tile(offset, shape, rows, sub):
    row = lax.broadcasted_iota(jnp.int32, shape, 0)
    col = lax.broadcasted_iota(jnp.int32, shape, 1)
    return col - LANES - (rows * (row // sub) + offset + row % sub)


def forward_kernel(
    place_ref,
    table_ref,
    own_ref,
    other_ref,
    weight_ref,
    gain_ref,
    seg_key_ref,
    seg_query_ref,
    attended_ref,
    probs_ref,
    query_ref,
    pair_ref,
    normed_ref,
    normed_all,
    project,
    scores,
    strip,
    *,
    groups,
    half,
    rows,
    sub,
    head_dim,
):
    core_at = pl.multiple_of(place_ref[0], half)
    other_at = pl.multiple_of(half - place_ref[0], half)
    query_at = pl.multiple_of(place_ref[1], sub)
    width = gain_ref.shape[1]
    length = groups * rows
    heads = attended_ref.shape[1] // head_dim
    head_width = heads * head_dim
    per = LANES // rows
    tile = per * sub
    steps = length // LANES
    gain = gain_ref[...]

    def norm(x):
        x = x.astype(f32)
        scale = lax.rsqrt(jnp.mean(x * x, axis=-1, keepdims=True) + EPS)
        return ((x * scale) * gain).astype(bf16)

    def norm_step(p, carry):
        own = norm(own_ref[p, 0:half, :])
        normed_ref[p] = own
        normed_all[p, pl.ds(core_at, half), :] = own
        normed_all[p, pl.ds(other_at, half), :] = norm(other_ref[p, 0:half, :])
        return carry

    lax.fori_loop(0, groups, norm_step, 0)
    chunk = 4

    def project_step(c, carry):
        block = normed_all[pl.ds(c * chunk, chunk)].reshape(chunk * rows, width)
        result = dot(block, weight_ref[...]).astype(bf16)
        project[pl.ds(c * chunk, chunk)] = result.reshape(chunk, rows, 3 * head_width)
        pair_ref[pl.ds(c * chunk * rows, chunk * rows), :] = result[:, head_width:]
        return carry

    lax.fori_loop(0, groups // chunk, project_step, 0)

    def query_step(p, carry):
        query_ref[pl.ds(p * sub, sub), :] = project[p, pl.ds(query_at, sub), 0:head_width]
        return carry

    lax.fori_loop(0, groups, query_step, 0)
    factor = head_dim ** (-0.5)
    left = length - 2 * LANES
    right = length + LANES
    relative = relative_tile(place_ref[1], (tile, 3 * LANES), rows, sub)
    magnitude = jnp.abs(relative)
    for h in range(heads):
        at = h * head_dim
        bias = jnp.where(relative > 0, table_ref[16, h], table_ref[0, h])
        for k, threshold in enumerate(LIMITS):
            value = jnp.where(relative > 0, table_ref[17 + k, h], table_ref[1 + k, h])
            bias = jnp.where(magnitude >= threshold, value, bias)
        strip[:, 0:left] = jnp.full((tile, left), table_ref[15, h], f32)
        strip[:, left:right] = bias
        strip[:, right:] = jnp.full((tile, strip.shape[1] - right), table_ref[31, h], f32)
        scores[...] = (
            dot(query_ref[:, at : at + head_dim], pair_ref[:, at : at + head_dim], ((1,), (1,)))
            * factor
        )

        def soft_step(qb, carry):
            start = pl.multiple_of(length - LANES - qb * LANES, LANES)
            for par in range(per):
                here = pl.ds(qb * tile + par * sub, sub)
                value = scores[here, :] + strip[par * sub : (par + 1) * sub, pl.ds(start, length)]
                same = seg_query_ref[here, :] == seg_key_ref[...]
                value = jnp.where(same, value, NEGATIVE)
                top = jnp.max(value, axis=-1, keepdims=True)
                value = jnp.exp(value - top)
                total = jnp.sum(value, axis=-1, keepdims=True)
                probs_ref[h, here, :] = (value * (1.0 / total)).astype(bf16)
            return carry

        lax.fori_loop(0, steps, soft_step, 0)
        attended_ref[:, at : at + head_dim] = dot(
            probs_ref[h], pair_ref[:, head_width + at : head_width + at + head_dim]
        ).astype(bf16)


def backward_kernel(
    place_ref,
    probs_ref,
    query_ref,
    pair_ref,
    grad_ref,
    d_query_ref,
    d_own_ref,
    d_other_ref,
    table_ref,
    scores,
    low,
    strip,
    flipped,
    turned,
    *,
    groups,
    half,
    rows,
    sub,
    head_dim,
):
    core_at = pl.multiple_of(place_ref[0], half)
    other_at = pl.multiple_of(half - place_ref[0], half)
    length = groups * rows
    head_width = query_ref.shape[1]
    heads = head_width // head_dim
    per = LANES // rows
    tile = per * sub
    steps = length // LANES
    factor = head_dim ** (-0.5)
    left = length - 2 * LANES
    right = length + LANES
    relative = relative_tile(place_ref[1], (tile, 3 * LANES), rows, sub)
    magnitude = jnp.abs(relative)
    count = jnp.zeros_like(relative)
    for threshold in LIMITS:
        count = count + (magnitude >= threshold).astype(jnp.int32)
    bucket = count + jnp.where(relative > 0, 16, 0)

    def lanes_sum(value):
        value = jnp.sum(value, axis=0, keepdims=True)
        total = value[:, 0:LANES]
        for k in range(1, value.shape[1] // LANES):
            total = total + value[:, k * LANES : (k + 1) * LANES]
        return total

    for h in range(heads):
        at = h * head_dim
        grad = grad_ref[:, at : at + head_dim]
        scores[...] = dot(
            grad, pair_ref[:, head_width + at : head_width + at + head_dim], ((1,), (1,))
        )
        strip[...] = jnp.zeros_like(strip)

        def score_step(qb, carry):
            start = pl.multiple_of(length - LANES - qb * LANES, LANES)
            for par in range(per):
                here = pl.ds(qb * tile + par * sub, sub)
                probs = probs_ref[h, here, :].astype(f32)
                value = scores[here, :]
                delta = jnp.sum(probs * value, axis=-1, keepdims=True)
                value = probs * (value - delta)
                low[here, :] = value.astype(bf16)
                strip[par * sub : (par + 1) * sub, pl.ds(start, length)] += value
            return carry

        lax.fori_loop(0, steps, score_step, 0)
        d_query_ref[:, at : at + head_dim] = (
            dot(low[...], pair_ref[:, at : at + head_dim]) * factor
        ).astype(bf16)
        flipped[at : at + head_dim, :] = (
            dot(query_ref[:, at : at + head_dim], low[...], ((0,), (0,))) * factor
        )
        flipped[head_width + at : head_width + at + head_dim, :] = dot(
            grad, probs_ref[h], ((0,), (0,))
        )
        near = strip[:, left:right]
        for b in range(32):
            table_ref[h, b : b + 1, :] = lanes_sum(jnp.where(bucket == b, near, 0.0))
        table_ref[h, 15:16, :] += lanes_sum(strip[:, 0:left])
        table_ref[h, 31:32, :] += lanes_sum(strip[:, right:])
    for c in range(length // LANES):
        block = flipped[:, c * LANES : (c + 1) * LANES]
        turned[c * per : (c + 1) * per] = block.T.reshape(per, rows, 2 * head_width)

    def split_step(p, carry):
        d_own_ref[p] = turned[p, pl.ds(core_at, half), :]
        d_other_ref[p] = turned[p, pl.ds(other_at, half), :].astype(bf16)
        return carry

    lax.fori_loop(0, groups, split_step, 0)


def norm_back(d_normed, unit, scale, gain):
    d_unit = d_normed * gain
    return scale * (d_unit - unit * jnp.mean(d_unit * unit, axis=-1, keepdims=True))


def exchange(value):
    return lax.all_to_all(value, "sq", split_axis=0, concat_axis=0, tiled=True)


def local(
    inputs,
    w_query,
    w_key,
    w_value,
    w_out,
    table,
    gain_one,
    gain_two,
    w_router,
    w_up,
    w_down,
    routes,
    segments,
    cotangent,
):
    seqs, rows, width = inputs.shape
    heads = table.shape[1]
    head_dim = width // heads
    reps = lax.axis_size("rep")
    groups = lax.axis_size("sq")
    length = rows * groups
    tokens = seqs * rows
    share = groups // EXPERTS
    half = rows // 2
    all_seqs = 2 * seqs
    split = groups // (all_seqs * HEAD_GROUPS)
    sub = half // split
    group_heads = heads // HEAD_GROUPS
    head_width = group_heads * head_dim
    shard = w_query.shape[0]
    part = shard // 2
    bucket_rows = table.shape[0]
    core = lax.axis_index("rep") % 2
    me = lax.axis_index("sq")
    group_at = (me // split) % HEAD_GROUPS
    first = core == 0
    pairs = [(i, i ^ 1) for i in range(reps)]

    def swap(value):
        return lax.ppermute(value, "rep", pairs)

    def by_core(own, other, axis):
        return jnp.where(
            first,
            jnp.concatenate([own, other], axis=axis),
            jnp.concatenate([other, own], axis=axis),
        )

    def mine(value, axis, size):
        return lax.dynamic_slice_in_dim(value, core * size, size, axis)

    def yours(value, axis, size):
        return lax.dynamic_slice_in_dim(value, (1 - core) * size, size, axis)

    def over_pairs(value):
        if reps == 2:
            return value
        sets = [list(range(0, reps, 2)), list(range(1, reps, 2))]
        return lax.psum(value, "rep", axis_index_groups=sets)

    out_full = lax.all_gather(w_out, "sq", axis=0, tiled=True)
    x_pair = by_core(mine(inputs, 1, half), swap(yours(inputs, 1, half)), 0)
    seg_low = segments.astype(bf16)
    seg_pair = by_core(seg_low, swap(seg_low), 0)
    w_three = jnp.stack([mine(w, 0, part) for w in (w_query, w_key, w_value)], axis=1)
    w_three = w_three.reshape(part, 3, HEAD_GROUPS, head_width)
    w_send = jnp.transpose(w_three, (2, 0, 1, 3)).reshape(HEAD_GROUPS, part, 3 * head_width)
    spare = width - 3 * head_width

    def widen(value):
        return jnp.pad(value, ((0, 0), (0, spare - value.shape[1])))

    small = jnp.concatenate(
        [
            widen(gain_one[None]),
            widen(gain_two[None]),
            widen(w_router.T),
            widen(table.reshape(1, -1)),
        ],
        axis=0,
    )
    small = jnp.broadcast_to(small[None], (all_seqs,) + small.shape)
    small = jnp.concatenate(
        [small, jnp.pad(seg_pair, ((0, 0), (0, spare - rows)))[:, None, :]], axis=1
    )
    small = jnp.pad(small, ((0, 0), (0, part - small.shape[1]), (0, 0)))

    shape = (all_seqs, HEAD_GROUPS, split)
    lower = jnp.concatenate(
        [
            jnp.broadcast_to(w_send[None, :, None], shape + w_send.shape[1:]),
            jnp.broadcast_to(small[:, None, None], shape + small.shape[1:]),
        ],
        axis=-1,
    )
    send = jnp.concatenate(
        [jnp.broadcast_to(x_pair[:, None, None], shape + x_pair.shape[1:]), lower], axis=3
    ).reshape(groups, half + part, width)
    own = exchange(send)
    other = swap(own)
    w_rows = by_core(own[:, half:, : 3 * head_width], other[:, half:, : 3 * head_width], 1)
    w_group = w_rows.reshape(width, 3 * head_width)
    small_in = own[:, half:, 3 * head_width :]
    gain_one_full = small_in[:, 0, :shard].reshape(1, width).astype(f32)
    gain_two_full = small_in[:, 1, :shard].reshape(1, width).astype(f32)
    router_full = jnp.transpose(small_in[:, 2 : 2 + EXPERTS, :shard], (1, 0, 2)).reshape(
        EXPERTS, width
    )
    shard_table = table.shape[0] * heads
    table_full = small_in[:, 2 + EXPERTS, :shard_table].reshape(groups * bucket_rows, heads)
    table_group = lax.dynamic_slice_in_dim(
        table_full.astype(f32), group_at * group_heads, group_heads, 1
    )
    seg_all = small_in[:, 3 + EXPERTS, :rows].astype(f32)
    query_at = core * half + (me % split) * sub
    seg_query = lax.dynamic_slice_in_dim(seg_all, query_at, sub, 1).reshape(groups * sub, 1)
    place = jnp.stack([core * half, query_at]).astype(jnp.int32)
    queries_count = groups * sub
    tile = (LANES // rows) * sub
    sizes = dict(groups=groups, half=half, rows=rows, sub=sub, head_dim=head_dim)
    smem = pl.BlockSpec(memory_space=pltpu.SMEM)
    vmem = pl.BlockSpec(memory_space=pltpu.VMEM)
    limit = pltpu.CompilerParams(vmem_limit_bytes=56 * 1024 * 1024)
    attended_part, probs, queries, pair, normed_half = pl.pallas_call(
        partial(forward_kernel, **sizes),
        name="attention_forward",
        out_shape=(
            jax.ShapeDtypeStruct((queries_count, head_width), bf16),
            jax.ShapeDtypeStruct((group_heads, queries_count, length), bf16),
            jax.ShapeDtypeStruct((queries_count, head_width), bf16),
            jax.ShapeDtypeStruct((length, 2 * head_width), bf16),
            jax.ShapeDtypeStruct((groups, half, width), bf16),
        ),
        in_specs=[smem, smem] + [vmem] * 6,
        out_specs=[vmem] * 5,
        scratch_shapes=[
            pltpu.VMEM((groups, rows, width), bf16),
            pltpu.VMEM((groups, rows, 3 * head_width), bf16),
            pltpu.VMEM((queries_count, length), f32),
            pltpu.VMEM((tile, 2 * length - LANES), f32),
        ],
        compiler_params=limit,
    )(
        place,
        table_group,
        own,
        other,
        w_group,
        gain_one_full,
        seg_all.reshape(1, length),
        seg_query,
    )
    back = exchange(attended_part.reshape(groups, sub, head_width))
    back = back.reshape(all_seqs, HEAD_GROUPS, split, sub, head_width)
    back = jnp.transpose(back, (0, 2, 3, 1, 4)).reshape(all_seqs, half, width)
    attended = by_core(mine(back, 0, seqs), swap(yours(back, 0, seqs)), 1).reshape(tokens, width)
    x_flat = inputs.reshape(tokens, width).astype(f32)
    scale_one = lax.rsqrt(jnp.mean(x_flat * x_flat, axis=-1, keepdims=True) + EPS)
    unit_one = x_flat * scale_one
    hidden = x_flat + dot(attended, out_full)
    scale_two = lax.rsqrt(jnp.mean(hidden * hidden, axis=-1, keepdims=True) + EPS)
    unit_two = hidden * scale_two
    normed_two = (unit_two * gain_two_full).astype(bf16)
    router_probs = jax.nn.softmax(dot(normed_two, router_full, ((1,), (1,))), axis=-1)
    chosen = routes.reshape(tokens)
    picked_int = (chosen[:, None] == jnp.arange(EXPERTS, dtype=jnp.int32)[None, :]).astype(
        jnp.int32
    )
    picked = picked_int.astype(f32)
    gate = jnp.sum(router_probs * picked, axis=-1)
    slot = jnp.sum((jnp.cumsum(picked_int, axis=0) - 1) * picked_int, axis=-1)
    spot = chosen * CAP + slot
    dispatch = (spot[None, :] == jnp.arange(EXPERTS * CAP, dtype=jnp.int32)[:, None]).astype(bf16)
    d_final = cotangent.reshape(tokens, width).astype(f32)
    d_expert = (gate[:, None] * d_final).astype(bf16)
    both = jnp.concatenate([normed_two, d_expert], axis=1)
    buffer = dot(dispatch, both).astype(bf16).reshape(EXPERTS, 1, CAP, 2, width)
    buffer = jnp.transpose(buffer, (0, 1, 3, 2, 4))
    buffer = jnp.broadcast_to(buffer, (EXPERTS, share, 2, CAP, width)).reshape(
        groups, 2 * CAP, width
    )
    arrived = exchange(buffer)
    received = arrived[:, :CAP].reshape(groups * CAP, width)
    got = arrived[:, CAP:].reshape(groups * CAP, width)
    pre = dot(received, w_up)
    act_value, gelu_pull = jax.vjp(partial(jax.nn.gelu, approximate=True), pre)
    act = act_value.astype(bf16)
    partial_out = dot(act, w_down)
    d_act = dot(got, w_down, ((1,), (1,)))
    d_pre = gelu_pull(d_act)[0].astype(bf16)
    d_rows = dot(d_pre, w_up, ((1,), (1,)))
    results = jnp.concatenate(
        [
            partial_out.astype(bf16).reshape(groups, CAP, width),
            d_rows.astype(bf16).reshape(groups, CAP, width),
        ],
        axis=1,
    )
    returned = exchange(results)
    up_local = dot(received, d_pre, ((0,), (0,)))
    down_local = dot(act, got, ((0,), (0,)))

    def both_reps(value):
        low = value.astype(bf16)
        if reps == 2:
            return value + swap(low).astype(f32)
        return lax.psum(low, "rep").astype(f32)

    up_grad = both_reps(up_local)
    down_grad = both_reps(down_local)
    returned = returned.reshape(EXPERTS, share, 2, CAP, width).astype(f32)
    combined = jnp.sum(returned, axis=1)
    combined = jnp.transpose(combined, (0, 2, 1, 3)).reshape(EXPERTS * CAP, 2 * width)
    collected = jnp.take(combined, spot, axis=0)
    expert_out = collected[:, :width]
    output = (hidden + gate[:, None] * expert_out).astype(bf16).reshape(inputs.shape)
    d_gate = jnp.sum(d_final * expert_out, axis=-1)
    d_logits = gate[:, None] * (picked - router_probs) * d_gate[:, None]
    router_wide = router_full.astype(f32)
    d_normed_two = collected[:, width:] + jnp.dot(
        d_logits, router_wide, precision=lax.Precision.HIGHEST
    )
    router_grad = jnp.dot(d_logits.T, normed_two.astype(f32), precision=lax.Precision.HIGHEST)
    gain_two_grad = jnp.sum(d_normed_two * unit_two, axis=0)
    d_hidden = d_final + norm_back(d_normed_two, unit_two, scale_two, gain_two_full)
    d_branch = d_hidden.astype(bf16)
    d_attended = dot(d_branch, out_full, ((1,), (1,))).astype(bf16).reshape(seqs, rows, width)
    grads = by_core(mine(d_attended, 1, half), swap(yours(d_attended, 1, half)), 0)
    grads = grads.reshape(all_seqs, split, sub, HEAD_GROUPS, head_width)
    grads = jnp.transpose(grads, (0, 3, 1, 2, 4)).reshape(groups, sub, head_width)
    grads = exchange(grads).reshape(queries_count, head_width)
    out_grad = dot(attended, d_branch, ((0,), (0,))).reshape(groups, shard, width)
    out_send = mine(out_grad, 1, part) + swap(yours(out_grad, 1, part).astype(bf16)).astype(f32)
    out_back = exchange(out_send.astype(bf16))
    d_query, d_own, d_other, table_part = pl.pallas_call(
        partial(backward_kernel, **sizes),
        name="attention_backward",
        out_shape=(
            jax.ShapeDtypeStruct((queries_count, head_width), bf16),
            jax.ShapeDtypeStruct((groups, half, 2 * head_width), f32),
            jax.ShapeDtypeStruct((groups, half, 2 * head_width), bf16),
            jax.ShapeDtypeStruct((group_heads, groups * bucket_rows, LANES), f32),
        ),
        in_specs=[smem] + [vmem] * 4,
        out_specs=[vmem] * 4,
        scratch_shapes=[
            pltpu.VMEM((queries_count, length), f32),
            pltpu.VMEM((queries_count, length), bf16),
            pltpu.VMEM((tile, 2 * length - LANES), f32),
            pltpu.VMEM((2 * head_width, length), f32),
            pltpu.VMEM((groups, rows, 2 * head_width), f32),
        ],
        compiler_params=limit,
    )(place, probs, queries, pair, grads)
    d_pair = (d_own + swap(d_other).astype(f32)).astype(bf16)
    d_query = d_query.reshape(groups, 1, sub, head_width)
    if split > 1:
        here = (jnp.arange(split) == me % split).reshape(1, split, 1, 1)
        d_query = jnp.where(here, d_query, jnp.zeros((), bf16))
    d_all = jnp.concatenate([d_query.reshape(groups, half, head_width), d_pair], axis=-1)
    d_flat = d_all.reshape(groups * half, 3 * head_width)
    d_normed_part = dot(d_flat, w_group, ((1,), (1,)))
    x_half = own[:, :half].reshape(groups * half, width).astype(f32)
    unit_half = x_half * lax.rsqrt(jnp.mean(x_half * x_half, axis=-1, keepdims=True) + EPS)
    gain_one_part = jnp.sum(d_normed_part * unit_half, axis=0)
    w_grad = dot(normed_half.reshape(groups * half, width), d_flat, ((0,), (0,)))
    w_grad = w_grad.reshape(groups, shard, 3 * head_width)
    w_grad_send = mine(w_grad, 1, part) + swap(yours(w_grad, 1, part).astype(bf16)).astype(f32)
    table_group_grad = jnp.sum(table_part, axis=-1).T
    table_wide = lax.dynamic_update_slice(
        jnp.zeros((groups * bucket_rows, heads), f32),
        table_group_grad,
        (jnp.zeros((), jnp.int32), (group_at * group_heads).astype(jnp.int32)),
    )

    def widen_three(value):
        return jnp.pad(value, ((0, 0), (0, 0), (0, spare - value.shape[2])))

    small_grad = jnp.concatenate(
        [
            widen_three(gain_one_part.reshape(groups, 1, shard)),
            widen_three(gain_two_grad.reshape(groups, 1, shard)),
            widen_three(jnp.transpose(router_grad.reshape(EXPERTS, groups, shard), (1, 0, 2))),
            widen_three(table_wide.reshape(groups, 1, shard_table)),
        ],
        axis=1,
    )
    small_grad = jnp.pad(small_grad, ((0, 0), (0, part - small_grad.shape[1]), (0, 0)))
    last = jnp.concatenate(
        [
            d_normed_part.reshape(groups, half, width).astype(bf16),
            jnp.concatenate([w_grad_send, small_grad], axis=-1).astype(bf16),
        ],
        axis=1,
    )
    final = exchange(last).astype(f32)
    d_normed_all = jnp.sum(
        final[:, :half].reshape(all_seqs, HEAD_GROUPS * split, half, width), axis=1
    )
    d_normed_other = swap(yours(d_normed_all, 0, seqs).astype(bf16)).astype(f32)
    d_normed = by_core(mine(d_normed_all, 0, seqs), d_normed_other, 1).reshape(tokens, width)
    input_grad = d_hidden + norm_back(d_normed, unit_one, scale_one, gain_one_full)
    w_sum = jnp.sum(
        final[:, half:, : 3 * head_width].reshape(
            all_seqs, HEAD_GROUPS, split, part, 3, head_width
        ),
        axis=(0, 2),
    )
    w_sum = jnp.transpose(w_sum, (2, 1, 0, 3)).reshape(3, part, width)
    out_sum = jnp.sum(out_back.astype(f32), axis=0)
    four = over_pairs(jnp.concatenate([w_sum, out_sum[None]], axis=0))
    four = by_core(four, swap(four.astype(bf16)).astype(f32), 1)
    small_sum = over_pairs(jnp.sum(final[:, half:, 3 * head_width :], axis=0))
    small_sum = small_sum + swap(small_sum)
    return (
        output,
        input_grad.reshape(inputs.shape),
        four[0],
        four[1],
        four[2],
        four[3],
        small_sum[2 + EXPERTS, :shard_table].reshape(bucket_rows, heads),
        small_sum[0, :shard],
        small_sum[1, :shard],
        small_sum[2 : 2 + EXPERTS, :shard].T,
        up_grad,
        down_grad,
    )


def solution(mesh):
    in_specs = (
        P("rep", "sq", None),
        P("sq", None),
        P("sq", None),
        P("sq", None),
        P("sq", None),
        P("sq", None),
        P("sq"),
        P("sq"),
        P("sq", None),
        P(None, "sq"),
        P("sq", None),
        P("rep", "sq", None),
        P("rep", "sq"),
        P("rep", "sq", None),
    )
    out_specs = (
        P("rep", "sq", None),
        P("rep", "sq", None),
        P("sq", None),
        P("sq", None),
        P("sq", None),
        P("sq", None),
        P("sq", None),
        P("sq"),
        P("sq"),
        P("sq", None),
        P(None, "sq"),
        P("sq", None),
    )
    return jax.shard_map(local, mesh=mesh, in_specs=in_specs, out_specs=out_specs, check_vma=False)
```

```python
from functools import partial

import jax
import jax.numpy as jnp
from jax import lax
from jax.experimental import pallas as pl
from jax.experimental.pallas import tpu as pltpu
from jax.sharding import PartitionSpec as P

EXPERTS = 8
CAP = 32
HEAD_GROUPS = 4
EPS = 1e-06
NEGATIVE = -1e30
LIMITS = (1, 2, 3, 4, 5, 6, 7, 8, 12, 16, 23, 32, 46, 64, 91)
LANES = 128
f32 = jnp.float32
bf16 = jnp.bfloat16


def dot(a, b, dims=((1,), (0,))):
    return lax.dot_general(a, b, (dims, ((), ())), preferred_element_type=f32)


def relative_tile(offset, shape, rows, sub):
    row = lax.broadcasted_iota(jnp.int32, shape, 0)
    col = lax.broadcasted_iota(jnp.int32, shape, 1)
    return col - LANES - (rows * (row // sub) + offset + row % sub)


def forward_kernel(
    place_ref,
    own_ref,
    other_ref,
    attended_ref,
    probs_ref,
    query_ref,
    pair_ref,
    normed_all,
    weight_ref,
    gain_one_ref,
    gain_two_ref,
    router_ref,
    weights,
    project,
    scores,
    strip,
    seg_key_ref,
    seg_query_ref,
    table_ref,
    *,
    groups,
    half,
    rows,
    sub,
    head_dim,
    shard,
    all_heads,
):
    core_at = pl.multiple_of(place_ref[0], half)
    other_at = pl.multiple_of(half - place_ref[0], half)
    query_at = pl.multiple_of(place_ref[1], sub)
    width = gain_one_ref.shape[1]
    length = groups * rows
    heads = attended_ref.shape[1] // head_dim
    head_width = heads * head_dim
    per = LANES // rows
    tile = per * sub
    steps = length // LANES
    base = 3 * head_width
    table_rows = 32 // groups
    seg_row = lax.broadcasted_iota(jnp.int32, (sub, rows), 0)
    seg_col = lax.broadcasted_iota(jnp.int32, (sub, rows), 1)
    seg_pick = seg_col == seg_row + place_ref[1]
    for p in range(groups):
        at = slice(p * shard, (p + 1) * shard)
        small = own_ref[p, half:, base:].astype(f32)
        gain_one_ref[:, at] = small[0:1, 0:shard]
        gain_two_ref[:, at] = small[1:2, 0:shard]
        router_ref[:, at] = small[2 : 2 + EXPERTS, 0:shard]
        for k in range(table_rows):
            table_ref[p * table_rows + k : p * table_rows + k + 1, :] = small[
                2 + EXPERTS : 3 + EXPERTS, k * all_heads : (k + 1) * all_heads
            ]
        seg = small[3 + EXPERTS : 4 + EXPERTS, 0:rows]
        seg_key_ref[:, p * rows : (p + 1) * rows] = seg
        seg_query_ref[p * sub : (p + 1) * sub, :] = jnp.sum(
            jnp.where(seg_pick, jnp.broadcast_to(seg, (sub, rows)), 0.0), axis=1, keepdims=True
        )
    part = shard // 2
    for c in range(2):

        @pl.when(place_ref[4] == c)
        def _():
            at = slice(c * part, (c + 1) * part)
            weights[:, at, :] = own_ref[:, half:, 0:base].astype(f32)
            at = slice((1 - c) * part, (2 - c) * part)
            weights[:, at, :] = other_ref[:, half:, 0:base].astype(f32)

    weight_ref[...] = weights[...].reshape(width, base).astype(bf16)
    gain = gain_one_ref[...]
    head_col = lax.broadcasted_iota(jnp.int32, (32, all_heads), 1)

    def norm(x):
        x = x.astype(f32)
        scale = lax.rsqrt(jnp.mean(x * x, axis=-1, keepdims=True) + EPS)
        return ((x * scale) * gain).astype(bf16)

    def norm_step(p, carry):
        normed_all[p, pl.ds(core_at, half), :] = norm(own_ref[p, 0:half, :])
        normed_all[p, pl.ds(other_at, half), :] = norm(other_ref[p, 0:half, :])
        return carry

    lax.fori_loop(0, groups, norm_step, 0)
    chunk = 4

    def project_step(c, carry):
        block = normed_all[pl.ds(c * chunk, chunk)].reshape(chunk * rows, width)
        result = dot(block, weight_ref[...]).astype(bf16)
        project[pl.ds(c * chunk, chunk)] = result.reshape(chunk, rows, 3 * head_width)
        pair_ref[pl.ds(c * chunk * rows, chunk * rows), :] = result[:, head_width:]
        return carry

    lax.fori_loop(0, groups // chunk, project_step, 0)

    def query_step(p, carry):
        query_ref[pl.ds(p * sub, sub), :] = project[p, pl.ds(query_at, sub), 0:head_width]
        return carry

    lax.fori_loop(0, groups, query_step, 0)
    factor = head_dim ** (-0.5)
    left = length - 2 * LANES
    right = length + LANES
    relative = relative_tile(place_ref[1], (tile, 3 * LANES), rows, sub)
    magnitude = jnp.abs(relative)
    for h in range(heads):
        at = h * head_dim
        mine = head_col == place_ref[2] + h
        column = jnp.sum(jnp.where(mine, table_ref[...], 0.0), axis=1, keepdims=True)
        entry = [column[b : b + 1, :] for b in range(32)]
        bias = jnp.where(relative > 0, entry[16], entry[0])
        for k, threshold in enumerate(LIMITS):
            value = jnp.where(relative > 0, entry[17 + k], entry[1 + k])
            bias = jnp.where(magnitude >= threshold, value, bias)
        strip[:, 0:left] = jnp.broadcast_to(entry[15], (tile, left))
        strip[:, left:right] = bias
        strip[:, right:] = jnp.broadcast_to(entry[31], (tile, strip.shape[1] - right))
        scores[...] = (
            dot(query_ref[:, at : at + head_dim], pair_ref[:, at : at + head_dim], ((1,), (1,)))
            * factor
        )

        def soft_step(qb, carry):
            start = pl.multiple_of(length - LANES - qb * LANES, LANES)
            for par in range(per):
                here = pl.ds(qb * tile + par * sub, sub)
                value = scores[here, :] + strip[par * sub : (par + 1) * sub, pl.ds(start, length)]
                same = seg_query_ref[here, :] == seg_key_ref[...]
                value = jnp.where(same, value, NEGATIVE)
                top = jnp.max(value, axis=-1, keepdims=True)
                value = jnp.exp(value - top)
                total = jnp.sum(value, axis=-1, keepdims=True)
                probs_ref[h, here, :] = (value * (1.0 / total)).astype(bf16)
            return carry

        lax.fori_loop(0, steps, soft_step, 0)
        attended_ref[:, at : at + head_dim] = dot(
            probs_ref[h], pair_ref[:, head_width + at : head_width + at + head_dim]
        ).astype(bf16)


def backward_kernel(
    place_ref,
    probs_ref,
    query_ref,
    pair_ref,
    grad_ref,
    d_all_ref,
    table_ref,
    scores,
    low,
    strip,
    flipped,
    d_query,
    *,
    groups,
    half,
    rows,
    sub,
    head_dim,
):
    query_at = pl.multiple_of(place_ref[1], sub)
    length = groups * rows
    head_width = query_ref.shape[1]
    heads = head_width // head_dim
    per = LANES // rows
    tile = per * sub
    steps = length // LANES
    factor = head_dim ** (-0.5)
    left = length - 2 * LANES
    right = length + LANES
    relative = relative_tile(place_ref[1], (tile, 3 * LANES), rows, sub)
    magnitude = jnp.abs(relative)
    count = jnp.zeros_like(relative)
    for threshold in LIMITS:
        count = count + (magnitude >= threshold).astype(jnp.int32)
    bucket = count + jnp.where(relative > 0, 16, 0)

    def lanes_sum(value):
        value = jnp.sum(value, axis=0, keepdims=True)
        total = value[:, 0:LANES]
        for k in range(1, value.shape[1] // LANES):
            total = total + value[:, k * LANES : (k + 1) * LANES]
        return total

    for h in range(heads):
        at = h * head_dim
        grad = grad_ref[:, at : at + head_dim]
        scores[...] = dot(
            grad, pair_ref[:, head_width + at : head_width + at + head_dim], ((1,), (1,))
        )
        strip[...] = jnp.zeros_like(strip)

        def score_step(qb, carry):
            start = pl.multiple_of(length - LANES - qb * LANES, LANES)
            for par in range(per):
                here = pl.ds(qb * tile + par * sub, sub)
                probs = probs_ref[h, here, :].astype(f32)
                value = scores[here, :]
                delta = jnp.sum(probs * value, axis=-1, keepdims=True)
                value = probs * (value - delta)
                low[here, :] = value.astype(bf16)
                strip[par * sub : (par + 1) * sub, pl.ds(start, length)] += value
            return carry

        lax.fori_loop(0, steps, score_step, 0)
        d_query[:, at : at + head_dim] = dot(low[...], pair_ref[:, at : at + head_dim]) * factor
        flipped[at : at + head_dim, :] = (
            dot(query_ref[:, at : at + head_dim], low[...], ((0,), (0,))) * factor
        )
        flipped[head_width + at : head_width + at + head_dim, :] = dot(
            grad, probs_ref[h], ((0,), (0,))
        )
        near = strip[:, left:right]
        for b in range(32):
            table_ref[h, b : b + 1, :] = lanes_sum(jnp.where(bucket == b, near, 0.0))
        table_ref[h, 15:16, :] += lanes_sum(strip[:, 0:left])
        table_ref[h, 31:32, :] += lanes_sum(strip[:, right:])
    d_all_ref[:, :, 0:head_width] = jnp.zeros((groups, rows, head_width), bf16)
    for c in range(length // LANES):
        block = flipped[:, c * LANES : (c + 1) * LANES].T.astype(bf16)
        d_all_ref[c * per : (c + 1) * per, :, head_width:] = block.reshape(
            per, rows, 2 * head_width
        )

    def place_step(p, carry):
        d_all_ref[p, pl.ds(query_at, sub), 0:head_width] = d_query[
            pl.ds(p * sub, sub), :
        ].astype(bf16)
        return carry

    lax.fori_loop(0, groups, place_step, 0)


def last_kernel(
    place_ref,
    d_own_ref,
    d_other_ref,
    weight_ref,
    normed_ref,
    own_ref,
    gain_two_ref,
    router_ref,
    table_ref,
    last_ref,
    d_sum,
    w_grad,
    gain_sum,
    small,
    *,
    groups,
    half,
    rows,
    shard,
    all_heads,
):
    core_at = pl.multiple_of(place_ref[0], half)
    width = weight_ref.shape[0]
    base = weight_ref.shape[1]
    part = shard // 2
    length = groups * rows
    d_sum[...] = (d_own_ref[...].astype(f32) + d_other_ref[...].astype(f32)).astype(bf16)
    gain_sum[...] = jnp.zeros_like(gain_sum)
    chunk = 4

    def normed_step(c, carry):
        at = pl.ds(c * chunk, chunk)
        block = d_sum[at, pl.ds(core_at, half), :].reshape(chunk * half, base)
        d_normed = dot(block, weight_ref[...], ((1,), (1,)))
        x = own_ref[at, 0:half, :].astype(f32).reshape(chunk * half, width)
        unit = x * lax.rsqrt(jnp.mean(x * x, axis=-1, keepdims=True) + EPS)
        gain_sum[...] += jnp.sum(d_normed * unit, axis=0, keepdims=True)
        last_ref[at, 0:half, :] = d_normed.reshape(chunk, half, width).astype(bf16)
        return carry

    lax.fori_loop(0, groups // chunk, normed_step, 0)
    w_grad[...] = dot(
        normed_ref[...].reshape(length, width), d_sum[...].reshape(length, base), ((0,), (0,))
    ).reshape(groups, shard, base)
    for c in range(2):

        @pl.when(place_ref[4] == c)
        def _():
            last_ref[:, half:, 0:base] = w_grad[:, c * part : (c + 1) * part, :].astype(bf16)

    heads = table_ref.shape[0]
    head_col = lax.broadcasted_iota(jnp.int32, (32, all_heads), 1)
    table = jnp.zeros((32, all_heads), f32)
    for h in range(heads):
        column = jnp.sum(table_ref[h], axis=1, keepdims=True)
        table = table + jnp.where(head_col == place_ref[2] + h, column, 0.0)
    table_rows = 32 // groups
    small[...] = jnp.zeros_like(small)
    for p in range(groups):
        at = slice(p * shard, (p + 1) * shard)
        small[p, 0:1, 0:shard] = gain_sum[:, at]
        small[p, 1:2, 0:shard] = gain_two_ref[:, at]
        small[p, 2 : 2 + EXPERTS, 0:shard] = router_ref[:, at]
        for k in range(table_rows):
            small[p, 2 + EXPERTS : 3 + EXPERTS, k * all_heads : (k + 1) * all_heads] = table[
                p * table_rows + k : p * table_rows + k + 1, :
            ]
    last_ref[:, half:, base:] = small[...].astype(bf16)


def out_grad_kernel(
    place_ref, attended_ref, other_ref, d_ref, d_other_ref, out_ref, total, *, groups, shard
):
    part = shard // 2
    width = total.shape[2]
    grad = dot(attended_ref[...], d_ref[...], ((0,), (0,)))
    grad = grad + dot(other_ref[...], d_other_ref[...], ((0,), (0,)))
    total[...] = grad.reshape(groups, shard, width)
    for c in range(2):

        @pl.when(place_ref[4] == c)
        def _():
            out_ref[...] = total[:, c * part : (c + 1) * part, :].astype(bf16)


def sum_kernel(
    place_ref, final_ref, keep_ref, give_ref, four_ref, small_ref, *, half, seqs
):
    groups, _, width = final_ref.shape
    part = four_ref.shape[1]
    base = width - small_ref.shape[1]
    head_width = base // 3
    per_seq = groups // (2 * seqs)
    split = per_seq // HEAD_GROUPS
    mine = place_ref[3]
    yours = seqs - mine
    for l in range(seqs):

        def total(first):
            value = final_ref[first, 0:half, :].astype(f32)
            for k in range(1, per_seq):
                value = value + final_ref[first + k, 0:half, :].astype(f32)
            return value

        keep_ref[l] = total((mine + l) * per_seq)
        give_ref[l] = total((yours + l) * per_seq).astype(bf16)
    for g in range(HEAD_GROUPS):
        grad = jnp.zeros((part, base), f32)
        for s in range(2 * seqs):
            for t in range(split):
                grad = grad + final_ref[(s * HEAD_GROUPS + g) * split + t, half:, 0:base].astype(
                    f32
                )
        for i in range(3):
            four_ref[i, :, g * head_width : (g + 1) * head_width] = grad[
                :, i * head_width : (i + 1) * head_width
            ]
    small = final_ref[0, half:, base:].astype(f32)
    for p in range(1, groups):
        small = small + final_ref[p, half:, base:].astype(f32)
    small_ref[...] = small


def input_kernel(
    place_ref,
    keep_ref,
    given_ref,
    four_ref,
    other_ref,
    out_mine_ref,
    out_other_ref,
    x_ref,
    d_hidden_ref,
    gain_ref,
    input_ref,
    query_ref,
    key_ref,
    value_ref,
    out_ref,
    d_normed_ref,
    *,
    half,
):
    core_at = pl.multiple_of(place_ref[0], half)
    other_at = pl.multiple_of(half - place_ref[0], half)
    seqs, rows, width = x_ref.shape
    part = four_ref.shape[1]
    d_normed_ref[:, pl.ds(core_at, half), :] = keep_ref[...]
    d_normed_ref[:, pl.ds(other_at, half), :] = given_ref[...].astype(f32)
    d_normed = d_normed_ref[...].reshape(seqs * rows, width)
    x = x_ref[...].reshape(seqs * rows, width).astype(f32)
    scale = lax.rsqrt(jnp.mean(x * x, axis=-1, keepdims=True) + EPS)
    unit = x * scale
    d_unit = d_normed * gain_ref[...]
    grad = scale * (d_unit - unit * jnp.mean(d_unit * unit, axis=-1, keepdims=True))
    input_ref[...] = (d_hidden_ref[...] + grad).reshape(seqs, rows, width)
    for c in range(2):

        @pl.when(place_ref[4] == c)
        def _():
            here = slice(c * part, (c + 1) * part)
            there = slice((1 - c) * part, (2 - c) * part)
            for i, ref in enumerate((query_ref, key_ref, value_ref)):
                ref[here, :] = four_ref[i]
                ref[there, :] = other_ref[i].astype(f32)
            out_ref[here, :] = out_mine_ref[...]
            out_ref[there, :] = out_other_ref[...]


def middle_kernel(
    place_ref,
    back_ref,
    swapped_ref,
    x_ref,
    out_ref,
    out_other_ref,
    gain_ref,
    router_ref,
    routes_ref,
    cotangent_ref,
    send_ref,
    attended_ref,
    hidden_ref,
    normed_ref,
    probs_ref,
    spread_ref,
    attended,
    *,
    half,
    sub,
    split,
    few,
    share,
):
    seqs, rows, width = attended.shape
    tokens = seqs * rows
    head_width = back_ref.shape[2]
    core_at = place_ref[0]
    first = place_ref[3]
    for l in range(seqs):
        for g in range(HEAD_GROUPS):
            lanes = slice(g * head_width, (g + 1) * head_width)
            for t in range(split):
                here = pl.multiple_of(core_at + t * sub, sub)
                there = pl.multiple_of(half - core_at + t * sub, sub)
                at = (l * HEAD_GROUPS + g) * split + t
                kept = first * (HEAD_GROUPS * split) + at
                attended[l, pl.ds(here, sub), lanes] = back_ref[kept]
                attended[l, pl.ds(there, sub), lanes] = swapped_ref[at]
    low = attended[...].reshape(tokens, width)
    attended_ref[...] = low
    out_half = width // 2
    here = pl.multiple_of(place_ref[4] * out_half, LANES)
    there = pl.multiple_of(out_half - place_ref[4] * out_half, LANES)
    hidden_ref[:, pl.ds(here, out_half)] = dot(low, out_ref[...])
    hidden_ref[:, pl.ds(there, out_half)] = dot(low, out_other_ref[...])
    hidden = x_ref[...].reshape(tokens, width).astype(f32) + hidden_ref[...]
    hidden_ref[...] = hidden
    scale = lax.rsqrt(jnp.mean(hidden * hidden, axis=-1, keepdims=True) + EPS)
    normed = ((hidden * scale) * gain_ref[...]).astype(bf16)
    normed_ref[...] = normed
    logits = dot(normed, router_ref[...].astype(bf16), ((1,), (1,)))
    logits = jnp.exp(logits - jnp.max(logits, axis=-1, keepdims=True))
    probs = logits / jnp.sum(logits, axis=-1, keepdims=True)
    probs_ref[...] = probs
    chosen = routes_ref[...]
    picked = (chosen == lax.broadcasted_iota(jnp.int32, (tokens, EXPERTS), 1)).astype(f32)
    gate = jnp.sum(probs * picked, axis=-1, keepdims=True)
    row = lax.broadcasted_iota(jnp.int32, (tokens, tokens), 0)
    col = lax.broadcasted_iota(jnp.int32, (tokens, tokens), 1)
    before = (col < row).astype(bf16)
    earlier = dot(before, picked.astype(bf16))
    slot = jnp.sum(earlier * picked, axis=-1, keepdims=True).astype(jnp.int32)
    spot = chosen * CAP + slot
    spread = (spot == lax.broadcasted_iota(jnp.int32, (tokens, EXPERTS * CAP), 1)).astype(bf16)
    spread_ref[...] = spread
    d_expert = (gate * cotangent_ref[...].reshape(tokens, width).astype(f32)).astype(bf16)
    for i, rows_in in enumerate((normed, d_expert)):
        rows_out = dot(spread, rows_in, ((0,), (0,))).astype(bf16)
        for e in range(EXPERTS):
            for k in range(share):
                send_ref[e * share + k, i * few : (i + 1) * few, :] = rows_out[
                    e * few : (e + 1) * few, :
                ]


def expert_step(received, got, up, down):
    pre = dot(received, up)
    root = 0.7978845608028654
    square = pre * pre
    bend = jnp.tanh(root * (pre + 0.044715 * (square * pre)))
    side = 0.5 * (1.0 + bend)
    act = (pre * side).astype(bf16)
    slope = side + 0.5 * pre * (1.0 - bend * bend) * (root * (1.0 + 3 * 0.044715 * square))
    d_pre = (dot(got, down, ((1,), (1,))) * slope).astype(bf16)
    return act, d_pre, dot(act, down), dot(d_pre, up, ((1,), (1,)))


def expert_kernel(
    arrived_ref,
    up_ref,
    down_ref,
    results_ref,
    received_ref,
    got_ref,
    act_ref,
    d_pre_ref,
    out_sum,
    row_sum,
    *,
    few,
):
    groups, _, width = arrived_ref.shape
    step = pl.program_id(0)

    @pl.when(step == 0)
    def _():
        out_sum[...] = jnp.zeros_like(out_sum)
        row_sum[...] = jnp.zeros_like(row_sum)
        shape = (groups * few, width)
        received_ref[...] = arrived_ref[:, 0:few, :].reshape(shape)
        got_ref[...] = arrived_ref[:, few:, :].reshape(shape)

    act, d_pre, out, rows = expert_step(
        received_ref[...], got_ref[...], up_ref[...], down_ref[...]
    )
    act_ref[...] = act
    d_pre_ref[...] = d_pre
    out_sum[...] += out
    row_sum[...] += rows

    @pl.when(step == pl.num_programs(0) - 1)
    def _():
        shape = (groups, few, width)
        results_ref[:, 0:few, :] = out_sum[...].reshape(shape).astype(bf16)
        results_ref[:, few:, :] = row_sum[...].reshape(shape).astype(bf16)


def turn_kernel(
    place_ref,
    returned_ref,
    spread_ref,
    hidden_ref,
    normed_ref,
    probs_ref,
    routes_ref,
    cotangent_ref,
    gain_ref,
    router_ref,
    out_ref,
    out_other_ref,
    output_ref,
    d_hidden_ref,
    d_branch_ref,
    keep_ref,
    give_ref,
    router_grad_ref,
    gain_grad_ref,
    d_attended,
    *,
    half,
    sub,
    split,
    few,
    share,
):
    seqs, rows, width = output_ref.shape
    tokens = seqs * rows
    head_width = keep_ref.shape[2]
    core_at = place_ref[0]
    spread = spread_ref[...]

    def collect(at):
        pieces = []
        for e in range(EXPERTS):
            piece = returned_ref[e * share, at, :].astype(f32)
            for k in range(1, share):
                piece = piece + returned_ref[e * share + k, at, :].astype(f32)
            pieces.append(piece)
        value = jnp.concatenate(pieces, axis=0)
        high = value.astype(bf16)
        low = (value - high.astype(f32)).astype(bf16)
        return dot(spread, high) + dot(spread, low)

    expert_out = collect(slice(0, few))
    d_rows = collect(slice(few, 2 * few))
    hidden = hidden_ref[...]
    probs = probs_ref[...]
    picked = (
        routes_ref[...] == lax.broadcasted_iota(jnp.int32, (tokens, EXPERTS), 1)
    ).astype(f32)
    gate = jnp.sum(probs * picked, axis=-1, keepdims=True)
    output_ref[...] = (hidden + gate * expert_out).astype(bf16).reshape(seqs, rows, width)
    d_final = cotangent_ref[...].reshape(tokens, width).astype(f32)
    d_gate = jnp.sum(d_final * expert_out, axis=-1, keepdims=True)
    d_logits = gate * (picked - probs) * d_gate
    d_normed = d_rows
    for e in range(EXPERTS):
        d_normed = d_normed + d_logits[:, e : e + 1] * router_ref[e : e + 1, :]
    router_grad_ref[...] = lax.dot_general(
        d_logits,
        normed_ref[...].astype(f32),
        (((0,), (0,)), ((), ())),
        precision=lax.Precision.HIGHEST,
        preferred_element_type=f32,
    )
    scale = lax.rsqrt(jnp.mean(hidden * hidden, axis=-1, keepdims=True) + EPS)
    unit = hidden * scale
    gain_grad_ref[...] = jnp.sum(d_normed * unit, axis=0, keepdims=True)
    d_unit = d_normed * gain_ref[...]
    d_hidden = d_final + scale * (d_unit - unit * jnp.mean(d_unit * unit, axis=-1, keepdims=True))
    d_hidden_ref[...] = d_hidden
    d_branch = d_hidden.astype(bf16)
    d_branch_ref[...] = d_branch
    out_half = width // 2
    here = pl.multiple_of(place_ref[4] * out_half, LANES)
    there = pl.multiple_of(out_half - place_ref[4] * out_half, LANES)
    d_low = dot(d_branch_ref[:, pl.ds(here, out_half)], out_ref[...], ((1,), (1,)))
    d_low = d_low + dot(d_branch_ref[:, pl.ds(there, out_half)], out_other_ref[...], ((1,), (1,)))
    d_attended[...] = d_low.astype(bf16).reshape(seqs, rows, width)
    for l in range(seqs):
        for g in range(HEAD_GROUPS):
            lanes = slice(g * head_width, (g + 1) * head_width)
            for t in range(split):
                here = pl.multiple_of(core_at + t * sub, sub)
                there = pl.multiple_of(half - core_at + t * sub, sub)
                at = (l * HEAD_GROUPS + g) * split + t
                keep_ref[at] = d_attended[l, pl.ds(here, sub), lanes]
                give_ref[at] = d_attended[l, pl.ds(there, sub), lanes]


def exchange(value):
    return lax.all_to_all(value, "sq", split_axis=0, concat_axis=0, tiled=True)


def local(
    inputs,
    w_query,
    w_key,
    w_value,
    w_out,
    table,
    gain_one,
    gain_two,
    w_router,
    w_up,
    w_down,
    routes,
    segments,
    cotangent,
):
    seqs, rows, width = inputs.shape
    heads = table.shape[1]
    head_dim = width // heads
    reps = lax.axis_size("rep")
    groups = lax.axis_size("sq")
    length = rows * groups
    tokens = seqs * rows
    share = groups // EXPERTS
    half = rows // 2
    all_seqs = 2 * seqs
    split = groups // (all_seqs * HEAD_GROUPS)
    sub = half // split
    group_heads = heads // HEAD_GROUPS
    head_width = group_heads * head_dim
    shard = w_query.shape[0]
    part = shard // 2
    bucket_rows = table.shape[0]
    core = lax.axis_index("rep") % 2
    me = lax.axis_index("sq")
    group_at = (me // split) % HEAD_GROUPS
    first = core == 0
    pairs = [(i, i ^ 1) for i in range(reps)]

    def swap(value):
        return lax.ppermute(value, "rep", pairs)

    def by_core(own, other, axis):
        return jnp.where(
            first,
            jnp.concatenate([own, other], axis=axis),
            jnp.concatenate([other, own], axis=axis),
        )

    def mine(value, axis, size):
        return lax.dynamic_slice_in_dim(value, core * size, size, axis)

    def yours(value, axis, size):
        return lax.dynamic_slice_in_dim(value, (1 - core) * size, size, axis)

    def over_pairs(value):
        if reps == 2:
            return value
        sets = [list(range(0, reps, 2)), list(range(1, reps, 2))]
        return lax.psum(value, "rep", axis_index_groups=sets)

    x_pair = by_core(mine(inputs, 1, half), swap(yours(inputs, 1, half)), 0)
    seg_low = segments.astype(bf16)
    seg_pair = by_core(seg_low, swap(seg_low), 0)
    w_three = jnp.stack([mine(w, 0, part) for w in (w_query, w_key, w_value)], axis=1)
    w_three = w_three.reshape(part, 3, HEAD_GROUPS, head_width)
    w_send = jnp.transpose(w_three, (2, 0, 1, 3)).reshape(HEAD_GROUPS, part, 3 * head_width)
    spare = width - 3 * head_width

    def widen(value):
        return jnp.pad(value, ((0, 0), (0, spare - value.shape[1])))

    small = jnp.concatenate(
        [
            widen(gain_one[None]),
            widen(gain_two[None]),
            widen(w_router.T),
            widen(table.reshape(1, -1)),
        ],
        axis=0,
    )
    small = jnp.broadcast_to(small[None], (all_seqs,) + small.shape)
    small = jnp.concatenate(
        [small, jnp.pad(seg_pair, ((0, 0), (0, spare - rows)))[:, None, :]], axis=1
    )
    small = jnp.pad(small, ((0, 0), (0, part - small.shape[1]), (0, 0)))

    shape = (all_seqs, HEAD_GROUPS, split)
    lower = jnp.concatenate(
        [
            jnp.broadcast_to(w_send[None, :, None], shape + w_send.shape[1:]),
            jnp.broadcast_to(small[:, None, None], shape + small.shape[1:]),
        ],
        axis=-1,
    )
    send = jnp.concatenate(
        [jnp.broadcast_to(x_pair[:, None, None], shape + x_pair.shape[1:]), lower], axis=3
    ).reshape(groups, half + part, width)
    own = exchange(send)
    own, out_half = lax.optimization_barrier((own, mine(w_out, 1, width // 2)))
    other, out_half = lax.optimization_barrier((swap(own), out_half))
    out_mine = exchange(jnp.broadcast_to(out_half[None], (groups, shard, width // 2)))
    query_at = core * half + (me % split) * sub
    place = jnp.stack([core * half, query_at, group_at * group_heads, core * seqs, core])
    place = place.astype(jnp.int32)
    shard_table = bucket_rows * heads
    queries_count = groups * sub
    tile = (LANES // rows) * sub
    sizes = dict(groups=groups, half=half, rows=rows, sub=sub, head_dim=head_dim)
    smem = pl.BlockSpec(memory_space=pltpu.SMEM)
    vmem = pl.BlockSpec(memory_space=pltpu.VMEM)

    def cost(microseconds):
        return pl.CostEstimate(
            flops=microseconds * 900_000_000,
            bytes_accessed=microseconds * 1_000_000,
            transcendentals=0,
        )

    limit = pltpu.CompilerParams(vmem_limit_bytes=56 * 1024 * 1024)
    (
        attended_part,
        probs,
        queries,
        pair,
        normed_all,
        w_group,
        gain_one_full,
        gain_two_full,
        router_full,
    ) = pl.pallas_call(
        partial(forward_kernel, shard=shard, all_heads=heads, **sizes),
        name="attention_forward",
        out_shape=(
            jax.ShapeDtypeStruct((queries_count, head_width), bf16),
            jax.ShapeDtypeStruct((group_heads, queries_count, length), bf16),
            jax.ShapeDtypeStruct((queries_count, head_width), bf16),
            jax.ShapeDtypeStruct((length, 2 * head_width), bf16),
            jax.ShapeDtypeStruct((groups, rows, width), bf16),
            jax.ShapeDtypeStruct((width, 3 * head_width), bf16),
            jax.ShapeDtypeStruct((1, width), f32),
            jax.ShapeDtypeStruct((1, width), f32),
            jax.ShapeDtypeStruct((EXPERTS, width), f32),
        ),
        in_specs=[smem] + [vmem] * 2,
        out_specs=[vmem] * 9,
        scratch_shapes=[
            pltpu.VMEM((groups, shard, 3 * head_width), f32),
            pltpu.VMEM((groups, rows, 3 * head_width), bf16),
            pltpu.VMEM((queries_count, length), f32),
            pltpu.VMEM((tile, 2 * length - LANES), f32),
            pltpu.VMEM((1, length), f32),
            pltpu.VMEM((queries_count, 1), f32),
            pltpu.VMEM((32, heads), f32),
        ],
        compiler_params=limit,
        cost_estimate=cost(60),
    )(place, own, other)
    attended_part, out_mine = lax.optimization_barrier((attended_part, out_mine))
    back = exchange(attended_part.reshape(groups, sub, head_width))
    out_mine = out_mine.reshape(width, width // 2)
    out_yours = swap(out_mine)
    back_given = swap(yours(back, 0, groups // 2))
    few = CAP
    routes_flat = routes.reshape(tokens, 1)
    pieces = dict(half=half, sub=sub, split=split, few=few)
    buffer, attended, hidden, normed_two, router_probs, spread = pl.pallas_call(
        partial(middle_kernel, share=share, **pieces),
        name="router_and_dispatch",
        out_shape=(
            jax.ShapeDtypeStruct((groups, 2 * few, width), bf16),
            jax.ShapeDtypeStruct((tokens, width), bf16),
            jax.ShapeDtypeStruct((tokens, width), f32),
            jax.ShapeDtypeStruct((tokens, width), bf16),
            jax.ShapeDtypeStruct((tokens, EXPERTS), f32),
            jax.ShapeDtypeStruct((tokens, EXPERTS * CAP), bf16),
        ),
        in_specs=[smem] + [vmem] * 9,
        out_specs=[vmem] * 6,
        scratch_shapes=[pltpu.VMEM((seqs, rows, width), bf16)],
        compiler_params=limit,
        cost_estimate=cost(5),
    )(
        place,
        back,
        back_given,
        inputs,
        out_mine,
        out_yours,
        gain_two_full,
        router_full,
        routes_flat,
        cotangent,
    )
    arrived = exchange(buffer)
    expert_rows = groups * few
    hidden_units = w_up.shape[1]
    chunk = hidden_units // 3 if hidden_units % (3 * LANES) == 0 else hidden_units
    whole = [
        pl.BlockSpec((groups, 2 * few, width), lambda i: (0, 0, 0)),
        pl.BlockSpec((expert_rows, width), lambda i: (0, 0)),
        pl.BlockSpec((expert_rows, chunk), lambda i: (0, i)),
    ]
    rows_low = jax.ShapeDtypeStruct((expert_rows, width), bf16)
    units_low = jax.ShapeDtypeStruct((expert_rows, hidden_units), bf16)
    results, received, got, act, d_pre = pl.pallas_call(
        partial(expert_kernel, few=few),
        name="experts",
        grid=(hidden_units // chunk,),
        out_shape=(
            jax.ShapeDtypeStruct((groups, 2 * few, width), bf16),
            rows_low,
            rows_low,
            units_low,
            units_low,
        ),
        in_specs=[
            whole[0],
            pl.BlockSpec((width, chunk), lambda i: (0, i)),
            pl.BlockSpec((chunk, width), lambda i: (i, 0)),
        ],
        out_specs=[whole[0]] + [whole[1]] * 2 + [whole[2]] * 2,
        scratch_shapes=[pltpu.VMEM((expert_rows, width), f32)] * 2,
        compiler_params=limit,
        cost_estimate=cost(8),
    )(arrived, w_up, w_down)
    returned = exchange(results)
    up_local = dot(received, d_pre, ((0,), (0,))).astype(bf16)
    down_local = dot(act, got, ((0,), (0,))).astype(bf16)
    returned, up_local, down_local = lax.optimization_barrier((returned, up_local, down_local))

    def both_reps(value):
        if reps == 2:
            return value.astype(f32) + swap(value).astype(f32)
        return lax.psum(value, "rep").astype(f32)

    output, d_hidden, d_branch, keep, give, router_grad, gain_two_grad = pl.pallas_call(
        partial(turn_kernel, share=share, **pieces),
        name="combine_and_turn",
        out_shape=(
            jax.ShapeDtypeStruct((seqs, rows, width), bf16),
            jax.ShapeDtypeStruct((tokens, width), f32),
            jax.ShapeDtypeStruct((tokens, width), bf16),
            jax.ShapeDtypeStruct((groups // 2, sub, head_width), bf16),
            jax.ShapeDtypeStruct((groups // 2, sub, head_width), bf16),
            jax.ShapeDtypeStruct((EXPERTS, width), f32),
            jax.ShapeDtypeStruct((1, width), f32),
        ),
        in_specs=[smem] + [vmem] * 11,
        out_specs=[vmem] * 7,
        scratch_shapes=[pltpu.VMEM((seqs, rows, width), bf16)],
        compiler_params=limit,
        cost_estimate=cost(5),
    )(
        place,
        returned,
        spread,
        hidden,
        normed_two,
        router_probs,
        routes_flat,
        cotangent,
        gain_two_full,
        router_full,
        out_mine,
        out_yours,
    )
    grads = exchange(by_core(keep, swap(give), 0))
    out_send = pl.pallas_call(
        partial(out_grad_kernel, groups=groups, shard=shard),
        name="out_grad",
        out_shape=jax.ShapeDtypeStruct((groups, part, width), bf16),
        in_specs=[smem] + [vmem] * 4,
        out_specs=vmem,
        scratch_shapes=[pltpu.VMEM((groups, shard, width), f32)],
        compiler_params=limit,
        cost_estimate=cost(3),
    )(place, attended, swap(attended), d_branch, swap(d_branch))
    grads, out_send = lax.optimization_barrier((grads, out_send))
    grads = grads.reshape(queries_count, head_width)
    out_back = exchange(out_send)
    d_all, table_part = pl.pallas_call(
        partial(backward_kernel, **sizes),
        name="attention_backward",
        out_shape=(
            jax.ShapeDtypeStruct((groups, rows, 3 * head_width), bf16),
            jax.ShapeDtypeStruct((group_heads, groups * bucket_rows, LANES), f32),
        ),
        in_specs=[smem] + [vmem] * 4,
        out_specs=[vmem] * 2,
        scratch_shapes=[
            pltpu.VMEM((queries_count, length), f32),
            pltpu.VMEM((queries_count, length), bf16),
            pltpu.VMEM((tile, 2 * length - LANES), f32),
            pltpu.VMEM((2 * head_width, length), f32),
            pltpu.VMEM((queries_count, head_width), f32),
        ],
        compiler_params=limit,
        cost_estimate=cost(1),
    )(place, probs, queries, pair, grads)
    out_sum = jnp.sum(out_back.astype(f32), axis=0)
    out_sum = over_pairs(out_sum)
    out_other = swap(out_sum)
    last = pl.pallas_call(
        partial(last_kernel, groups=groups, half=half, rows=rows, shard=shard, all_heads=heads),
        name="input_side",
        out_shape=jax.ShapeDtypeStruct((groups, half + part, width), bf16),
        in_specs=[smem] + [vmem] * 8,
        out_specs=vmem,
        scratch_shapes=[
            pltpu.VMEM((groups, rows, 3 * head_width), bf16),
            pltpu.VMEM((groups, shard, 3 * head_width), f32),
            pltpu.VMEM((1, width), f32),
            pltpu.VMEM((groups, part, spare), f32),
        ],
        compiler_params=limit,
        cost_estimate=cost(1),
    )(
        place,
        d_all,
        swap(d_all),
        w_group,
        normed_all,
        own,
        gain_two_grad,
        router_grad,
        table_part,
    )
    last, out_other = lax.optimization_barrier((last, out_other))
    final = exchange(last)
    up_grad = both_reps(up_local)
    down_grad = both_reps(down_local)
    final, up_grad, down_grad = lax.optimization_barrier((final, up_grad, down_grad))
    keep, give, four, small_sum = pl.pallas_call(
        partial(sum_kernel, half=half, seqs=seqs),
        name="sums",
        out_shape=(
            jax.ShapeDtypeStruct((seqs, half, width), f32),
            jax.ShapeDtypeStruct((seqs, half, width), bf16),
            jax.ShapeDtypeStruct((3, part, width), f32),
            jax.ShapeDtypeStruct((part, spare), f32),
        ),
        in_specs=[smem] + [vmem],
        out_specs=[vmem] * 4,
        compiler_params=limit,
        cost_estimate=cost(2),
    )(place, final)
    four = over_pairs(four)
    small_sum = over_pairs(small_sum)
    small_sum = small_sum + swap(small_sum)
    input_grad, query_grad, key_grad, value_grad, out_grad = pl.pallas_call(
        partial(input_kernel, half=half),
        name="input_grad",
        out_shape=(jax.ShapeDtypeStruct((seqs, rows, width), f32),)
        + (jax.ShapeDtypeStruct((shard, width), f32),) * 4,
        in_specs=[smem] + [vmem] * 9,
        out_specs=[vmem] * 5,
        scratch_shapes=[pltpu.VMEM((seqs, rows, width), f32)],
        compiler_params=limit,
        cost_estimate=cost(2),
    )(
        place,
        keep,
        swap(give),
        four,
        swap(four.astype(bf16)),
        out_sum,
        out_other,
        inputs,
        d_hidden,
        gain_one_full,
    )
    return (
        output,
        input_grad,
        query_grad,
        key_grad,
        value_grad,
        out_grad,
        small_sum[2 + EXPERTS, :shard_table].reshape(bucket_rows, heads),
        small_sum[0, :shard],
        small_sum[1, :shard],
        small_sum[2 : 2 + EXPERTS, :shard].T,
        up_grad,
        down_grad,
    )


def solution(mesh):
    in_specs = (
        P("rep", "sq", None),
        P("sq", None),
        P("sq", None),
        P("sq", None),
        P("sq", None),
        P("sq", None),
        P("sq"),
        P("sq"),
        P("sq", None),
        P(None, "sq"),
        P("sq", None),
        P("rep", "sq", None),
        P("rep", "sq"),
        P("rep", "sq", None),
    )
    out_specs = (
        P("rep", "sq", None),
        P("rep", "sq", None),
        P("sq", None),
        P("sq", None),
        P("sq", None),
        P("sq", None),
        P("sq", None),
        P("sq"),
        P("sq"),
        P("sq", None),
        P(None, "sq"),
        P("sq", None),
    )
    return jax.shard_map(local, mesh=mesh, in_specs=in_specs, out_specs=out_specs, check_vma=False)
```

```python
from functools import partial

import jax
import jax.numpy as jnp
from jax import lax
from jax.experimental import pallas as pl
from jax.experimental.pallas import tpu as pltpu
from jax.sharding import PartitionSpec as P

EXPERTS = 8
CAP = 32
HEAD_GROUPS = 4
EPS = 1e-06
NEGATIVE = -1e30
LIMITS = (1, 2, 3, 4, 5, 6, 7, 8, 12, 16, 23, 32, 46, 64, 91)
LANES = 128
f32 = jnp.float32
bf16 = jnp.bfloat16


def dot(a, b, dims=((1,), (0,))):
    return lax.dot_general(a, b, (dims, ((), ())), preferred_element_type=f32)


def relative_tile(offset, shape, rows, sub):
    row = lax.broadcasted_iota(jnp.int32, shape, 0)
    col = lax.broadcasted_iota(jnp.int32, shape, 1)
    return col - LANES - (rows * (row // sub) + offset + row % sub)


def pack_kernel(
    place_ref,
    x_ref,
    x_other_ref,
    seg_ref,
    seg_other_ref,
    query_ref,
    key_ref,
    value_ref,
    gain_one_ref,
    gain_two_ref,
    router_ref,
    table_ref,
    send_ref,
    weights,
    small,
    *,
    half,
    split,
):
    seqs, rows, width = x_ref.shape
    shard = query_ref.shape[0]
    part = shard // 2
    head_width = width // HEAD_GROUPS
    base = 3 * head_width
    per_seq = HEAD_GROUPS * split
    heads = table_ref.shape[1]
    for c in range(2):

        @pl.when(place_ref[4] == c)
        def _():
            at = slice(c * part, (c + 1) * part)
            for i, ref in enumerate((query_ref, key_ref, value_ref)):
                for g in range(HEAD_GROUPS):
                    weights[g, :, i * head_width : (i + 1) * head_width] = ref[
                        at, g * head_width : (g + 1) * head_width
                    ].astype(f32)

    small[...] = jnp.zeros_like(small)
    small[0:1, 0:shard] = gain_one_ref[...].astype(f32)
    small[1:2, 0:shard] = gain_two_ref[...].astype(f32)
    small[2 : 2 + EXPERTS, 0:shard] = router_ref[...].astype(f32)
    for k in range(table_ref.shape[0]):
        small[2 + EXPERTS : 3 + EXPERTS, k * heads : (k + 1) * heads] = table_ref[
            k : k + 1, :
        ].astype(f32)
    x_at = pl.ds(pl.multiple_of(place_ref[0], half), half)
    for c in range(2):
        x, seg = (x_ref, seg_ref) if c == 0 else (x_other_ref, seg_other_ref)
        first = (place_ref[3] if c == 0 else seqs - place_ref[3]) * per_seq
        for l in range(seqs):
            small[3 + EXPERTS : 4 + EXPERTS, 0:rows] = seg[l : l + 1, :].astype(f32)
            for k in range(per_seq):
                at = first + l * per_seq + k
                send_ref[at, 0:half, :] = x[l, x_at, :]
                send_ref[at, half:, 0:base] = weights[k // split].astype(bf16)
                send_ref[at, half:, base:] = small[...].astype(bf16)


def forward_kernel(
    place_ref,
    own_ref,
    other_ref,
    attended_ref,
    probs_ref,
    query_ref,
    pair_ref,
    normed_all,
    weight_ref,
    gain_one_ref,
    gain_two_ref,
    router_ref,
    weights,
    project,
    scores,
    strip,
    seg_key_ref,
    seg_query_ref,
    table_ref,
    *,
    groups,
    half,
    rows,
    sub,
    head_dim,
    shard,
    all_heads,
):
    core_at = pl.multiple_of(place_ref[0], half)
    other_at = pl.multiple_of(half - place_ref[0], half)
    query_at = pl.multiple_of(place_ref[1], sub)
    width = gain_one_ref.shape[1]
    length = groups * rows
    heads = attended_ref.shape[1] // head_dim
    head_width = heads * head_dim
    per = LANES // rows
    tile = per * sub
    steps = length // LANES
    base = 3 * head_width
    table_rows = 32 // groups
    seg_row = lax.broadcasted_iota(jnp.int32, (sub, rows), 0)
    seg_col = lax.broadcasted_iota(jnp.int32, (sub, rows), 1)
    seg_pick = seg_col == seg_row + place_ref[1]
    for p in range(groups):
        at = slice(p * shard, (p + 1) * shard)
        small = own_ref[p, half:, base:].astype(f32)
        gain_one_ref[:, at] = small[0:1, 0:shard]
        gain_two_ref[:, at] = small[1:2, 0:shard]
        router_ref[:, at] = small[2 : 2 + EXPERTS, 0:shard]
        for k in range(table_rows):
            table_ref[p * table_rows + k : p * table_rows + k + 1, :] = small[
                2 + EXPERTS : 3 + EXPERTS, k * all_heads : (k + 1) * all_heads
            ]
        seg = small[3 + EXPERTS : 4 + EXPERTS, 0:rows]
        seg_key_ref[:, p * rows : (p + 1) * rows] = seg
        seg_query_ref[p * sub : (p + 1) * sub, :] = jnp.sum(
            jnp.where(seg_pick, jnp.broadcast_to(seg, (sub, rows)), 0.0), axis=1, keepdims=True
        )
    part = shard // 2
    for c in range(2):

        @pl.when(place_ref[4] == c)
        def _():
            at = slice(c * part, (c + 1) * part)
            weights[:, at, :] = own_ref[:, half:, 0:base].astype(f32)
            at = slice((1 - c) * part, (2 - c) * part)
            weights[:, at, :] = other_ref[:, half:, 0:base].astype(f32)

    weight_ref[...] = weights[...].reshape(width, base).astype(bf16)
    gain = gain_one_ref[...]
    head_col = lax.broadcasted_iota(jnp.int32, (32, all_heads), 1)

    def norm(x):
        x = x.astype(f32)
        scale = lax.rsqrt(jnp.mean(x * x, axis=-1, keepdims=True) + EPS)
        return ((x * scale) * gain).astype(bf16)

    def norm_step(p, carry):
        normed_all[p, pl.ds(core_at, half), :] = norm(own_ref[p, 0:half, :])
        normed_all[p, pl.ds(other_at, half), :] = norm(other_ref[p, 0:half, :])
        return carry

    lax.fori_loop(0, groups, norm_step, 0, unroll=2)
    chunk = 4

    def project_step(c, carry):
        block = normed_all[pl.ds(c * chunk, chunk)].reshape(chunk * rows, width)
        result = dot(block, weight_ref[...]).astype(bf16)
        project[pl.ds(c * chunk, chunk)] = result.reshape(chunk, rows, 3 * head_width)
        pair_ref[pl.ds(c * chunk * rows, chunk * rows), :] = result[:, head_width:]
        return carry

    lax.fori_loop(0, groups // chunk, project_step, 0)

    def query_step(p, carry):
        query_ref[pl.ds(p * sub, sub), :] = project[p, pl.ds(query_at, sub), 0:head_width]
        return carry

    lax.fori_loop(0, groups, query_step, 0)
    factor = head_dim ** (-0.5)
    left = length - 2 * LANES
    right = length + LANES
    relative = relative_tile(place_ref[1], (tile, 3 * LANES), rows, sub)
    magnitude = jnp.abs(relative)
    for h in range(heads):
        at = h * head_dim
        mine = head_col == place_ref[2] + h
        column = jnp.sum(jnp.where(mine, table_ref[...], 0.0), axis=1, keepdims=True)
        entry = [column[b : b + 1, :] for b in range(32)]
        bias = jnp.where(relative > 0, entry[16], entry[0])
        for k, threshold in enumerate(LIMITS):
            value = jnp.where(relative > 0, entry[17 + k], entry[1 + k])
            bias = jnp.where(magnitude >= threshold, value, bias)
        strip[:, 0:left] = jnp.broadcast_to(entry[15], (tile, left))
        strip[:, left:right] = bias
        strip[:, right:] = jnp.broadcast_to(entry[31], (tile, strip.shape[1] - right))
        scores[...] = (
            dot(query_ref[:, at : at + head_dim], pair_ref[:, at : at + head_dim], ((1,), (1,)))
            * factor
        )

        def soft_step(qb, carry):
            start = pl.multiple_of(length - LANES - qb * LANES, LANES)
            for par in range(per):
                here = pl.ds(qb * tile + par * sub, sub)
                value = scores[here, :] + strip[par * sub : (par + 1) * sub, pl.ds(start, length)]
                same = seg_query_ref[here, :] == seg_key_ref[...]
                value = jnp.where(same, value, NEGATIVE)
                top = jnp.max(value, axis=-1, keepdims=True)
                value = jnp.exp(value - top)
                total = jnp.sum(value, axis=-1, keepdims=True)
                probs_ref[h, here, :] = (value * (1.0 / total)).astype(bf16)
            return carry

        lax.fori_loop(0, steps, soft_step, 0, unroll=2)
        attended_ref[:, at : at + head_dim] = dot(
            probs_ref[h], pair_ref[:, head_width + at : head_width + at + head_dim]
        ).astype(bf16)


def backward_kernel(
    place_ref,
    probs_ref,
    query_ref,
    pair_ref,
    grad_ref,
    d_all_ref,
    table_ref,
    scores,
    low,
    strip,
    flipped,
    d_query,
    *,
    groups,
    half,
    rows,
    sub,
    head_dim,
):
    query_at = pl.multiple_of(place_ref[1], sub)
    length = groups * rows
    head_width = query_ref.shape[1]
    heads = head_width // head_dim
    per = LANES // rows
    tile = per * sub
    steps = length // LANES
    factor = head_dim ** (-0.5)
    left = length - 2 * LANES
    right = length + LANES
    relative = relative_tile(place_ref[1], (tile, 3 * LANES), rows, sub)
    magnitude = jnp.abs(relative)
    count = jnp.zeros_like(relative)
    for threshold in LIMITS:
        count = count + (magnitude >= threshold).astype(jnp.int32)
    bucket = count + jnp.where(relative > 0, 16, 0)

    def lanes_sum(value):
        value = jnp.sum(value, axis=0, keepdims=True)
        total = value[:, 0:LANES]
        for k in range(1, value.shape[1] // LANES):
            total = total + value[:, k * LANES : (k + 1) * LANES]
        return total

    for h in range(heads):
        at = h * head_dim
        grad = grad_ref[:, at : at + head_dim]
        scores[...] = dot(
            grad, pair_ref[:, head_width + at : head_width + at + head_dim], ((1,), (1,))
        )
        strip[...] = jnp.zeros_like(strip)

        def score_step(qb, carry):
            start = pl.multiple_of(length - LANES - qb * LANES, LANES)
            for par in range(per):
                here = pl.ds(qb * tile + par * sub, sub)
                probs = probs_ref[h, here, :].astype(f32)
                value = scores[here, :]
                delta = jnp.sum(probs * value, axis=-1, keepdims=True)
                value = probs * (value - delta)
                low[here, :] = value.astype(bf16)
                strip[par * sub : (par + 1) * sub, pl.ds(start, length)] += value
            return carry

        lax.fori_loop(0, steps, score_step, 0, unroll=2)
        d_query[:, at : at + head_dim] = dot(low[...], pair_ref[:, at : at + head_dim]) * factor
        flipped[at : at + head_dim, :] = (
            dot(query_ref[:, at : at + head_dim], low[...], ((0,), (0,))) * factor
        )
        flipped[head_width + at : head_width + at + head_dim, :] = dot(
            grad, probs_ref[h], ((0,), (0,))
        )
        near = strip[:, left:right]
        for b in range(32):
            table_ref[h, b : b + 1, :] = lanes_sum(jnp.where(bucket == b, near, 0.0))
        table_ref[h, 15:16, :] += lanes_sum(strip[:, 0:left])
        table_ref[h, 31:32, :] += lanes_sum(strip[:, right:])
    d_all_ref[:, :, 0:head_width] = jnp.zeros((groups, rows, head_width), bf16)
    for c in range(length // LANES):
        block = flipped[:, c * LANES : (c + 1) * LANES].T.astype(bf16)
        d_all_ref[c * per : (c + 1) * per, :, head_width:] = block.reshape(
            per, rows, 2 * head_width
        )

    def place_step(p, carry):
        d_all_ref[p, pl.ds(query_at, sub), 0:head_width] = d_query[
            pl.ds(p * sub, sub), :
        ].astype(bf16)
        return carry

    lax.fori_loop(0, groups, place_step, 0)


def last_kernel(
    place_ref,
    d_own_ref,
    d_other_ref,
    weight_ref,
    normed_ref,
    own_ref,
    gain_two_ref,
    router_ref,
    table_ref,
    last_ref,
    d_sum,
    w_grad,
    gain_sum,
    small,
    *,
    groups,
    half,
    rows,
    shard,
    all_heads,
):
    core_at = pl.multiple_of(place_ref[0], half)
    width = weight_ref.shape[0]
    base = weight_ref.shape[1]
    part = shard // 2
    length = groups * rows
    d_sum[...] = (d_own_ref[...].astype(f32) + d_other_ref[...].astype(f32)).astype(bf16)
    gain_sum[...] = jnp.zeros_like(gain_sum)
    chunk = 4

    def normed_step(c, carry):
        at = pl.ds(c * chunk, chunk)
        block = d_sum[at, pl.ds(core_at, half), :].reshape(chunk * half, base)
        d_normed = dot(block, weight_ref[...], ((1,), (1,)))
        x = own_ref[at, 0:half, :].astype(f32).reshape(chunk * half, width)
        unit = x * lax.rsqrt(jnp.mean(x * x, axis=-1, keepdims=True) + EPS)
        gain_sum[...] += jnp.sum(d_normed * unit, axis=0, keepdims=True)
        last_ref[at, 0:half, :] = d_normed.reshape(chunk, half, width).astype(bf16)
        return carry

    lax.fori_loop(0, groups // chunk, normed_step, 0)
    w_grad[...] = dot(
        normed_ref[...].reshape(length, width), d_sum[...].reshape(length, base), ((0,), (0,))
    ).reshape(groups, shard, base)
    for c in range(2):

        @pl.when(place_ref[4] == c)
        def _():
            last_ref[:, half:, 0:base] = w_grad[:, c * part : (c + 1) * part, :].astype(bf16)

    heads = table_ref.shape[0]
    head_col = lax.broadcasted_iota(jnp.int32, (32, all_heads), 1)
    table = jnp.zeros((32, all_heads), f32)
    for h in range(heads):
        column = jnp.sum(table_ref[h], axis=1, keepdims=True)
        table = table + jnp.where(head_col == place_ref[2] + h, column, 0.0)
    table_rows = 32 // groups
    small[...] = jnp.zeros_like(small)
    for p in range(groups):
        at = slice(p * shard, (p + 1) * shard)
        small[p, 0:1, 0:shard] = gain_sum[:, at]
        small[p, 1:2, 0:shard] = gain_two_ref[:, at]
        small[p, 2 : 2 + EXPERTS, 0:shard] = router_ref[:, at]
        for k in range(table_rows):
            small[p, 2 + EXPERTS : 3 + EXPERTS, k * all_heads : (k + 1) * all_heads] = table[
                p * table_rows + k : p * table_rows + k + 1, :
            ]
    last_ref[:, half:, base:] = small[...].astype(bf16)


def out_grad_kernel(
    place_ref, attended_ref, other_ref, d_ref, d_other_ref, out_ref, total, *, groups, shard
):
    part = shard // 2
    width = total.shape[2]
    grad = dot(attended_ref[...], d_ref[...], ((0,), (0,)))
    grad = grad + dot(other_ref[...], d_other_ref[...], ((0,), (0,)))
    total[...] = grad.reshape(groups, shard, width)
    for c in range(2):

        @pl.when(place_ref[4] == c)
        def _():
            out_ref[...] = total[:, c * part : (c + 1) * part, :].astype(bf16)


def sum_kernel(
    place_ref, final_ref, keep_ref, give_ref, four_ref, low_ref, small_ref, *, half, seqs
):
    groups, _, width = final_ref.shape
    part = four_ref.shape[1]
    base = width - small_ref.shape[1]
    head_width = base // 3
    per_seq = groups // (2 * seqs)
    split = per_seq // HEAD_GROUPS
    mine = place_ref[3]
    yours = seqs - mine
    for l in range(seqs):

        def total(first):
            value = final_ref[first, 0:half, :].astype(f32)
            for k in range(1, per_seq):
                value = value + final_ref[first + k, 0:half, :].astype(f32)
            return value

        keep_ref[l] = total((mine + l) * per_seq)
        give_ref[l] = total((yours + l) * per_seq).astype(bf16)
    for g in range(HEAD_GROUPS):
        grad = jnp.zeros((part, base), f32)
        for s in range(2 * seqs):
            for t in range(split):
                grad = grad + final_ref[(s * HEAD_GROUPS + g) * split + t, half:, 0:base].astype(
                    f32
                )
        for i in range(3):
            four_ref[i, :, g * head_width : (g + 1) * head_width] = grad[
                :, i * head_width : (i + 1) * head_width
            ]
    low_ref[...] = four_ref[...].astype(bf16)
    small = final_ref[0, half:, base:].astype(f32)
    for p in range(1, groups):
        small = small + final_ref[p, half:, base:].astype(f32)
    small_ref[...] = small


def input_kernel(
    place_ref,
    keep_ref,
    given_ref,
    four_ref,
    other_ref,
    out_mine_ref,
    out_other_ref,
    small_ref,
    small_other_ref,
    x_ref,
    d_hidden_ref,
    gain_ref,
    input_ref,
    query_ref,
    key_ref,
    value_ref,
    out_ref,
    table_ref,
    gain_one_ref,
    gain_two_ref,
    router_ref,
    d_normed_ref,
    *,
    half,
):
    small = small_ref[...] + small_other_ref[...]
    shard = gain_one_ref.shape[1]
    heads = table_ref.shape[1]
    gain_one_ref[...] = small[0:1, 0:shard]
    gain_two_ref[...] = small[1:2, 0:shard]
    router_ref[...] = small[2 : 2 + EXPERTS, 0:shard]
    for k in range(table_ref.shape[0]):
        table_ref[k : k + 1, :] = small[2 + EXPERTS : 3 + EXPERTS, k * heads : (k + 1) * heads]
    core_at = pl.multiple_of(place_ref[0], half)
    other_at = pl.multiple_of(half - place_ref[0], half)
    seqs, rows, width = x_ref.shape
    part = four_ref.shape[1]
    d_normed_ref[:, pl.ds(core_at, half), :] = keep_ref[...]
    d_normed_ref[:, pl.ds(other_at, half), :] = given_ref[...].astype(f32)
    d_normed = d_normed_ref[...].reshape(seqs * rows, width)
    x = x_ref[...].reshape(seqs * rows, width).astype(f32)
    scale = lax.rsqrt(jnp.mean(x * x, axis=-1, keepdims=True) + EPS)
    unit = x * scale
    d_unit = d_normed * gain_ref[...]
    grad = scale * (d_unit - unit * jnp.mean(d_unit * unit, axis=-1, keepdims=True))
    input_ref[...] = (d_hidden_ref[...] + grad).reshape(seqs, rows, width)
    for c in range(2):

        @pl.when(place_ref[4] == c)
        def _():
            here = slice(c * part, (c + 1) * part)
            there = slice((1 - c) * part, (2 - c) * part)
            for i, ref in enumerate((query_ref, key_ref, value_ref)):
                ref[here, :] = four_ref[i]
                ref[there, :] = other_ref[i].astype(f32)
            out_ref[here, :] = out_mine_ref[...]
            out_ref[there, :] = out_other_ref[...]


def middle_kernel(
    place_ref,
    back_ref,
    swapped_ref,
    x_ref,
    out_ref,
    out_other_ref,
    gain_ref,
    router_ref,
    routes_ref,
    cotangent_ref,
    send_ref,
    attended_ref,
    hidden_ref,
    normed_ref,
    probs_ref,
    spread_ref,
    attended,
    *,
    half,
    sub,
    split,
    few,
    share,
):
    seqs, rows, width = attended.shape
    tokens = seqs * rows
    head_width = back_ref.shape[2]
    core_at = place_ref[0]
    first = place_ref[3]
    for l in range(seqs):
        for g in range(HEAD_GROUPS):
            lanes = slice(g * head_width, (g + 1) * head_width)
            for t in range(split):
                here = pl.multiple_of(core_at + t * sub, sub)
                there = pl.multiple_of(half - core_at + t * sub, sub)
                at = (l * HEAD_GROUPS + g) * split + t
                kept = first * (HEAD_GROUPS * split) + at
                attended[l, pl.ds(here, sub), lanes] = back_ref[kept]
                attended[l, pl.ds(there, sub), lanes] = swapped_ref[at]
    low = attended[...].reshape(tokens, width)
    attended_ref[...] = low
    out_half = width // 2
    here = pl.multiple_of(place_ref[4] * out_half, LANES)
    there = pl.multiple_of(out_half - place_ref[4] * out_half, LANES)
    hidden_ref[:, pl.ds(here, out_half)] = dot(low, out_ref[...])
    hidden_ref[:, pl.ds(there, out_half)] = dot(low, out_other_ref[...])
    hidden = x_ref[...].reshape(tokens, width).astype(f32) + hidden_ref[...]
    hidden_ref[...] = hidden
    scale = lax.rsqrt(jnp.mean(hidden * hidden, axis=-1, keepdims=True) + EPS)
    normed = ((hidden * scale) * gain_ref[...]).astype(bf16)
    normed_ref[...] = normed
    logits = dot(normed, router_ref[...].astype(bf16), ((1,), (1,)))
    logits = jnp.exp(logits - jnp.max(logits, axis=-1, keepdims=True))
    probs = logits / jnp.sum(logits, axis=-1, keepdims=True)
    probs_ref[...] = probs
    chosen = routes_ref[...]
    picked = (chosen == lax.broadcasted_iota(jnp.int32, (tokens, EXPERTS), 1)).astype(f32)
    gate = jnp.sum(probs * picked, axis=-1, keepdims=True)
    row = lax.broadcasted_iota(jnp.int32, (tokens, tokens), 0)
    col = lax.broadcasted_iota(jnp.int32, (tokens, tokens), 1)
    before = (col < row).astype(bf16)
    earlier = dot(before, picked.astype(bf16))
    slot = jnp.sum(earlier * picked, axis=-1, keepdims=True).astype(jnp.int32)
    spot = chosen * CAP + slot
    spread = (spot == lax.broadcasted_iota(jnp.int32, (tokens, EXPERTS * CAP), 1)).astype(bf16)
    spread_ref[...] = spread
    d_expert = (gate * cotangent_ref[...].reshape(tokens, width).astype(f32)).astype(bf16)
    for i, rows_in in enumerate((normed, d_expert)):
        rows_out = dot(spread, rows_in, ((0,), (0,))).astype(bf16)
        for e in range(EXPERTS):
            for k in range(share):
                send_ref[e * share + k, i * few : (i + 1) * few, :] = rows_out[
                    e * few : (e + 1) * few, :
                ]


def expert_kernel(arrived_ref, up_ref, down_ref, results_ref, act_ref, d_pre_ref, *, few):
    groups, _, width = arrived_ref.shape
    rows = groups * few
    received = arrived_ref[:, 0:few, :].reshape(rows, width)
    got = arrived_ref[:, few:, :].reshape(rows, width)
    root = 0.7978845608028654
    up, down = up_ref[...], down_ref[...]
    pre = dot(received, up)
    square = pre * pre
    bend = jnp.tanh(root * (pre + 0.044715 * (square * pre)))
    side = 0.5 * (1.0 + bend)
    act = (pre * side).astype(bf16)
    slope = side + 0.5 * pre * (1.0 - bend * bend) * (root * (1.0 + 3 * 0.044715 * square))
    d_pre = (dot(got, down, ((1,), (1,))) * slope).astype(bf16)
    act_ref[...] = act
    d_pre_ref[...] = d_pre
    out = dot(act, down).astype(bf16)
    back = dot(d_pre, up, ((1,), (1,))).astype(bf16)
    results_ref[:, 0:few, :] = out.reshape(groups, few, width)
    results_ref[:, few:, :] = back.reshape(groups, few, width)


def turn_kernel(
    place_ref,
    returned_ref,
    spread_ref,
    hidden_ref,
    normed_ref,
    probs_ref,
    routes_ref,
    cotangent_ref,
    gain_ref,
    router_ref,
    out_ref,
    out_other_ref,
    output_ref,
    d_hidden_ref,
    d_branch_ref,
    keep_ref,
    give_ref,
    router_grad_ref,
    gain_grad_ref,
    d_attended,
    *,
    half,
    sub,
    split,
    few,
    share,
):
    seqs, rows, width = output_ref.shape
    tokens = seqs * rows
    head_width = keep_ref.shape[2]
    core_at = place_ref[0]
    spread = spread_ref[...]

    def collect(at):
        pieces = []
        for e in range(EXPERTS):
            piece = returned_ref[e * share, at, :].astype(f32)
            for k in range(1, share):
                piece = piece + returned_ref[e * share + k, at, :].astype(f32)
            pieces.append(piece)
        value = jnp.concatenate(pieces, axis=0)
        high = value.astype(bf16)
        low = (value - high.astype(f32)).astype(bf16)
        return dot(spread, high) + dot(spread, low)

    expert_out = collect(slice(0, few))
    d_rows = collect(slice(few, 2 * few))
    hidden = hidden_ref[...]
    probs = probs_ref[...]
    picked = (
        routes_ref[...] == lax.broadcasted_iota(jnp.int32, (tokens, EXPERTS), 1)
    ).astype(f32)
    gate = jnp.sum(probs * picked, axis=-1, keepdims=True)
    output_ref[...] = (hidden + gate * expert_out).astype(bf16).reshape(seqs, rows, width)
    d_final = cotangent_ref[...].reshape(tokens, width).astype(f32)
    d_gate = jnp.sum(d_final * expert_out, axis=-1, keepdims=True)
    d_logits = gate * (picked - probs) * d_gate
    d_normed = d_rows
    for e in range(EXPERTS):
        d_normed = d_normed + d_logits[:, e : e + 1] * router_ref[e : e + 1, :]
    router_grad_ref[...] = lax.dot_general(
        d_logits,
        normed_ref[...].astype(f32),
        (((0,), (0,)), ((), ())),
        precision=lax.Precision.HIGHEST,
        preferred_element_type=f32,
    )
    scale = lax.rsqrt(jnp.mean(hidden * hidden, axis=-1, keepdims=True) + EPS)
    unit = hidden * scale
    gain_grad_ref[...] = jnp.sum(d_normed * unit, axis=0, keepdims=True)
    d_unit = d_normed * gain_ref[...]
    d_hidden = d_final + scale * (d_unit - unit * jnp.mean(d_unit * unit, axis=-1, keepdims=True))
    d_hidden_ref[...] = d_hidden
    d_branch = d_hidden.astype(bf16)
    d_branch_ref[...] = d_branch
    out_half = width // 2
    here = pl.multiple_of(place_ref[4] * out_half, LANES)
    there = pl.multiple_of(out_half - place_ref[4] * out_half, LANES)
    d_low = dot(d_branch_ref[:, pl.ds(here, out_half)], out_ref[...], ((1,), (1,)))
    d_low = d_low + dot(d_branch_ref[:, pl.ds(there, out_half)], out_other_ref[...], ((1,), (1,)))
    d_attended[...] = d_low.astype(bf16).reshape(seqs, rows, width)
    for l in range(seqs):
        for g in range(HEAD_GROUPS):
            lanes = slice(g * head_width, (g + 1) * head_width)
            for t in range(split):
                here = pl.multiple_of(core_at + t * sub, sub)
                there = pl.multiple_of(half - core_at + t * sub, sub)
                at = (l * HEAD_GROUPS + g) * split + t
                keep_ref[at] = d_attended[l, pl.ds(here, sub), lanes]
                give_ref[at] = d_attended[l, pl.ds(there, sub), lanes]


def exchange(value):
    return lax.all_to_all(value, "sq", split_axis=0, concat_axis=0, tiled=True)


def local(
    inputs,
    w_query,
    w_key,
    w_value,
    w_out,
    table,
    gain_one,
    gain_two,
    w_router,
    w_up,
    w_down,
    routes,
    segments,
    cotangent,
):
    seqs, rows, width = inputs.shape
    heads = table.shape[1]
    head_dim = width // heads
    reps = lax.axis_size("rep")
    groups = lax.axis_size("sq")
    length = rows * groups
    tokens = seqs * rows
    share = groups // EXPERTS
    half = rows // 2
    all_seqs = 2 * seqs
    split = groups // (all_seqs * HEAD_GROUPS)
    sub = half // split
    group_heads = heads // HEAD_GROUPS
    head_width = group_heads * head_dim
    shard = w_query.shape[0]
    part = shard // 2
    bucket_rows = table.shape[0]
    core = lax.axis_index("rep") % 2
    me = lax.axis_index("sq")
    group_at = (me // split) % HEAD_GROUPS
    first = core == 0
    pairs = [(i, i ^ 1) for i in range(reps)]

    def swap(value):
        return lax.ppermute(value, "rep", pairs)

    def by_core(own, other, axis):
        return jnp.where(
            first,
            jnp.concatenate([own, other], axis=axis),
            jnp.concatenate([other, own], axis=axis),
        )

    def mine(value, axis, size):
        return lax.dynamic_slice_in_dim(value, core * size, size, axis)

    def yours(value, axis, size):
        return lax.dynamic_slice_in_dim(value, (1 - core) * size, size, axis)

    def over_pairs(value):
        if reps == 2:
            return value
        sets = [list(range(0, reps, 2)), list(range(1, reps, 2))]
        return lax.psum(value, "rep", axis_index_groups=sets)

    smem = pl.BlockSpec(memory_space=pltpu.SMEM)
    vmem = pl.BlockSpec(memory_space=pltpu.VMEM)

    def cost(microseconds):
        return pl.CostEstimate(
            flops=microseconds * 900_000_000,
            bytes_accessed=microseconds * 1_000_000,
            transcendentals=0,
        )

    limit = pltpu.CompilerParams(vmem_limit_bytes=56 * 1024 * 1024)
    spare = width - 3 * head_width
    query_at = core * half + (me % split) * sub
    place = jnp.stack([core * half, query_at, group_at * group_heads, core * seqs, core])
    place = place.astype(jnp.int32)
    shard_table = bucket_rows * heads
    send = pl.pallas_call(
        partial(pack_kernel, half=half, split=split),
        name="pack",
        out_shape=jax.ShapeDtypeStruct((groups, half + part, width), bf16),
        in_specs=[smem] + [vmem] * 11,
        out_specs=vmem,
        scratch_shapes=[
            pltpu.VMEM((HEAD_GROUPS, part, 3 * head_width), f32),
            pltpu.VMEM((part, spare), f32),
        ],
        compiler_params=limit,
        cost_estimate=cost(3),
    )(
        place,
        inputs,
        swap(inputs),
        segments,
        swap(segments),
        w_query,
        w_key,
        w_value,
        gain_one.reshape(1, shard),
        gain_two.reshape(1, shard),
        w_router.T,
        table,
    )
    own = exchange(send)
    out_half = mine(w_out, 1, width // 2)
    out_send = jnp.broadcast_to(out_half[None], (groups, shard, width // 2))
    own, out_send, place, routes_flat = lax.optimization_barrier(
        (own, out_send, place, routes.reshape(tokens, 1))
    )
    other, out_send = lax.optimization_barrier((swap(own), out_send))
    out_mine = exchange(out_send)
    queries_count = groups * sub
    tile = (LANES // rows) * sub
    sizes = dict(groups=groups, half=half, rows=rows, sub=sub, head_dim=head_dim)
    (
        attended_part,
        probs,
        queries,
        pair,
        normed_all,
        w_group,
        gain_one_full,
        gain_two_full,
        router_full,
    ) = pl.pallas_call(
        partial(forward_kernel, shard=shard, all_heads=heads, **sizes),
        name="attention_forward",
        out_shape=(
            jax.ShapeDtypeStruct((queries_count, head_width), bf16),
            jax.ShapeDtypeStruct((group_heads, queries_count, length), bf16),
            jax.ShapeDtypeStruct((queries_count, head_width), bf16),
            jax.ShapeDtypeStruct((length, 2 * head_width), bf16),
            jax.ShapeDtypeStruct((groups, rows, width), bf16),
            jax.ShapeDtypeStruct((width, 3 * head_width), bf16),
            jax.ShapeDtypeStruct((1, width), f32),
            jax.ShapeDtypeStruct((1, width), f32),
            jax.ShapeDtypeStruct((EXPERTS, width), f32),
        ),
        in_specs=[smem] + [vmem] * 2,
        out_specs=[vmem] * 9,
        scratch_shapes=[
            pltpu.VMEM((groups, shard, 3 * head_width), f32),
            pltpu.VMEM((groups, rows, 3 * head_width), bf16),
            pltpu.VMEM((queries_count, length), f32),
            pltpu.VMEM((tile, 2 * length - LANES), f32),
            pltpu.VMEM((1, length), f32),
            pltpu.VMEM((queries_count, 1), f32),
            pltpu.VMEM((32, heads), f32),
        ],
        compiler_params=limit,
        cost_estimate=cost(60),
    )(place, own, other)
    attended_part, out_mine = lax.optimization_barrier((attended_part, out_mine))
    back = exchange(attended_part.reshape(groups, sub, head_width))
    out_mine = out_mine.reshape(width, width // 2)
    out_yours = swap(out_mine)
    back_given = swap(yours(back, 0, groups // 2))
    few = CAP
    pieces = dict(half=half, sub=sub, split=split, few=few)
    buffer, attended, hidden, normed_two, router_probs, spread = pl.pallas_call(
        partial(middle_kernel, share=share, **pieces),
        name="router_and_dispatch",
        out_shape=(
            jax.ShapeDtypeStruct((groups, 2 * few, width), bf16),
            jax.ShapeDtypeStruct((tokens, width), bf16),
            jax.ShapeDtypeStruct((tokens, width), f32),
            jax.ShapeDtypeStruct((tokens, width), bf16),
            jax.ShapeDtypeStruct((tokens, EXPERTS), f32),
            jax.ShapeDtypeStruct((tokens, EXPERTS * CAP), bf16),
        ),
        in_specs=[smem] + [vmem] * 9,
        out_specs=[vmem] * 6,
        scratch_shapes=[pltpu.VMEM((seqs, rows, width), bf16)],
        compiler_params=limit,
        cost_estimate=cost(5),
    )(
        place,
        back,
        back_given,
        inputs,
        out_mine,
        out_yours,
        gain_two_full,
        router_full,
        routes_flat,
        cotangent,
    )
    arrived = exchange(buffer)
    expert_rows = groups * few
    units_low = jax.ShapeDtypeStruct((expert_rows, w_up.shape[1]), bf16)
    results, act, d_pre = pl.pallas_call(
        partial(expert_kernel, few=few),
        name="experts",
        out_shape=(
            jax.ShapeDtypeStruct((groups, 2 * few, width), bf16),
            units_low,
            units_low,
        ),
        in_specs=[vmem] * 3,
        out_specs=[vmem] * 3,
        compiler_params=limit,
        cost_estimate=cost(8),
    )(arrived, w_up, w_down)
    returned = exchange(results)
    received = arrived[:, :few].reshape(expert_rows, width)
    got = arrived[:, few:].reshape(expert_rows, width)
    up_local = dot(received, d_pre, ((0,), (0,))).astype(bf16)
    down_local = dot(act, got, ((0,), (0,))).astype(bf16)
    returned, up_local, down_local = lax.optimization_barrier((returned, up_local, down_local))

    def both_reps(value):
        if reps == 2:
            return value.astype(f32) + swap(value).astype(f32)
        return lax.psum(value, "rep").astype(f32)

    output, d_hidden, d_branch, keep, give, router_grad, gain_two_grad = pl.pallas_call(
        partial(turn_kernel, share=share, **pieces),
        name="combine_and_turn",
        out_shape=(
            jax.ShapeDtypeStruct((seqs, rows, width), bf16),
            jax.ShapeDtypeStruct((tokens, width), f32),
            jax.ShapeDtypeStruct((tokens, width), bf16),
            jax.ShapeDtypeStruct((groups // 2, sub, head_width), bf16),
            jax.ShapeDtypeStruct((groups // 2, sub, head_width), bf16),
            jax.ShapeDtypeStruct((EXPERTS, width), f32),
            jax.ShapeDtypeStruct((1, width), f32),
        ),
        in_specs=[smem] + [vmem] * 11,
        out_specs=[vmem] * 7,
        scratch_shapes=[pltpu.VMEM((seqs, rows, width), bf16)],
        compiler_params=limit,
        cost_estimate=cost(5),
    )(
        place,
        returned,
        spread,
        hidden,
        normed_two,
        router_probs,
        routes_flat,
        cotangent,
        gain_two_full,
        router_full,
        out_mine,
        out_yours,
    )
    grads = exchange(by_core(keep, swap(give), 0))
    out_send = pl.pallas_call(
        partial(out_grad_kernel, groups=groups, shard=shard),
        name="out_grad",
        out_shape=jax.ShapeDtypeStruct((groups, part, width), bf16),
        in_specs=[smem] + [vmem] * 4,
        out_specs=vmem,
        scratch_shapes=[pltpu.VMEM((groups, shard, width), f32)],
        compiler_params=limit,
        cost_estimate=cost(3),
    )(place, attended, swap(attended), d_branch, swap(d_branch))
    grads, out_send = lax.optimization_barrier((grads, out_send))
    grads = grads.reshape(queries_count, head_width)
    out_back = exchange(out_send)
    d_all, table_part = pl.pallas_call(
        partial(backward_kernel, **sizes),
        name="attention_backward",
        out_shape=(
            jax.ShapeDtypeStruct((groups, rows, 3 * head_width), bf16),
            jax.ShapeDtypeStruct((group_heads, groups * bucket_rows, LANES), f32),
        ),
        in_specs=[smem] + [vmem] * 4,
        out_specs=[vmem] * 2,
        scratch_shapes=[
            pltpu.VMEM((queries_count, length), f32),
            pltpu.VMEM((queries_count, length), bf16),
            pltpu.VMEM((tile, 2 * length - LANES), f32),
            pltpu.VMEM((2 * head_width, length), f32),
            pltpu.VMEM((queries_count, head_width), f32),
        ],
        compiler_params=limit,
        cost_estimate=cost(1),
    )(place, probs, queries, pair, grads)
    out_sum = jnp.sum(out_back.astype(f32), axis=0)
    out_sum = over_pairs(out_sum)
    out_other = swap(out_sum)
    last = pl.pallas_call(
        partial(last_kernel, groups=groups, half=half, rows=rows, shard=shard, all_heads=heads),
        name="input_side",
        out_shape=jax.ShapeDtypeStruct((groups, half + part, width), bf16),
        in_specs=[smem] + [vmem] * 8,
        out_specs=vmem,
        scratch_shapes=[
            pltpu.VMEM((groups, rows, 3 * head_width), bf16),
            pltpu.VMEM((groups, shard, 3 * head_width), f32),
            pltpu.VMEM((1, width), f32),
            pltpu.VMEM((groups, part, spare), f32),
        ],
        compiler_params=limit,
        cost_estimate=cost(1),
    )(
        place,
        d_all,
        swap(d_all),
        w_group,
        normed_all,
        own,
        gain_two_grad,
        router_grad,
        table_part,
    )
    last, out_other = lax.optimization_barrier((last, out_other))
    final = exchange(last)
    up_grad = both_reps(up_local)
    down_grad = both_reps(down_local)
    final, up_grad, down_grad = lax.optimization_barrier((final, up_grad, down_grad))
    keep, give, four, four_low, small_sum = pl.pallas_call(
        partial(sum_kernel, half=half, seqs=seqs),
        name="sums",
        out_shape=(
            jax.ShapeDtypeStruct((seqs, half, width), f32),
            jax.ShapeDtypeStruct((seqs, half, width), bf16),
            jax.ShapeDtypeStruct((3, part, width), f32),
            jax.ShapeDtypeStruct((3, part, width), bf16),
            jax.ShapeDtypeStruct((part, spare), f32),
        ),
        in_specs=[smem] + [vmem],
        out_specs=[vmem] * 5,
        compiler_params=limit,
        cost_estimate=cost(2),
    )(place, final)
    if reps > 2:
        four, small_sum = over_pairs(four), over_pairs(small_sum)
        four_low = four.astype(bf16)
    (
        input_grad,
        query_grad,
        key_grad,
        value_grad,
        out_grad,
        table_grad,
        gain_one_grad,
        gain_two_grad,
        router_grad,
    ) = pl.pallas_call(
        partial(input_kernel, half=half),
        name="input_grad",
        out_shape=(jax.ShapeDtypeStruct((seqs, rows, width), f32),)
        + (jax.ShapeDtypeStruct((shard, width), f32),) * 4
        + (
            jax.ShapeDtypeStruct((bucket_rows, heads), f32),
            jax.ShapeDtypeStruct((1, shard), f32),
            jax.ShapeDtypeStruct((1, shard), f32),
            jax.ShapeDtypeStruct((EXPERTS, shard), f32),
        ),
        in_specs=[smem] + [vmem] * 11,
        out_specs=[vmem] * 9,
        scratch_shapes=[pltpu.VMEM((seqs, rows, width), f32)],
        compiler_params=limit,
        cost_estimate=cost(2),
    )(
        place,
        keep,
        swap(give),
        four,
        swap(four_low),
        out_sum,
        out_other,
        small_sum,
        swap(small_sum),
        inputs,
        d_hidden,
        gain_one_full,
    )
    return (
        output,
        input_grad,
        query_grad,
        key_grad,
        value_grad,
        out_grad,
        table_grad,
        gain_one_grad.reshape(shard),
        gain_two_grad.reshape(shard),
        router_grad.T,
        up_grad,
        down_grad,
    )


def solution(mesh):
    in_specs = (
        P("rep", "sq", None),
        P("sq", None),
        P("sq", None),
        P("sq", None),
        P("sq", None),
        P("sq", None),
        P("sq"),
        P("sq"),
        P("sq", None),
        P(None, "sq"),
        P("sq", None),
        P("rep", "sq", None),
        P("rep", "sq"),
        P("rep", "sq", None),
    )
    out_specs = (
        P("rep", "sq", None),
        P("rep", "sq", None),
        P("sq", None),
        P("sq", None),
        P("sq", None),
        P("sq", None),
        P("sq", None),
        P("sq"),
        P("sq"),
        P("sq", None),
        P(None, "sq"),
        P("sq", None),
    )
    return jax.shard_map(local, mesh=mesh, in_specs=in_specs, out_specs=out_specs, check_vma=False)
```

```python
from functools import partial

import jax
import jax.numpy as jnp
from jax import lax
from jax.experimental import pallas as pl
from jax.experimental.pallas import tpu as pltpu
from jax.sharding import PartitionSpec as P

EXPERTS = 8
CAP = 32
HEAD_GROUPS = 4
EPS = 1e-06
NEGATIVE = -1e30
LIMITS = (1, 2, 3, 4, 5, 6, 7, 8, 12, 16, 23, 32, 46, 64, 91)
LANES = 128
f32 = jnp.float32
bf16 = jnp.bfloat16


def dot(a, b, dims=((1,), (0,))):
    return lax.dot_general(a, b, (dims, ((), ())), preferred_element_type=f32)


def relative_tile(offset, shape, rows, sub):
    row = lax.broadcasted_iota(jnp.int32, shape, 0)
    col = lax.broadcasted_iota(jnp.int32, shape, 1)
    return col - LANES - (rows * (row // sub) + offset + row % sub)


def pack_kernel(
    place_ref,
    marks_ref,
    marks_other_ref,
    query_ref,
    key_ref,
    value_ref,
    gain_one_ref,
    gain_two_ref,
    router_ref,
    table_ref,
    send_ref,
    weights,
    small,
    *,
    split,
):
    seqs = marks_ref.shape[0]
    rows = marks_ref.shape[1] // 2
    shard, width = query_ref.shape
    part = shard // 2
    head_width = width // HEAD_GROUPS
    base = 3 * head_width
    per_seq = HEAD_GROUPS * split
    heads = table_ref.shape[1]
    for c in range(2):

        @pl.when(place_ref[4] == c)
        def _():
            at = slice(c * part, (c + 1) * part)
            for i, ref in enumerate((query_ref, key_ref, value_ref)):
                for g in range(HEAD_GROUPS):
                    weights[g, :, i * head_width : (i + 1) * head_width] = ref[
                        at, g * head_width : (g + 1) * head_width
                    ].astype(f32)

    small[...] = jnp.zeros_like(small)
    small[0:1, 0:shard] = gain_one_ref[...].astype(f32)
    small[1:2, 0:shard] = gain_two_ref[...].astype(f32)
    small[2 : 2 + EXPERTS, 0:shard] = router_ref[...].astype(f32)
    for k in range(table_ref.shape[0]):
        small[2 + EXPERTS : 3 + EXPERTS, k * heads : (k + 1) * heads] = table_ref[
            k : k + 1, :
        ].astype(f32)
    for c in range(2):
        marks = marks_ref if c == 0 else marks_other_ref
        first = (place_ref[3] if c == 0 else seqs - place_ref[3]) * per_seq
        for l in range(seqs):
            small[3 + EXPERTS : 4 + EXPERTS, 0 : 2 * rows] = marks[l : l + 1, :].astype(f32)
            for k in range(per_seq):
                at = first + l * per_seq + k
                send_ref[at, :, 0:base] = weights[k // split].astype(bf16)
                send_ref[at, :, base:] = small[...].astype(bf16)


def forward_kernel(
    place_ref,
    own_ref,
    other_ref,
    *refs,
    groups,
    half,
    rows,
    sub,
    head_dim,
    shard,
    all_heads,
):
    chips = (len(refs) - 17) // 4
    x_refs = refs[: 2 * chips]
    (
        probs_ref,
        query_ref,
        pair_ref,
        normed_all,
        weight_ref,
        gain_one_ref,
        gain_two_ref,
        router_ref,
        routes_ref,
    ) = refs[2 * chips : 2 * chips + 9]
    pieces = refs[2 * chips + 9 : -8]
    weights, project, scores, strip, seg_key_ref, seg_query_ref, table_ref, attended_ref = refs[-8:]
    query_at = pl.multiple_of(place_ref[1], sub)
    width = gain_one_ref.shape[1]
    length = groups * rows
    heads = attended_ref.shape[1] // head_dim
    head_width = heads * head_dim
    per = LANES // rows
    tile = per * sub
    steps = length // LANES
    base = 3 * head_width
    table_rows = 32 // groups
    seg_row = lax.broadcasted_iota(jnp.int32, (sub, rows), 0)
    seg_col = lax.broadcasted_iota(jnp.int32, (sub, rows), 1)
    seg_pick = seg_col == seg_row + place_ref[1]
    for p in range(groups):
        at = slice(p * shard, (p + 1) * shard)
        small = own_ref[p, :, base:].astype(f32)
        gain_one_ref[:, at] = small[0:1, 0:shard]
        gain_two_ref[:, at] = small[1:2, 0:shard]
        router_ref[:, at] = small[2 : 2 + EXPERTS, 0:shard]
        for k in range(table_rows):
            table_ref[p * table_rows + k : p * table_rows + k + 1, :] = small[
                2 + EXPERTS : 3 + EXPERTS, k * all_heads : (k + 1) * all_heads
            ]
        seg = small[3 + EXPERTS : 4 + EXPERTS, 0:rows]
        routes_ref[p : p + 1, :] = small[3 + EXPERTS : 4 + EXPERTS, rows : 2 * rows]
        seg_key_ref[:, p * rows : (p + 1) * rows] = seg
        seg_query_ref[p * sub : (p + 1) * sub, :] = jnp.sum(
            jnp.where(seg_pick, jnp.broadcast_to(seg, (sub, rows)), 0.0), axis=1, keepdims=True
        )
    part = shard // 2
    for c in range(2):

        @pl.when(place_ref[4] == c)
        def _():
            at = slice(c * part, (c + 1) * part)
            weights[:, at, :] = own_ref[:, :, 0:base].astype(f32)
            at = slice((1 - c) * part, (2 - c) * part)
            weights[:, at, :] = other_ref[:, :, 0:base].astype(f32)

    weight_ref[...] = weights[...].reshape(width, base).astype(bf16)
    gain = gain_one_ref[...]
    head_col = lax.broadcasted_iota(jnp.int32, (32, all_heads), 1)

    def norm(x):
        x = x.astype(f32)
        scale = lax.rsqrt(jnp.mean(x * x, axis=-1, keepdims=True) + EPS)
        return ((x * scale) * gain).astype(bf16)

    for k in range(chips):
        for c in range(2):
            at = 2 * (place_ref[4] ^ c) * chips + (place_ref[5] ^ k)
            for b in range(2):
                normed_all[at + b * chips] = norm(x_refs[c * chips + k][b])
    chunk = 4

    def project_step(c, carry):
        block = normed_all[pl.ds(c * chunk, chunk)].reshape(chunk * rows, width)
        result = dot(block, weight_ref[...]).astype(bf16)
        project[pl.ds(c * chunk, chunk)] = result.reshape(chunk, rows, 3 * head_width)
        pair_ref[pl.ds(c * chunk * rows, chunk * rows), :] = result[:, head_width:]
        return carry

    lax.fori_loop(0, groups // chunk, project_step, 0)

    def query_step(p, carry):
        query_ref[pl.ds(p * sub, sub), :] = project[p, pl.ds(query_at, sub), 0:head_width]
        return carry

    lax.fori_loop(0, groups, query_step, 0)
    factor = head_dim ** (-0.5)
    left = length - 2 * LANES
    right = length + LANES
    relative = relative_tile(place_ref[1], (tile, 3 * LANES), rows, sub)
    magnitude = jnp.abs(relative)
    for h in range(heads):
        at = h * head_dim
        mine = head_col == place_ref[2] + h
        column = jnp.sum(jnp.where(mine, table_ref[...], 0.0), axis=1, keepdims=True)
        entry = [column[b : b + 1, :] for b in range(32)]
        bias = jnp.where(relative > 0, entry[16], entry[0])
        for k, threshold in enumerate(LIMITS):
            value = jnp.where(relative > 0, entry[17 + k], entry[1 + k])
            bias = jnp.where(magnitude >= threshold, value, bias)
        strip[:, 0:left] = jnp.broadcast_to(entry[15], (tile, left))
        strip[:, left:right] = bias
        strip[:, right:] = jnp.broadcast_to(entry[31], (tile, strip.shape[1] - right))
        scores[...] = (
            dot(query_ref[:, at : at + head_dim], pair_ref[:, at : at + head_dim], ((1,), (1,)))
            * factor
        )

        def soft_step(qb, carry):
            start = pl.multiple_of(length - LANES - qb * LANES, LANES)
            for par in range(per):
                here = pl.ds(qb * tile + par * sub, sub)
                value = scores[here, :] + strip[par * sub : (par + 1) * sub, pl.ds(start, length)]
                same = seg_query_ref[here, :] == seg_key_ref[...]
                value = jnp.where(same, value, NEGATIVE)
                top = jnp.max(value, axis=-1, keepdims=True)
                value = jnp.exp(value - top)
                total = jnp.sum(value, axis=-1, keepdims=True)
                probs_ref[h, here, :] = (value * (1.0 / total)).astype(bf16)
            return carry

        lax.fori_loop(0, steps, soft_step, 0, unroll=2)
        attended_ref[:, at : at + head_dim] = dot(
            probs_ref[h], pair_ref[:, head_width + at : head_width + at + head_dim]
        ).astype(bf16)
    for k in range(len(pieces) // 2):
        for c in range(2):
            at = 2 * (place_ref[4] ^ c) * (len(pieces) // 2) + (place_ref[5] ^ k)
            for b in range(2):
                block = at + b * (len(pieces) // 2)
                rows_at = pl.ds(pl.multiple_of(block * sub, sub), sub)
                pieces[2 * k + c][b] = attended_ref[rows_at, :]


def backward_kernel(
    place_ref,
    probs_ref,
    query_ref,
    pair_ref,
    *refs,
    groups,
    half,
    rows,
    sub,
    head_dim,
):
    pieces = refs[:-8]
    d_all_ref, table_ref, scores, low, strip, flipped, d_query, grad_ref = refs[-8:]
    for k in range(len(pieces) // 2):
        for c in range(2):
            at = 2 * (place_ref[4] ^ c) * (len(pieces) // 2) + (place_ref[5] ^ k)
            for b in range(2):
                block = at + b * (len(pieces) // 2)
                rows_at = pl.ds(pl.multiple_of(block * sub, sub), sub)
                grad_ref[rows_at, :] = pieces[2 * k + c][b]
    query_at = pl.multiple_of(place_ref[1], sub)
    length = groups * rows
    head_width = query_ref.shape[1]
    heads = head_width // head_dim
    per = LANES // rows
    tile = per * sub
    steps = length // LANES
    factor = head_dim ** (-0.5)
    left = length - 2 * LANES
    right = length + LANES
    relative = relative_tile(place_ref[1], (tile, 3 * LANES), rows, sub)
    magnitude = jnp.abs(relative)
    count = jnp.zeros_like(relative)
    for threshold in LIMITS:
        count = count + (magnitude >= threshold).astype(jnp.int32)
    bucket = count + jnp.where(relative > 0, 16, 0)

    def lanes_sum(value):
        value = jnp.sum(value, axis=0, keepdims=True)
        total = value[:, 0:LANES]
        for k in range(1, value.shape[1] // LANES):
            total = total + value[:, k * LANES : (k + 1) * LANES]
        return total

    for h in range(heads):
        at = h * head_dim
        grad = grad_ref[:, at : at + head_dim]
        scores[...] = dot(
            grad, pair_ref[:, head_width + at : head_width + at + head_dim], ((1,), (1,))
        )
        strip[...] = jnp.zeros_like(strip)

        def score_step(qb, carry):
            start = pl.multiple_of(length - LANES - qb * LANES, LANES)
            for par in range(per):
                here = pl.ds(qb * tile + par * sub, sub)
                probs = probs_ref[h, here, :].astype(f32)
                value = scores[here, :]
                delta = jnp.sum(probs * value, axis=-1, keepdims=True)
                value = probs * (value - delta)
                low[here, :] = value.astype(bf16)
                strip[par * sub : (par + 1) * sub, pl.ds(start, length)] += value
            return carry

        lax.fori_loop(0, steps, score_step, 0, unroll=2)
        d_query[:, at : at + head_dim] = dot(low[...], pair_ref[:, at : at + head_dim]) * factor
        flipped[at : at + head_dim, :] = (
            dot(query_ref[:, at : at + head_dim], low[...], ((0,), (0,))) * factor
        )
        flipped[head_width + at : head_width + at + head_dim, :] = dot(
            grad, probs_ref[h], ((0,), (0,))
        )
        near = strip[:, left:right]
        for b in range(32):
            table_ref[h, b : b + 1, :] = lanes_sum(jnp.where(bucket == b, near, 0.0))
        table_ref[h, 15:16, :] += lanes_sum(strip[:, 0:left])
        table_ref[h, 31:32, :] += lanes_sum(strip[:, right:])
    d_all_ref[:, :, 0:head_width] = jnp.zeros((groups, rows, head_width), bf16)
    for c in range(length // LANES):
        block = flipped[:, c * LANES : (c + 1) * LANES].T.astype(bf16)
        d_all_ref[c * per : (c + 1) * per, :, head_width:] = block.reshape(
            per, rows, 2 * head_width
        )

    def place_step(p, carry):
        d_all_ref[p, pl.ds(query_at, sub), 0:head_width] = d_query[
            pl.ds(p * sub, sub), :
        ].astype(bf16)
        return carry

    lax.fori_loop(0, groups, place_step, 0)


def rows_kernel(
    place_ref,
    d_own_ref,
    d_other_ref,
    weight_ref,
    normed_ref,
    gain_ref,
    rows_ref,
    d_sum,
    gain_sum,
    *,
    half,
):
    core_at = pl.multiple_of(place_ref[0], half)
    groups, _, base = d_own_ref.shape
    chips = rows_ref.shape[0]
    width = weight_ref.shape[0]
    d_sum[...] = (d_own_ref[...].astype(f32) + d_other_ref[...].astype(f32)).astype(bf16)
    gain_sum[...] = jnp.zeros_like(gain_sum)
    chunk = 4

    def normed_step(c, carry):
        at = pl.ds(c * chunk, chunk)
        block = d_sum[at, pl.ds(core_at, half), :].reshape(chunk * half, base)
        d_normed = dot(block, weight_ref[...], ((1,), (1,)))
        normed = normed_ref[at, pl.ds(core_at, half), :].astype(f32).reshape(chunk * half, width)
        gain_sum[...] += jnp.sum(d_normed * normed, axis=0, keepdims=True)
        d_rows = d_normed.reshape(chunk, half, width).astype(bf16)
        for k in range(chunk):
            p = c * chunk + k
            rows_ref[lax.rem(p, chips), lax.div(p, chips)] = d_rows[k]
        return carry

    lax.fori_loop(0, groups // chunk, normed_step, 0)
    gain_sum[...] = gain_sum[...] / gain_ref[...]


def weight_kernel(
    place_ref,
    d_sum,
    normed_ref,
    gain_sum,
    gain_two_ref,
    router_ref,
    table_ref,
    last_ref,
    w_grad,
    small,
    *,
    shard,
    all_heads,
):
    groups, rows, width = normed_ref.shape
    base = d_sum.shape[2]
    part = shard // 2
    length = groups * rows
    w_grad[...] = dot(
        normed_ref[...].reshape(length, width), d_sum[...].reshape(length, base), ((0,), (0,))
    ).reshape(groups, shard, base)
    for c in range(2):

        @pl.when(place_ref[4] == c)
        def _():
            last_ref[:, :, 0:base] = w_grad[:, c * part : (c + 1) * part, :].astype(bf16)

    heads = table_ref.shape[0]
    head_col = lax.broadcasted_iota(jnp.int32, (32, all_heads), 1)
    table = jnp.zeros((32, all_heads), f32)
    for h in range(heads):
        column = jnp.sum(table_ref[h], axis=1, keepdims=True)
        table = table + jnp.where(head_col == place_ref[2] + h, column, 0.0)
    table_rows = 32 // groups
    small[...] = jnp.zeros_like(small)
    for p in range(groups):
        at = slice(p * shard, (p + 1) * shard)
        small[p, 0:1, 0:shard] = gain_sum[:, at]
        small[p, 1:2, 0:shard] = gain_two_ref[:, at]
        small[p, 2 : 2 + EXPERTS, 0:shard] = router_ref[:, at]
        for k in range(table_rows):
            small[p, 2 + EXPERTS : 3 + EXPERTS, k * all_heads : (k + 1) * all_heads] = table[
                p * table_rows + k : p * table_rows + k + 1, :
            ]
    last_ref[:, :, base:] = small[...].astype(bf16)


def out_grad_kernel(
    place_ref, attended_ref, other_ref, d_ref, d_other_ref, out_ref, total, *, groups, shard
):
    part = shard // 2
    width = total.shape[2]
    grad = dot(attended_ref[...], d_ref[...], ((0,), (0,)))
    grad = grad + dot(other_ref[...], d_other_ref[...], ((0,), (0,)))
    total[...] = grad.reshape(groups, shard, width)
    for c in range(2):

        @pl.when(place_ref[4] == c)
        def _():
            out_ref[...] = total[:, c * part : (c + 1) * part, :].astype(bf16)


def sum_kernel(final_ref, four_ref, low_ref, small_ref, *, seqs):
    groups, part, width = final_ref.shape
    base = width - small_ref.shape[1]
    head_width = base // 3
    split = groups // (2 * seqs * HEAD_GROUPS)
    for g in range(HEAD_GROUPS):
        grad = jnp.zeros((part, base), f32)
        for s in range(2 * seqs):
            for t in range(split):
                at = (s * HEAD_GROUPS + g) * split + t
                grad = grad + final_ref[at, :, 0:base].astype(f32)
        for i in range(3):
            four_ref[i, :, g * head_width : (g + 1) * head_width] = grad[
                :, i * head_width : (i + 1) * head_width
            ]
    low_ref[...] = four_ref[...].astype(bf16)
    small = final_ref[0, :, base:].astype(f32)
    for p in range(1, groups):
        small = small + final_ref[p, :, base:].astype(f32)
    small_ref[...] = small


def total_kernel(place_ref, rows_ref, keep_ref, give_ref):
    blocks = keep_ref.shape[0]
    for b in range(blocks):

        def total(w):
            value = rows_ref[0, w].astype(f32)
            for j in range(1, rows_ref.shape[0]):
                value = value + rows_ref[j, w].astype(f32)
            return value

        keep_ref[b] = total(place_ref[4] * blocks + b)
        give_ref[b] = total((1 - place_ref[4]) * blocks + b).astype(bf16)


def token_kernel(
    place_ref,
    x_ref,
    d_hidden_ref,
    gain_ref,
    keep_ref,
    given_ref,
    first_ref,
    second_ref,
    d_normed_ref,
    grad_ref,
    *,
    half,
):
    blocks, rows, width = x_ref.shape
    core_at = pl.multiple_of(place_ref[0], half)
    other_at = pl.multiple_of(half - place_ref[0], half)
    d_normed_ref[:, pl.ds(core_at, half), :] = keep_ref[...]
    d_normed_ref[:, pl.ds(other_at, half), :] = given_ref[...].astype(f32)
    d_normed = d_normed_ref[...].reshape(blocks * rows, width)
    x = x_ref[...].reshape(blocks * rows, width).astype(f32)
    scale = lax.rsqrt(jnp.mean(x * x, axis=-1, keepdims=True) + EPS)
    unit = x * scale
    d_unit = d_normed * gain_ref[...]
    grad = scale * (d_unit - unit * jnp.mean(d_unit * unit, axis=-1, keepdims=True))
    grad_ref[...] = (d_hidden_ref[...] + grad).reshape(blocks, rows, width)
    first_ref[...] = grad_ref[place_ref[7]].astype(bf16)
    second_ref[...] = grad_ref[1 - place_ref[7]].astype(bf16)


def input_kernel(
    place_ref,
    grad_first_ref,
    grad_second_ref,
    out_first_ref,
    out_second_ref,
    four_ref,
    other_ref,
    out_mine_ref,
    out_other_ref,
    small_ref,
    small_other_ref,
    output_ref,
    input_ref,
    query_ref,
    key_ref,
    value_ref,
    out_ref,
    table_ref,
    gain_one_ref,
    gain_two_ref,
    router_ref,
):
    output_ref[place_ref[7]] = out_first_ref[...]
    output_ref[1 - place_ref[7]] = out_second_ref[...]
    input_ref[place_ref[7]] = grad_first_ref[...].astype(f32)
    input_ref[1 - place_ref[7]] = grad_second_ref[...].astype(f32)
    small = small_ref[...] + small_other_ref[...]
    shard = gain_one_ref.shape[1]
    heads = table_ref.shape[1]
    gain_one_ref[...] = small[0:1, 0:shard]
    gain_two_ref[...] = small[1:2, 0:shard]
    router_ref[...] = small[2 : 2 + EXPERTS, 0:shard]
    for k in range(table_ref.shape[0]):
        table_ref[k : k + 1, :] = small[2 + EXPERTS : 3 + EXPERTS, k * heads : (k + 1) * heads]
    part = four_ref.shape[1]
    for c in range(2):

        @pl.when(place_ref[4] == c)
        def _():
            here = slice(c * part, (c + 1) * part)
            there = slice((1 - c) * part, (2 - c) * part)
            for i, ref in enumerate((query_ref, key_ref, value_ref)):
                ref[here, :] = four_ref[i]
                ref[there, :] = other_ref[i].astype(f32)
            out_ref[here, :] = out_mine_ref[...]
            out_ref[there, :] = out_other_ref[...]


def middle_kernel(
    place_ref,
    x_ref,
    out_ref,
    out_other_ref,
    gain_ref,
    router_ref,
    routes_in_ref,
    first_ref,
    second_ref,
    *refs,
    half,
    sub,
    split,
    few,
    share,
):
    pieces = refs[:-11]
    (
        send_ref,
        attended_ref,
        hidden_ref,
        normed_ref,
        probs_ref,
        spread_ref,
        cotangent_ref,
        routes_ref,
        attended,
        stage,
        routes_turned,
    ) = refs[-11:]
    blocks, rows, width = attended.shape
    tokens = blocks * rows
    head_width = width // HEAD_GROUPS
    for k in range(len(pieces) // 2):
        for c in range(2):
            stage[place_ref[5] ^ k, place_ref[4] ^ c] = pieces[2 * k + c][...]
    for g in range(HEAD_GROUPS):
        lanes = slice(g * head_width, (g + 1) * head_width)
        for t in range(split):
            for c in range(2):
                at = c * half + t * sub
                attended[:, at : at + sub, lanes] = stage[g * split + t, c]
    cotangent_ref[place_ref[7]] = first_ref[...]
    cotangent_ref[1 - place_ref[7]] = second_ref[...]
    routes_turned[...] = routes_in_ref[...].T
    block_col = lax.broadcasted_iota(jnp.int32, routes_turned.shape, 1)
    for b in range(blocks):
        mine = block_col == place_ref[6] + b * (len(pieces) // 2)
        column = jnp.sum(jnp.where(mine, routes_turned[...], 0.0), axis=1, keepdims=True)
        routes_ref[b * rows : (b + 1) * rows, :] = column.astype(jnp.int32)
    low = attended[...].reshape(tokens, width)
    attended_ref[...] = low
    out_half = width // 2
    here = pl.multiple_of(place_ref[4] * out_half, LANES)
    there = pl.multiple_of(out_half - place_ref[4] * out_half, LANES)
    hidden_ref[:, pl.ds(here, out_half)] = dot(low, out_ref[...])
    hidden_ref[:, pl.ds(there, out_half)] = dot(low, out_other_ref[...])
    hidden = x_ref[...].reshape(tokens, width).astype(f32) + hidden_ref[...]
    hidden_ref[...] = hidden
    scale = lax.rsqrt(jnp.mean(hidden * hidden, axis=-1, keepdims=True) + EPS)
    normed = ((hidden * scale) * gain_ref[...]).astype(bf16)
    normed_ref[...] = normed
    logits = dot(normed, router_ref[...].astype(bf16), ((1,), (1,)))
    logits = jnp.exp(logits - jnp.max(logits, axis=-1, keepdims=True))
    probs = logits / jnp.sum(logits, axis=-1, keepdims=True)
    probs_ref[...] = probs
    chosen = routes_ref[...]
    picked = (chosen == lax.broadcasted_iota(jnp.int32, (tokens, EXPERTS), 1)).astype(f32)
    gate = jnp.sum(probs * picked, axis=-1, keepdims=True)
    row = lax.broadcasted_iota(jnp.int32, (tokens, tokens), 0)
    col = lax.broadcasted_iota(jnp.int32, (tokens, tokens), 1)
    before = (col < row).astype(bf16)
    earlier = dot(before, picked.astype(bf16))
    slot = jnp.sum(earlier * picked, axis=-1, keepdims=True).astype(jnp.int32)
    spot = chosen * CAP + slot
    spread = (spot == lax.broadcasted_iota(jnp.int32, (tokens, EXPERTS * CAP), 1)).astype(bf16)
    spread_ref[...] = spread
    d_expert = (gate * cotangent_ref[...].reshape(tokens, width).astype(f32)).astype(bf16)
    for i, rows_in in enumerate((normed, d_expert)):
        rows_out = dot(spread, rows_in, ((0,), (0,))).astype(bf16)
        for e in range(EXPERTS):
            for k in range(share):
                send_ref[e * share + k, i * few : (i + 1) * few, :] = rows_out[
                    e * few : (e + 1) * few, :
                ]


def expert_kernel(arrived_ref, up_ref, down_ref, results_ref, act_ref, d_pre_ref, *, few):
    groups, _, width = arrived_ref.shape
    rows = groups * few
    received = arrived_ref[:, 0:few, :].reshape(rows, width)
    got = arrived_ref[:, few:, :].reshape(rows, width)
    root = 0.7978845608028654
    up, down = up_ref[...], down_ref[...]
    pre = dot(received, up)
    square = pre * pre
    bend = jnp.tanh(root * (pre + 0.044715 * (square * pre)))
    side = 0.5 * (1.0 + bend)
    act = (pre * side).astype(bf16)
    slope = side + 0.5 * pre * (1.0 - bend * bend) * (root * (1.0 + 3 * 0.044715 * square))
    d_pre = (dot(got, down, ((1,), (1,))) * slope).astype(bf16)
    act_ref[...] = act
    d_pre_ref[...] = d_pre
    out = dot(act, down).astype(bf16)
    back = dot(d_pre, up, ((1,), (1,))).astype(bf16)
    results_ref[:, 0:few, :] = out.reshape(groups, few, width)
    results_ref[:, few:, :] = back.reshape(groups, few, width)


def turn_kernel(
    place_ref,
    returned_ref,
    spread_ref,
    hidden_ref,
    normed_ref,
    probs_ref,
    routes_ref,
    cotangent_ref,
    gain_ref,
    router_ref,
    out_ref,
    out_other_ref,
    *refs,
    half,
    sub,
    split,
    few,
    share,
):
    pieces = refs[:-9]
    (
        first_ref,
        second_ref,
        d_hidden_ref,
        d_branch_ref,
        router_grad_ref,
        gain_grad_ref,
        output,
        d_attended,
        stage,
    ) = refs[-9:]
    seqs, rows, width = cotangent_ref.shape
    tokens = seqs * rows
    head_width = width // HEAD_GROUPS
    spread = spread_ref[...]

    def collect(at):
        pieces = []
        for e in range(EXPERTS):
            piece = returned_ref[e * share, at, :].astype(f32)
            for k in range(1, share):
                piece = piece + returned_ref[e * share + k, at, :].astype(f32)
            pieces.append(piece)
        value = jnp.concatenate(pieces, axis=0)
        high = value.astype(bf16)
        low = (value - high.astype(f32)).astype(bf16)
        return dot(spread, high) + dot(spread, low)

    expert_out = collect(slice(0, few))
    d_rows = collect(slice(few, 2 * few))
    hidden = hidden_ref[...]
    probs = probs_ref[...]
    picked = (
        routes_ref[...] == lax.broadcasted_iota(jnp.int32, (tokens, EXPERTS), 1)
    ).astype(f32)
    gate = jnp.sum(probs * picked, axis=-1, keepdims=True)
    output[...] = (hidden + gate * expert_out).astype(bf16).reshape(seqs, rows, width)
    first_ref[...] = output[place_ref[7]]
    second_ref[...] = output[1 - place_ref[7]]
    d_final = cotangent_ref[...].reshape(tokens, width).astype(f32)
    d_gate = jnp.sum(d_final * expert_out, axis=-1, keepdims=True)
    d_logits = gate * (picked - probs) * d_gate
    d_normed = d_rows
    for e in range(EXPERTS):
        d_normed = d_normed + d_logits[:, e : e + 1] * router_ref[e : e + 1, :]
    router_grad_ref[...] = lax.dot_general(
        d_logits,
        normed_ref[...].astype(f32),
        (((0,), (0,)), ((), ())),
        precision=lax.Precision.HIGHEST,
        preferred_element_type=f32,
    )
    scale = lax.rsqrt(jnp.mean(hidden * hidden, axis=-1, keepdims=True) + EPS)
    unit = hidden * scale
    gain_grad_ref[...] = jnp.sum(d_normed * unit, axis=0, keepdims=True)
    d_unit = d_normed * gain_ref[...]
    d_hidden = d_final + scale * (d_unit - unit * jnp.mean(d_unit * unit, axis=-1, keepdims=True))
    d_hidden_ref[...] = d_hidden
    d_branch = d_hidden.astype(bf16)
    d_branch_ref[...] = d_branch
    out_half = width // 2
    here = pl.multiple_of(place_ref[4] * out_half, LANES)
    there = pl.multiple_of(out_half - place_ref[4] * out_half, LANES)
    d_low = dot(d_branch_ref[:, pl.ds(here, out_half)], out_ref[...], ((1,), (1,)))
    d_low = d_low + dot(d_branch_ref[:, pl.ds(there, out_half)], out_other_ref[...], ((1,), (1,)))
    d_attended[...] = d_low.astype(bf16).reshape(seqs, rows, width)
    for g in range(HEAD_GROUPS):
        lanes = slice(g * head_width, (g + 1) * head_width)
        for t in range(split):
            for c in range(2):
                at = c * half + t * sub
                stage[g * split + t, c] = d_attended[:, at : at + sub, lanes]
    for k in range(len(pieces) // 2):
        for c in range(2):
            pieces[2 * k + c][...] = stage[place_ref[5] ^ k, place_ref[4] ^ c]


def exchange(value):
    return lax.all_to_all(value, "sq", split_axis=0, concat_axis=0, tiled=True)


def local(
    inputs,
    w_query,
    w_key,
    w_value,
    w_out,
    table,
    gain_one,
    gain_two,
    w_router,
    w_up,
    w_down,
    routes,
    segments,
    cotangent,
):
    seqs, rows, width = inputs.shape
    heads = table.shape[1]
    head_dim = width // heads
    reps = lax.axis_size("rep")
    groups = lax.axis_size("sq")
    length = rows * groups
    tokens = seqs * rows
    share = groups // EXPERTS
    half = rows // 2
    all_seqs = 2 * seqs
    split = groups // (all_seqs * HEAD_GROUPS)
    sub = half // split
    group_heads = heads // HEAD_GROUPS
    head_width = group_heads * head_dim
    shard = w_query.shape[0]
    part = shard // 2
    bucket_rows = table.shape[0]
    core = lax.axis_index("rep") % 2
    me = lax.axis_index("sq")
    group_at = (me // split) % HEAD_GROUPS
    first = core == 0
    pairs = [(i, i ^ 1) for i in range(reps)]

    def swap(value):
        return lax.ppermute(value, "rep", pairs)

    chips = HEAD_GROUPS * split

    def plane(value, k, c):
        if k == 0 and c == 0:
            return value
        moves = [
            (r * groups + q, (r ^ c) * groups + (q ^ k)) for r in range(reps) for q in range(groups)
        ]
        return lax.ppermute(value, ("rep", "sq"), moves)

    def plane_all(pieces):
        return [plane(pieces[2 * k + c], k, c) for k in range(chips) for c in range(2)]

    def to_tokens(value, turn, back):
        moves = []
        for r in range(reps):
            for p in range(groups):
                w = p // chips
                s = seqs * (r % 2) + (w + turn) % 2
                there = (r // 2 * 2 + w // 2) * groups + s * chips + p % chips
                here = r * groups + p
                moves.append((there, here) if back else (here, there))
        return lax.ppermute(value, ("rep", "sq"), moves)

    def by_core(own, other, axis):
        return jnp.where(
            first,
            jnp.concatenate([own, other], axis=axis),
            jnp.concatenate([other, own], axis=axis),
        )

    def mine(value, axis, size):
        return lax.dynamic_slice_in_dim(value, core * size, size, axis)

    def yours(value, axis, size):
        return lax.dynamic_slice_in_dim(value, (1 - core) * size, size, axis)

    def over_pairs(value):
        if reps == 2:
            return value
        sets = [list(range(0, reps, 2)), list(range(1, reps, 2))]
        return lax.psum(value, "rep", axis_index_groups=sets)

    smem = pl.BlockSpec(memory_space=pltpu.SMEM)
    vmem = pl.BlockSpec(memory_space=pltpu.VMEM)

    def cost(microseconds):
        return pl.CostEstimate(
            flops=microseconds * 900_000_000,
            bytes_accessed=microseconds * 1_000_000,
            transcendentals=0,
        )

    limit = pltpu.CompilerParams(vmem_limit_bytes=56 * 1024 * 1024)
    spare = width - 3 * head_width
    query_at = core * half + (me % split) * sub
    inner = me % chips
    first_block = 2 * core * chips + inner
    parity = (me // chips) % 2
    place = jnp.stack(
        [
            core * half,
            query_at,
            group_at * group_heads,
            core * seqs,
            core,
            inner,
            first_block,
            parity,
        ]
    )
    place = place.astype(jnp.int32)
    shard_table = bucket_rows * heads
    marks = jnp.concatenate([segments, routes.reshape(seqs, rows)], axis=1)
    send = pl.pallas_call(
        partial(pack_kernel, split=split),
        name="pack",
        out_shape=jax.ShapeDtypeStruct((groups, part, width), bf16),
        in_specs=[smem] + [vmem] * 9,
        out_specs=vmem,
        scratch_shapes=[
            pltpu.VMEM((HEAD_GROUPS, part, 3 * head_width), f32),
            pltpu.VMEM((part, spare), f32),
        ],
        compiler_params=limit,
        cost_estimate=cost(3),
    )(
        place,
        marks,
        swap(marks),
        w_query,
        w_key,
        w_value,
        gain_one.reshape(1, shard),
        gain_two.reshape(1, shard),
        w_router.T,
        table,
    )
    def half_at(value, turn):
        return lax.dynamic_index_in_dim(value, (parity + turn) % 2, 0, keepdims=False)

    x_first, x_second = [to_tokens(half_at(inputs, turn), turn, False) for turn in range(2)]
    send, x_first, x_second = lax.optimization_barrier((send, x_first, x_second))
    x_tokens = jnp.where(
        parity == 0, jnp.stack([x_first, x_second]), jnp.stack([x_second, x_first])
    )
    x_parts = [x_tokens] + [plane(x_tokens, k, 0) for k in range(1, chips)]
    own = exchange(send)
    out_half = mine(w_out, 1, width // 2)
    out_send = jnp.broadcast_to(out_half[None], (groups, shard, width // 2))
    first, second = [to_tokens(half_at(cotangent, turn), turn, False) for turn in range(2)]
    own, out_send, place, x_parts, first, second = lax.optimization_barrier(
        (own, out_send, place, x_parts, first, second)
    )
    x_parts = x_parts + [swap(v) for v in x_parts]
    other, out_send = lax.optimization_barrier((swap(own), out_send))
    out_mine = exchange(out_send)
    queries_count = groups * sub
    tile = (LANES // rows) * sub
    sizes = dict(groups=groups, half=half, rows=rows, sub=sub, head_dim=head_dim)
    piece = jax.ShapeDtypeStruct((2, sub, head_width), bf16)
    (
        probs,
        queries,
        pair,
        normed_all,
        w_group,
        gain_one_full,
        gain_two_full,
        router_full,
        routes_all,
        *attended_parts,
    ) = pl.pallas_call(
        partial(forward_kernel, shard=shard, all_heads=heads, **sizes),
        name="attention_forward",
        out_shape=(
            jax.ShapeDtypeStruct((group_heads, queries_count, length), bf16),
            jax.ShapeDtypeStruct((queries_count, head_width), bf16),
            jax.ShapeDtypeStruct((length, 2 * head_width), bf16),
            jax.ShapeDtypeStruct((groups, rows, width), bf16),
            jax.ShapeDtypeStruct((width, 3 * head_width), bf16),
            jax.ShapeDtypeStruct((1, width), f32),
            jax.ShapeDtypeStruct((1, width), f32),
            jax.ShapeDtypeStruct((EXPERTS, width), f32),
            jax.ShapeDtypeStruct((groups, rows), f32),
        )
        + (piece,) * (2 * chips),
        in_specs=[smem] + [vmem] * (2 + 2 * chips),
        out_specs=[vmem] * (9 + 2 * chips),
        scratch_shapes=[
            pltpu.VMEM((groups, shard, 3 * head_width), f32),
            pltpu.VMEM((groups, rows, 3 * head_width), bf16),
            pltpu.VMEM((queries_count, length), f32),
            pltpu.VMEM((tile, 2 * length - LANES), f32),
            pltpu.VMEM((1, length), f32),
            pltpu.VMEM((queries_count, 1), f32),
            pltpu.VMEM((32, heads), f32),
            pltpu.VMEM((queries_count, head_width), bf16),
        ],
        compiler_params=limit,
        cost_estimate=cost(60),
    )(place, own, other, *x_parts)
    attended_parts, out_mine = lax.optimization_barrier((attended_parts, out_mine))
    back = plane_all(attended_parts)
    out_mine = out_mine.reshape(width, width // 2)
    out_yours = swap(out_mine)
    few = CAP
    pieces = dict(half=half, sub=sub, split=split, few=few)
    (
        buffer,
        attended,
        hidden,
        normed_two,
        router_probs,
        spread,
        cotangent_tokens,
        routes_tokens,
    ) = pl.pallas_call(
        partial(middle_kernel, share=share, **pieces),
        name="router_and_dispatch",
        out_shape=(
            jax.ShapeDtypeStruct((groups, 2 * few, width), bf16),
            jax.ShapeDtypeStruct((tokens, width), bf16),
            jax.ShapeDtypeStruct((tokens, width), f32),
            jax.ShapeDtypeStruct((tokens, width), bf16),
            jax.ShapeDtypeStruct((tokens, EXPERTS), f32),
            jax.ShapeDtypeStruct((tokens, EXPERTS * CAP), bf16),
            jax.ShapeDtypeStruct((seqs, rows, width), bf16),
            jax.ShapeDtypeStruct((tokens, 1), jnp.int32),
        ),
        in_specs=[smem] + [vmem] * (8 + 2 * chips),
        out_specs=[vmem] * 8,
        scratch_shapes=[
            pltpu.VMEM((seqs, rows, width), bf16),
            pltpu.VMEM((chips, 2, seqs, sub, head_width), bf16),
            pltpu.VMEM((rows, groups), f32),
        ],
        compiler_params=limit,
        cost_estimate=cost(5),
    )(
        place,
        x_tokens,
        out_mine,
        out_yours,
        gain_two_full,
        router_full,
        routes_all,
        first,
        second,
        *back,
    )
    arrived = exchange(buffer)
    expert_rows = groups * few
    units_low = jax.ShapeDtypeStruct((expert_rows, w_up.shape[1]), bf16)
    results, act, d_pre = pl.pallas_call(
        partial(expert_kernel, few=few),
        name="experts",
        out_shape=(
            jax.ShapeDtypeStruct((groups, 2 * few, width), bf16),
            units_low,
            units_low,
        ),
        in_specs=[vmem] * 3,
        out_specs=[vmem] * 3,
        compiler_params=limit,
        cost_estimate=cost(8),
    )(arrived, w_up, w_down)
    returned = exchange(results)
    received = arrived[:, :few].reshape(expert_rows, width)
    got = arrived[:, few:].reshape(expert_rows, width)
    up_local = dot(received, d_pre, ((0,), (0,))).astype(bf16)
    down_local = dot(act, got, ((0,), (0,))).astype(bf16)

    def both_reps(value):
        if reps == 2:
            return value.astype(f32) + swap(value).astype(f32)
        return lax.psum(value, "rep").astype(f32)

    returned, up_local, down_local = lax.optimization_barrier((returned, up_local, down_local))
    *d_parts, out_first, out_second, d_hidden, d_branch, router_grad, gain_two_grad = pl.pallas_call(
        partial(turn_kernel, share=share, **pieces),
        name="combine_and_turn",
        out_shape=[piece] * (2 * chips)
        + [
            jax.ShapeDtypeStruct((rows, width), bf16),
            jax.ShapeDtypeStruct((rows, width), bf16),
            jax.ShapeDtypeStruct((tokens, width), f32),
            jax.ShapeDtypeStruct((tokens, width), bf16),
            jax.ShapeDtypeStruct((EXPERTS, width), f32),
            jax.ShapeDtypeStruct((1, width), f32),
        ],
        in_specs=[smem] + [vmem] * 11,
        out_specs=[vmem] * (6 + 2 * chips),
        scratch_shapes=[
            pltpu.VMEM((seqs, rows, width), bf16),
            pltpu.VMEM((seqs, rows, width), bf16),
            pltpu.VMEM((chips, 2, seqs, sub, head_width), bf16),
        ],
        compiler_params=limit,
        cost_estimate=cost(5),
    )(
        place,
        returned,
        spread,
        hidden,
        normed_two,
        router_probs,
        routes_tokens,
        cotangent_tokens,
        gain_two_full,
        router_full,
        out_mine,
        out_yours,
    )
    grads = plane_all(d_parts)
    out_send = pl.pallas_call(
        partial(out_grad_kernel, groups=groups, shard=shard),
        name="out_grad",
        out_shape=jax.ShapeDtypeStruct((groups, part, width), bf16),
        in_specs=[smem] + [vmem] * 4,
        out_specs=vmem,
        scratch_shapes=[pltpu.VMEM((groups, shard, width), f32)],
        compiler_params=limit,
        cost_estimate=cost(3),
    )(place, attended, swap(attended), d_branch, swap(d_branch))
    grads, out_send = lax.optimization_barrier((grads, out_send))
    out_back = exchange(out_send)
    d_all, table_part = pl.pallas_call(
        partial(backward_kernel, **sizes),
        name="attention_backward",
        out_shape=(
            jax.ShapeDtypeStruct((groups, rows, 3 * head_width), bf16),
            jax.ShapeDtypeStruct((group_heads, groups * bucket_rows, LANES), f32),
        ),
        in_specs=[smem] + [vmem] * (3 + 2 * chips),
        out_specs=[vmem] * 2,
        scratch_shapes=[
            pltpu.VMEM((queries_count, length), f32),
            pltpu.VMEM((queries_count, length), bf16),
            pltpu.VMEM((tile, 2 * length - LANES), f32),
            pltpu.VMEM((2 * head_width, length), f32),
            pltpu.VMEM((queries_count, head_width), f32),
            pltpu.VMEM((queries_count, head_width), bf16),
        ],
        compiler_params=limit,
        cost_estimate=cost(1),
    )(place, probs, queries, pair, *grads)
    d_all, out_back = lax.optimization_barrier((d_all, out_back))
    d_all_other = swap(d_all)
    out_first = to_tokens(out_first, 0, True)
    out_second = to_tokens(out_second, 1, True)
    out_sum = jnp.sum(out_back.astype(f32), axis=0)
    out_sum = over_pairs(out_sum)
    out_other = swap(out_sum)
    d_normed_parts, d_sum, gain_one_part = pl.pallas_call(
        partial(rows_kernel, half=half),
        name="d_normed",
        out_shape=[
            jax.ShapeDtypeStruct((chips, groups // chips, half, width), bf16),
            jax.ShapeDtypeStruct((groups, rows, 3 * head_width), bf16),
            jax.ShapeDtypeStruct((1, width), f32),
        ],
        in_specs=[smem] + [vmem] * 5,
        out_specs=[vmem] * 3,
        compiler_params=limit,
        cost_estimate=cost(1),
    )(place, d_all, d_all_other, w_group, normed_all, gain_one_full)
    last = pl.pallas_call(
        partial(weight_kernel, shard=shard, all_heads=heads),
        name="weight_grads",
        out_shape=jax.ShapeDtypeStruct((groups, part, width), bf16),
        in_specs=[smem] + [vmem] * 6,
        out_specs=vmem,
        scratch_shapes=[
            pltpu.VMEM((groups, shard, 3 * head_width), f32),
            pltpu.VMEM((groups, part, spare), f32),
        ],
        compiler_params=limit,
        cost_estimate=cost(8),
    )(place, d_sum, normed_all, gain_one_part, gain_two_grad, router_grad, table_part)
    planes = [list(range(q, q + chips)) for q in range(0, groups, chips)]
    d_normed_parts = lax.all_to_all(
        d_normed_parts, "sq", 0, 0, axis_index_groups=planes, tiled=True
    )
    last, d_normed_parts, out_first, out_second = lax.optimization_barrier(
        (last, d_normed_parts, out_first, out_second)
    )
    final = exchange(last)
    d_keep, d_give = pl.pallas_call(
        total_kernel,
        name="d_normed_total",
        out_shape=[
            jax.ShapeDtypeStruct((seqs, half, width), f32),
            jax.ShapeDtypeStruct((seqs, half, width), bf16),
        ],
        in_specs=[smem, vmem],
        out_specs=[vmem] * 2,
        compiler_params=limit,
        cost_estimate=cost(1),
    )(place, d_normed_parts)
    grad_first, grad_second = pl.pallas_call(
        partial(token_kernel, half=half),
        name="token_grad",
        out_shape=[jax.ShapeDtypeStruct((rows, width), bf16)] * 2,
        in_specs=[smem] + [vmem] * 5,
        out_specs=[vmem] * 2,
        scratch_shapes=[pltpu.VMEM((seqs, rows, width), f32)] * 2,
        compiler_params=limit,
        cost_estimate=cost(2),
    )(place, x_tokens, d_hidden, gain_one_full, d_keep, swap(d_give))
    grad_first = to_tokens(grad_first, 0, True)
    grad_second = to_tokens(grad_second, 1, True)
    up_grad = both_reps(up_local)
    down_grad = both_reps(down_local)
    final, grad_first, grad_second, up_grad, down_grad = lax.optimization_barrier(
        (final, grad_first, grad_second, up_grad, down_grad)
    )
    four, four_low, small_sum = pl.pallas_call(
        partial(sum_kernel, seqs=seqs),
        name="sums",
        out_shape=(
            jax.ShapeDtypeStruct((3, part, width), f32),
            jax.ShapeDtypeStruct((3, part, width), bf16),
            jax.ShapeDtypeStruct((part, spare), f32),
        ),
        in_specs=[vmem],
        out_specs=[vmem] * 3,
        compiler_params=limit,
        cost_estimate=cost(2),
    )(final)
    if reps > 2:
        four, small_sum = over_pairs(four), over_pairs(small_sum)
        four_low = four.astype(bf16)
    (
        output,
        input_grad,
        query_grad,
        key_grad,
        value_grad,
        out_grad,
        table_grad,
        gain_one_grad,
        gain_two_grad,
        router_grad,
    ) = pl.pallas_call(
        input_kernel,
        name="input_grad",
        out_shape=(
            jax.ShapeDtypeStruct((seqs, rows, width), bf16),
            jax.ShapeDtypeStruct((seqs, rows, width), f32),
        )
        + (jax.ShapeDtypeStruct((shard, width), f32),) * 4
        + (
            jax.ShapeDtypeStruct((bucket_rows, heads), f32),
            jax.ShapeDtypeStruct((1, shard), f32),
            jax.ShapeDtypeStruct((1, shard), f32),
            jax.ShapeDtypeStruct((EXPERTS, shard), f32),
        ),
        in_specs=[smem] + [vmem] * 10,
        out_specs=[vmem] * 10,
        compiler_params=limit,
        cost_estimate=cost(2),
    )(
        place,
        grad_first,
        grad_second,
        out_first,
        out_second,
        four,
        swap(four_low),
        out_sum,
        out_other,
        small_sum,
        swap(small_sum),
    )
    return (
        output,
        input_grad,
        query_grad,
        key_grad,
        value_grad,
        out_grad,
        table_grad,
        gain_one_grad.reshape(shard),
        gain_two_grad.reshape(shard),
        router_grad.T,
        up_grad,
        down_grad,
    )


def solution(mesh):
    in_specs = (
        P("rep", "sq", None),
        P("sq", None),
        P("sq", None),
        P("sq", None),
        P("sq", None),
        P("sq", None),
        P("sq"),
        P("sq"),
        P("sq", None),
        P(None, "sq"),
        P("sq", None),
        P("rep", "sq", None),
        P("rep", "sq"),
        P("rep", "sq", None),
    )
    out_specs = (
        P("rep", "sq", None),
        P("rep", "sq", None),
        P("sq", None),
        P("sq", None),
        P("sq", None),
        P("sq", None),
        P("sq", None),
        P("sq"),
        P("sq"),
        P("sq", None),
        P(None, "sq"),
        P("sq", None),
    )
    return jax.shard_map(local, mesh=mesh, in_specs=in_specs, out_specs=out_specs, check_vma=False)
```

```python
from functools import partial

import jax
import jax.numpy as jnp
from jax import lax
from jax.experimental import pallas as pl
from jax.experimental.pallas import tpu as pltpu
from jax.sharding import PartitionSpec as P

EXPERTS = 8
CAP = 32
HEAD_GROUPS = 4
EPS = 1e-06
NEGATIVE = -1e30
LIMITS = (1, 2, 3, 4, 5, 6, 7, 8, 12, 16, 23, 32, 46, 64, 91)
LANES = 128
f32 = jnp.float32
bf16 = jnp.bfloat16


def dot(a, b, dims=((1,), (0,))):
    return lax.dot_general(a, b, (dims, ((), ())), preferred_element_type=f32)


def relative_tile(offset, shape, rows, sub):
    row = lax.broadcasted_iota(jnp.int32, shape, 0)
    col = lax.broadcasted_iota(jnp.int32, shape, 1)
    return col - LANES - (rows * (row // sub) + offset + row % sub)


def pack_kernel(
    place_ref,
    marks_ref,
    marks_other_ref,
    query_ref,
    key_ref,
    value_ref,
    gain_one_ref,
    gain_two_ref,
    router_ref,
    table_ref,
    send_ref,
    weights,
    small,
    *,
    split,
):
    seqs = marks_ref.shape[0]
    rows = marks_ref.shape[1] // 2
    shard, width = query_ref.shape
    part = shard // 2
    head_width = width // HEAD_GROUPS
    base = 3 * head_width
    per_seq = HEAD_GROUPS * split
    heads = table_ref.shape[1]
    for c in range(2):

        @pl.when(place_ref[4] == c)
        def _():
            at = slice(c * part, (c + 1) * part)
            for i, ref in enumerate((query_ref, key_ref, value_ref)):
                for g in range(HEAD_GROUPS):
                    weights[g, :, i * head_width : (i + 1) * head_width] = ref[
                        at, g * head_width : (g + 1) * head_width
                    ].astype(f32)

    small[...] = jnp.zeros_like(small)
    small[0:1, 0:shard] = gain_one_ref[...].astype(f32)
    small[1:2, 0:shard] = gain_two_ref[...].astype(f32)
    small[2 : 2 + EXPERTS, 0:shard] = router_ref[...].astype(f32)
    for k in range(table_ref.shape[0]):
        small[2 + EXPERTS : 3 + EXPERTS, k * heads : (k + 1) * heads] = table_ref[
            k : k + 1, :
        ].astype(f32)
    for c in range(2):
        marks = marks_ref if c == 0 else marks_other_ref
        first = (place_ref[3] if c == 0 else seqs - place_ref[3]) * per_seq
        for l in range(seqs):
            small[3 + EXPERTS : 4 + EXPERTS, 0 : 2 * rows] = marks[l : l + 1, :].astype(f32)
            for k in range(per_seq):
                at = first + l * per_seq + k
                send_ref[at, :, 0:base] = weights[k // split].astype(bf16)
                send_ref[at, :, base:] = small[...].astype(bf16)


def forward_kernel(
    place_ref,
    own_ref,
    other_ref,
    *refs,
    groups,
    half,
    rows,
    sub,
    head_dim,
    shard,
    all_heads,
):
    chips = (len(refs) - 17) // 4
    x_refs = refs[: 2 * chips]
    (
        probs_ref,
        query_ref,
        pair_ref,
        normed_all,
        weight_ref,
        gain_one_ref,
        gain_two_ref,
        router_ref,
        routes_ref,
    ) = refs[2 * chips : 2 * chips + 9]
    pieces = refs[2 * chips + 9 : -8]
    weights, project, scores, strip, seg_key_ref, seg_query_ref, table_ref, attended_ref = refs[-8:]
    query_at = pl.multiple_of(place_ref[1], sub)
    width = gain_one_ref.shape[1]
    length = groups * rows
    heads = attended_ref.shape[1] // head_dim
    head_width = heads * head_dim
    per = LANES // rows
    tile = per * sub
    steps = length // LANES
    base = 3 * head_width
    table_rows = 32 // groups
    seg_row = lax.broadcasted_iota(jnp.int32, (sub, rows), 0)
    seg_col = lax.broadcasted_iota(jnp.int32, (sub, rows), 1)
    seg_pick = seg_col == seg_row + place_ref[1]
    for p in range(groups):
        at = slice(p * shard, (p + 1) * shard)
        small = own_ref[p, :, base:].astype(f32)
        gain_one_ref[:, at] = small[0:1, 0:shard]
        gain_two_ref[:, at] = small[1:2, 0:shard]
        router_ref[:, at] = small[2 : 2 + EXPERTS, 0:shard]
        for k in range(table_rows):
            table_ref[p * table_rows + k : p * table_rows + k + 1, :] = small[
                2 + EXPERTS : 3 + EXPERTS, k * all_heads : (k + 1) * all_heads
            ]
        seg = small[3 + EXPERTS : 4 + EXPERTS, 0:rows]
        routes_ref[p : p + 1, :] = small[3 + EXPERTS : 4 + EXPERTS, rows : 2 * rows]
        seg_key_ref[:, p * rows : (p + 1) * rows] = seg
        seg_query_ref[p * sub : (p + 1) * sub, :] = jnp.sum(
            jnp.where(seg_pick, jnp.broadcast_to(seg, (sub, rows)), 0.0), axis=1, keepdims=True
        )
    part = shard // 2
    for c in range(2):

        @pl.when(place_ref[4] == c)
        def _():
            at = slice(c * part, (c + 1) * part)
            weights[:, at, :] = own_ref[:, :, 0:base].astype(f32)
            at = slice((1 - c) * part, (2 - c) * part)
            weights[:, at, :] = other_ref[:, :, 0:base].astype(f32)

    weight_ref[...] = weights[...].reshape(width, base).astype(bf16)
    gain = gain_one_ref[...]
    head_col = lax.broadcasted_iota(jnp.int32, (32, all_heads), 1)

    def norm(x):
        x = x.astype(f32)
        scale = lax.rsqrt(jnp.mean(x * x, axis=-1, keepdims=True) + EPS)
        return ((x * scale) * gain).astype(bf16)

    for k in range(chips):
        for c in range(2):
            at = 2 * (place_ref[4] ^ c) * chips + (place_ref[5] ^ k)
            for b in range(2):
                normed_all[at + b * chips] = norm(x_refs[c * chips + k][b])
    chunk = 4

    def project_step(c, carry):
        block = normed_all[pl.ds(c * chunk, chunk)].reshape(chunk * rows, width)
        result = dot(block, weight_ref[...]).astype(bf16)
        project[pl.ds(c * chunk, chunk)] = result.reshape(chunk, rows, 3 * head_width)
        pair_ref[pl.ds(c * chunk * rows, chunk * rows), :] = result[:, head_width:]
        return carry

    lax.fori_loop(0, groups // chunk, project_step, 0)

    def query_step(p, carry):
        query_ref[pl.ds(p * sub, sub), :] = project[p, pl.ds(query_at, sub), 0:head_width]
        return carry

    lax.fori_loop(0, groups, query_step, 0)
    factor = head_dim ** (-0.5)
    left = length - 2 * LANES
    right = length + LANES
    relative = relative_tile(place_ref[1], (tile, 3 * LANES), rows, sub)
    magnitude = jnp.abs(relative)
    for h in range(heads):
        at = h * head_dim
        mine = head_col == place_ref[2] + h
        column = jnp.sum(jnp.where(mine, table_ref[...], 0.0), axis=1, keepdims=True)
        entry = [column[b : b + 1, :] for b in range(32)]
        bias = jnp.where(relative > 0, entry[16], entry[0])
        for k, threshold in enumerate(LIMITS):
            value = jnp.where(relative > 0, entry[17 + k], entry[1 + k])
            bias = jnp.where(magnitude >= threshold, value, bias)
        strip[:, 0:left] = jnp.broadcast_to(entry[15], (tile, left))
        strip[:, left:right] = bias
        strip[:, right:] = jnp.broadcast_to(entry[31], (tile, strip.shape[1] - right))
        scores[...] = (
            dot(query_ref[:, at : at + head_dim], pair_ref[:, at : at + head_dim], ((1,), (1,)))
            * factor
        )

        def soft_step(qb, carry):
            start = pl.multiple_of(length - LANES - qb * LANES, LANES)
            for par in range(per):
                here = pl.ds(qb * tile + par * sub, sub)
                value = scores[here, :] + strip[par * sub : (par + 1) * sub, pl.ds(start, length)]
                same = seg_query_ref[here, :] == seg_key_ref[...]
                value = jnp.where(same, value, NEGATIVE)
                top = jnp.max(value, axis=-1, keepdims=True)
                value = jnp.exp(value - top)
                total = jnp.sum(value, axis=-1, keepdims=True)
                probs_ref[h, here, :] = (value * (1.0 / total)).astype(bf16)
            return carry

        lax.fori_loop(0, steps, soft_step, 0, unroll=2)
        attended_ref[:, at : at + head_dim] = dot(
            probs_ref[h], pair_ref[:, head_width + at : head_width + at + head_dim]
        ).astype(bf16)
    for k in range(len(pieces) // 2):
        for c in range(2):
            at = 2 * (place_ref[4] ^ c) * (len(pieces) // 2) + (place_ref[5] ^ k)
            for b in range(2):
                block = at + b * (len(pieces) // 2)
                rows_at = pl.ds(pl.multiple_of(block * sub, sub), sub)
                pieces[2 * k + c][b] = attended_ref[rows_at, :]


def backward_kernel(
    place_ref,
    probs_ref,
    query_ref,
    pair_ref,
    *refs,
    groups,
    half,
    rows,
    sub,
    head_dim,
):
    pieces = refs[:-8]
    d_all_ref, table_ref, scores, low, strip, flipped, d_query, grad_ref = refs[-8:]
    for k in range(len(pieces) // 2):
        for c in range(2):
            at = 2 * (place_ref[4] ^ c) * (len(pieces) // 2) + (place_ref[5] ^ k)
            for b in range(2):
                block = at + b * (len(pieces) // 2)
                rows_at = pl.ds(pl.multiple_of(block * sub, sub), sub)
                grad_ref[rows_at, :] = pieces[2 * k + c][b]
    query_at = pl.multiple_of(place_ref[1], sub)
    length = groups * rows
    head_width = query_ref.shape[1]
    heads = head_width // head_dim
    per = LANES // rows
    tile = per * sub
    steps = length // LANES
    factor = head_dim ** (-0.5)
    left = length - 2 * LANES
    right = length + LANES
    relative = relative_tile(place_ref[1], (tile, 3 * LANES), rows, sub)
    magnitude = jnp.abs(relative)
    count = jnp.zeros_like(relative)
    for threshold in LIMITS:
        count = count + (magnitude >= threshold).astype(jnp.int32)
    bucket = count + jnp.where(relative > 0, 16, 0)

    def lanes_sum(value):
        value = jnp.sum(value, axis=0, keepdims=True)
        total = value[:, 0:LANES]
        for k in range(1, value.shape[1] // LANES):
            total = total + value[:, k * LANES : (k + 1) * LANES]
        return total

    for h in range(heads):
        at = h * head_dim
        grad = grad_ref[:, at : at + head_dim]
        scores[...] = dot(
            grad, pair_ref[:, head_width + at : head_width + at + head_dim], ((1,), (1,))
        )
        strip[...] = jnp.zeros_like(strip)

        def score_step(qb, carry):
            start = pl.multiple_of(length - LANES - qb * LANES, LANES)
            for par in range(per):
                here = pl.ds(qb * tile + par * sub, sub)
                probs = probs_ref[h, here, :].astype(f32)
                value = scores[here, :]
                delta = jnp.sum(probs * value, axis=-1, keepdims=True)
                value = probs * (value - delta)
                low[here, :] = value.astype(bf16)
                strip[par * sub : (par + 1) * sub, pl.ds(start, length)] += value
            return carry

        lax.fori_loop(0, steps, score_step, 0, unroll=2)
        d_query[:, at : at + head_dim] = dot(low[...], pair_ref[:, at : at + head_dim]) * factor
        flipped[at : at + head_dim, :] = (
            dot(query_ref[:, at : at + head_dim], low[...], ((0,), (0,))) * factor
        )
        flipped[head_width + at : head_width + at + head_dim, :] = dot(
            grad, probs_ref[h], ((0,), (0,))
        )
        near = strip[:, left:right]
        for b in range(32):
            table_ref[h, b : b + 1, :] = lanes_sum(jnp.where(bucket == b, near, 0.0))
        table_ref[h, 15:16, :] += lanes_sum(strip[:, 0:left])
        table_ref[h, 31:32, :] += lanes_sum(strip[:, right:])
    d_all_ref[:, :, 0:head_width] = jnp.zeros((groups, rows, head_width), bf16)
    for c in range(length // LANES):
        block = flipped[:, c * LANES : (c + 1) * LANES].T.astype(bf16)
        d_all_ref[c * per : (c + 1) * per, :, head_width:] = block.reshape(
            per, rows, 2 * head_width
        )

    def place_step(p, carry):
        d_all_ref[p, pl.ds(query_at, sub), 0:head_width] = d_query[
            pl.ds(p * sub, sub), :
        ].astype(bf16)
        return carry

    lax.fori_loop(0, groups, place_step, 0)


def rows_kernel(
    place_ref,
    d_own_ref,
    d_other_ref,
    weight_ref,
    normed_ref,
    gain_ref,
    rows_ref,
    d_sum,
    gain_sum,
    *,
    half,
):
    core_at = pl.multiple_of(place_ref[0], half)
    groups, _, base = d_own_ref.shape
    chips = rows_ref.shape[0]
    width = weight_ref.shape[0]
    d_sum[...] = (d_own_ref[...].astype(f32) + d_other_ref[...].astype(f32)).astype(bf16)
    gain_sum[...] = jnp.zeros_like(gain_sum)
    chunk = 4

    def normed_step(c, carry):
        at = pl.ds(c * chunk, chunk)
        block = d_sum[at, pl.ds(core_at, half), :].reshape(chunk * half, base)
        d_normed = dot(block, weight_ref[...], ((1,), (1,)))
        normed = normed_ref[at, pl.ds(core_at, half), :].astype(f32).reshape(chunk * half, width)
        gain_sum[...] += jnp.sum(d_normed * normed, axis=0, keepdims=True)
        d_rows = d_normed.reshape(chunk, half, width).astype(bf16)
        for k in range(chunk):
            p = c * chunk + k
            rows_ref[lax.rem(p, chips), lax.div(p, chips)] = d_rows[k]
        return carry

    lax.fori_loop(0, groups // chunk, normed_step, 0)
    gain_sum[...] = gain_sum[...] / gain_ref[...]


def weight_kernel(
    place_ref,
    d_sum,
    normed_ref,
    gain_sum,
    gain_two_ref,
    router_ref,
    table_ref,
    last_ref,
    w_grad,
    small,
    *,
    shard,
    all_heads,
):
    groups, rows, width = normed_ref.shape
    base = d_sum.shape[2]
    part = shard // 2
    length = groups * rows
    w_grad[...] = dot(
        normed_ref[...].reshape(length, width), d_sum[...].reshape(length, base), ((0,), (0,))
    ).reshape(groups, shard, base)
    for c in range(2):

        @pl.when(place_ref[4] == c)
        def _():
            last_ref[:, :, 0:base] = w_grad[:, c * part : (c + 1) * part, :].astype(bf16)

    heads = table_ref.shape[0]
    head_col = lax.broadcasted_iota(jnp.int32, (32, all_heads), 1)
    table = jnp.zeros((32, all_heads), f32)
    for h in range(heads):
        column = jnp.sum(table_ref[h], axis=1, keepdims=True)
        table = table + jnp.where(head_col == place_ref[2] + h, column, 0.0)
    table_rows = 32 // groups
    small[...] = jnp.zeros_like(small)
    for p in range(groups):
        at = slice(p * shard, (p + 1) * shard)
        small[p, 0:1, 0:shard] = gain_sum[:, at]
        small[p, 1:2, 0:shard] = gain_two_ref[:, at]
        small[p, 2 : 2 + EXPERTS, 0:shard] = router_ref[:, at]
        for k in range(table_rows):
            small[p, 2 + EXPERTS : 3 + EXPERTS, k * all_heads : (k + 1) * all_heads] = table[
                p * table_rows + k : p * table_rows + k + 1, :
            ]
    last_ref[:, :, base:] = small[...].astype(bf16)


def out_grad_kernel(
    place_ref, attended_ref, other_ref, d_ref, d_other_ref, out_ref, total, *, groups, shard
):
    part = shard // 2
    width = total.shape[2]
    grad = dot(attended_ref[...], d_ref[...], ((0,), (0,)))
    grad = grad + dot(other_ref[...], d_other_ref[...], ((0,), (0,)))
    total[...] = grad.reshape(groups, shard, width)
    for c in range(2):

        @pl.when(place_ref[4] == c)
        def _():
            out_ref[...] = total[:, c * part : (c + 1) * part, :].astype(bf16)


def sum_kernel(final_ref, four_ref, low_ref, small_ref, *, seqs):
    groups, part, width = final_ref.shape
    base = width - small_ref.shape[1]
    head_width = base // 3
    split = groups // (2 * seqs * HEAD_GROUPS)
    for g in range(HEAD_GROUPS):
        grad = jnp.zeros((part, base), f32)
        for s in range(2 * seqs):
            for t in range(split):
                at = (s * HEAD_GROUPS + g) * split + t
                grad = grad + final_ref[at, :, 0:base].astype(f32)
        for i in range(3):
            four_ref[i, :, g * head_width : (g + 1) * head_width] = grad[
                :, i * head_width : (i + 1) * head_width
            ]
    low_ref[...] = four_ref[...].astype(bf16)
    small = final_ref[0, :, base:].astype(f32)
    for p in range(1, groups):
        small = small + final_ref[p, :, base:].astype(f32)
    small_ref[...] = small


def total_kernel(place_ref, rows_ref, keep_ref, give_ref):
    blocks = keep_ref.shape[0]
    for b in range(blocks):

        def total(w):
            value = rows_ref[0, w].astype(f32)
            for j in range(1, rows_ref.shape[0]):
                value = value + rows_ref[j, w].astype(f32)
            return value

        keep_ref[b] = total(place_ref[4] * blocks + b)
        give_ref[b] = total((1 - place_ref[4]) * blocks + b).astype(bf16)


def token_kernel(
    place_ref,
    x_ref,
    d_hidden_ref,
    gain_ref,
    keep_ref,
    given_ref,
    first_ref,
    second_ref,
    d_normed_ref,
    grad_ref,
    *,
    half,
):
    blocks, rows, width = x_ref.shape
    core_at = pl.multiple_of(place_ref[0], half)
    other_at = pl.multiple_of(half - place_ref[0], half)
    d_normed_ref[:, pl.ds(core_at, half), :] = keep_ref[...]
    d_normed_ref[:, pl.ds(other_at, half), :] = given_ref[...].astype(f32)
    d_normed = d_normed_ref[...].reshape(blocks * rows, width)
    x = x_ref[...].reshape(blocks * rows, width).astype(f32)
    scale = lax.rsqrt(jnp.mean(x * x, axis=-1, keepdims=True) + EPS)
    unit = x * scale
    d_unit = d_normed * gain_ref[...]
    grad = scale * (d_unit - unit * jnp.mean(d_unit * unit, axis=-1, keepdims=True))
    grad_ref[...] = (d_hidden_ref[...] + grad).reshape(blocks, rows, width)
    first_ref[...] = grad_ref[place_ref[7]].astype(bf16)
    second_ref[...] = grad_ref[1 - place_ref[7]].astype(bf16)


def input_kernel(
    place_ref,
    grad_first_ref,
    grad_second_ref,
    out_first_ref,
    out_second_ref,
    four_ref,
    other_ref,
    out_mine_ref,
    out_other_ref,
    small_ref,
    small_other_ref,
    output_ref,
    input_ref,
    query_ref,
    key_ref,
    value_ref,
    out_ref,
    table_ref,
    gain_one_ref,
    gain_two_ref,
    router_ref,
):
    output_ref[place_ref[7]] = out_first_ref[...]
    output_ref[1 - place_ref[7]] = out_second_ref[...]
    input_ref[place_ref[7]] = grad_first_ref[...].astype(f32)
    input_ref[1 - place_ref[7]] = grad_second_ref[...].astype(f32)
    small = small_ref[...] + small_other_ref[...]
    shard = gain_one_ref.shape[1]
    heads = table_ref.shape[1]
    gain_one_ref[...] = small[0:1, 0:shard]
    gain_two_ref[...] = small[1:2, 0:shard]
    router_ref[...] = small[2 : 2 + EXPERTS, 0:shard]
    for k in range(table_ref.shape[0]):
        table_ref[k : k + 1, :] = small[2 + EXPERTS : 3 + EXPERTS, k * heads : (k + 1) * heads]
    part = four_ref.shape[1]
    for c in range(2):

        @pl.when(place_ref[4] == c)
        def _():
            here = slice(c * part, (c + 1) * part)
            there = slice((1 - c) * part, (2 - c) * part)
            for i, ref in enumerate((query_ref, key_ref, value_ref)):
                ref[here, :] = four_ref[i]
                ref[there, :] = other_ref[i].astype(f32)
            out_ref[here, :] = out_mine_ref[...]
            out_ref[there, :] = out_other_ref[...]


def middle_kernel(
    place_ref,
    x_ref,
    out_ref,
    out_other_ref,
    gain_ref,
    router_ref,
    routes_in_ref,
    first_ref,
    second_ref,
    *refs,
    half,
    sub,
    split,
    few,
    share,
):
    pieces = refs[:-11]
    (
        send_ref,
        attended_ref,
        hidden_ref,
        normed_ref,
        probs_ref,
        spread_ref,
        cotangent_ref,
        routes_ref,
        attended,
        stage,
        routes_turned,
    ) = refs[-11:]
    blocks, rows, width = attended.shape
    tokens = blocks * rows
    head_width = width // HEAD_GROUPS
    for k in range(len(pieces) // 2):
        for c in range(2):
            stage[place_ref[5] ^ k, place_ref[4] ^ c] = pieces[2 * k + c][...]
    for g in range(HEAD_GROUPS):
        lanes = slice(g * head_width, (g + 1) * head_width)
        for t in range(split):
            for c in range(2):
                at = c * half + t * sub
                attended[:, at : at + sub, lanes] = stage[g * split + t, c]
    cotangent_ref[place_ref[7]] = first_ref[...]
    cotangent_ref[1 - place_ref[7]] = second_ref[...]
    routes_turned[...] = routes_in_ref[...].T
    block_col = lax.broadcasted_iota(jnp.int32, routes_turned.shape, 1)
    for b in range(blocks):
        mine = block_col == place_ref[6] + b * (len(pieces) // 2)
        column = jnp.sum(jnp.where(mine, routes_turned[...], 0.0), axis=1, keepdims=True)
        routes_ref[b * rows : (b + 1) * rows, :] = column.astype(jnp.int32)
    low = attended[...].reshape(tokens, width)
    attended_ref[...] = low
    out_half = width // 2
    here = pl.multiple_of(place_ref[4] * out_half, LANES)
    there = pl.multiple_of(out_half - place_ref[4] * out_half, LANES)
    hidden_ref[:, pl.ds(here, out_half)] = dot(low, out_ref[...])
    hidden_ref[:, pl.ds(there, out_half)] = dot(low, out_other_ref[...])
    hidden = x_ref[...].reshape(tokens, width).astype(f32) + hidden_ref[...]
    hidden_ref[...] = hidden
    scale = lax.rsqrt(jnp.mean(hidden * hidden, axis=-1, keepdims=True) + EPS)
    normed = ((hidden * scale) * gain_ref[...]).astype(bf16)
    normed_ref[...] = normed
    logits = dot(normed, router_ref[...].astype(bf16), ((1,), (1,)))
    logits = jnp.exp(logits - jnp.max(logits, axis=-1, keepdims=True))
    probs = logits / jnp.sum(logits, axis=-1, keepdims=True)
    probs_ref[...] = probs
    chosen = routes_ref[...]
    picked = (chosen == lax.broadcasted_iota(jnp.int32, (tokens, EXPERTS), 1)).astype(f32)
    gate = jnp.sum(probs * picked, axis=-1, keepdims=True)
    row = lax.broadcasted_iota(jnp.int32, (tokens, tokens), 0)
    col = lax.broadcasted_iota(jnp.int32, (tokens, tokens), 1)
    before = (col < row).astype(bf16)
    earlier = dot(before, picked.astype(bf16))
    slot = jnp.sum(earlier * picked, axis=-1, keepdims=True).astype(jnp.int32)
    spot = chosen * CAP + slot
    spread = (spot == lax.broadcasted_iota(jnp.int32, (tokens, EXPERTS * CAP), 1)).astype(bf16)
    spread_ref[...] = spread
    d_expert = (gate * cotangent_ref[...].reshape(tokens, width).astype(f32)).astype(bf16)
    for i, rows_in in enumerate((normed, d_expert)):
        rows_out = dot(spread, rows_in, ((0,), (0,))).astype(bf16)
        for e in range(EXPERTS):
            for k in range(share):
                send_ref[e * share + k, i * few : (i + 1) * few, :] = rows_out[
                    e * few : (e + 1) * few, :
                ]


def expert_kernel(arrived_ref, up_ref, down_ref, results_ref, act_ref, d_pre_ref, *, few):
    groups, _, width = arrived_ref.shape
    rows = groups * few
    received = arrived_ref[:, 0:few, :].reshape(rows, width)
    got = arrived_ref[:, few:, :].reshape(rows, width)
    root = 0.7978845608028654
    up, down = up_ref[...], down_ref[...]
    pre = dot(received, up)
    square = pre * pre
    bend = jnp.tanh(root * (pre + 0.044715 * (square * pre)))
    side = 0.5 * (1.0 + bend)
    act = (pre * side).astype(bf16)
    slope = side + 0.5 * pre * (1.0 - bend * bend) * (root * (1.0 + 3 * 0.044715 * square))
    d_pre = (dot(got, down, ((1,), (1,))) * slope).astype(bf16)
    act_ref[...] = act
    d_pre_ref[...] = d_pre
    out = dot(act, down).astype(bf16)
    back = dot(d_pre, up, ((1,), (1,))).astype(bf16)
    results_ref[:, 0:few, :] = out.reshape(groups, few, width)
    results_ref[:, few:, :] = back.reshape(groups, few, width)


def turn_kernel(
    place_ref,
    returned_ref,
    spread_ref,
    hidden_ref,
    normed_ref,
    probs_ref,
    routes_ref,
    cotangent_ref,
    gain_ref,
    router_ref,
    out_ref,
    out_other_ref,
    *refs,
    half,
    sub,
    split,
    few,
    share,
):
    pieces = refs[:-9]
    (
        first_ref,
        second_ref,
        d_hidden_ref,
        d_branch_ref,
        router_grad_ref,
        gain_grad_ref,
        output,
        d_attended,
        stage,
    ) = refs[-9:]
    seqs, rows, width = cotangent_ref.shape
    tokens = seqs * rows
    head_width = width // HEAD_GROUPS
    spread = spread_ref[...]

    def collect(at):
        pieces = []
        for e in range(EXPERTS):
            piece = returned_ref[e * share, at, :].astype(f32)
            for k in range(1, share):
                piece = piece + returned_ref[e * share + k, at, :].astype(f32)
            pieces.append(piece)
        value = jnp.concatenate(pieces, axis=0)
        high = value.astype(bf16)
        low = (value - high.astype(f32)).astype(bf16)
        return dot(spread, high) + dot(spread, low)

    expert_out = collect(slice(0, few))
    d_rows = collect(slice(few, 2 * few))
    hidden = hidden_ref[...]
    probs = probs_ref[...]
    picked = (
        routes_ref[...] == lax.broadcasted_iota(jnp.int32, (tokens, EXPERTS), 1)
    ).astype(f32)
    gate = jnp.sum(probs * picked, axis=-1, keepdims=True)
    output[...] = (hidden + gate * expert_out).astype(bf16).reshape(seqs, rows, width)
    first_ref[...] = output[place_ref[7]]
    second_ref[...] = output[1 - place_ref[7]]
    d_final = cotangent_ref[...].reshape(tokens, width).astype(f32)
    d_gate = jnp.sum(d_final * expert_out, axis=-1, keepdims=True)
    d_logits = gate * (picked - probs) * d_gate
    d_normed = d_rows
    for e in range(EXPERTS):
        d_normed = d_normed + d_logits[:, e : e + 1] * router_ref[e : e + 1, :]
    router_grad_ref[...] = lax.dot_general(
        d_logits,
        normed_ref[...].astype(f32),
        (((0,), (0,)), ((), ())),
        precision=lax.Precision.HIGHEST,
        preferred_element_type=f32,
    )
    scale = lax.rsqrt(jnp.mean(hidden * hidden, axis=-1, keepdims=True) + EPS)
    unit = hidden * scale
    gain_grad_ref[...] = jnp.sum(d_normed * unit, axis=0, keepdims=True)
    d_unit = d_normed * gain_ref[...]
    d_hidden = d_final + scale * (d_unit - unit * jnp.mean(d_unit * unit, axis=-1, keepdims=True))
    d_hidden_ref[...] = d_hidden
    d_branch = d_hidden.astype(bf16)
    d_branch_ref[...] = d_branch
    out_half = width // 2
    here = pl.multiple_of(place_ref[4] * out_half, LANES)
    there = pl.multiple_of(out_half - place_ref[4] * out_half, LANES)
    d_low = dot(d_branch_ref[:, pl.ds(here, out_half)], out_ref[...], ((1,), (1,)))
    d_low = d_low + dot(d_branch_ref[:, pl.ds(there, out_half)], out_other_ref[...], ((1,), (1,)))
    d_attended[...] = d_low.astype(bf16).reshape(seqs, rows, width)
    for g in range(HEAD_GROUPS):
        lanes = slice(g * head_width, (g + 1) * head_width)
        for t in range(split):
            for c in range(2):
                at = c * half + t * sub
                stage[g * split + t, c] = d_attended[:, at : at + sub, lanes]
    for k in range(len(pieces) // 2):
        for c in range(2):
            pieces[2 * k + c][...] = stage[place_ref[5] ^ k, place_ref[4] ^ c]


def exchange(value):
    return lax.all_to_all(value, "sq", split_axis=0, concat_axis=0, tiled=True)


def local(
    inputs,
    w_query,
    w_key,
    w_value,
    w_out,
    table,
    gain_one,
    gain_two,
    w_router,
    w_up,
    w_down,
    routes,
    segments,
    cotangent,
):
    seqs, rows, width = inputs.shape
    heads = table.shape[1]
    head_dim = width // heads
    reps = lax.axis_size("rep")
    groups = lax.axis_size("sq")
    length = rows * groups
    tokens = seqs * rows
    share = groups // EXPERTS
    half = rows // 2
    all_seqs = 2 * seqs
    split = groups // (all_seqs * HEAD_GROUPS)
    sub = half // split
    group_heads = heads // HEAD_GROUPS
    head_width = group_heads * head_dim
    shard = w_query.shape[0]
    part = shard // 2
    bucket_rows = table.shape[0]
    core = lax.axis_index("rep") % 2
    me = lax.axis_index("sq")
    group_at = (me // split) % HEAD_GROUPS
    first = core == 0
    pairs = [(i, i ^ 1) for i in range(reps)]

    def swap(value):
        return lax.ppermute(value, "rep", pairs)

    chips = HEAD_GROUPS * split

    def plane(value, k, c):
        if k == 0 and c == 0:
            return value
        moves = [
            (r * groups + q, (r ^ c) * groups + (q ^ k)) for r in range(reps) for q in range(groups)
        ]
        return lax.ppermute(value, ("rep", "sq"), moves)

    def plane_all(pieces):
        return [plane(pieces[2 * k + c], k, c) for k in range(chips) for c in range(2)]

    def to_tokens(value, turn, back):
        moves = []
        for r in range(reps):
            for p in range(groups):
                w = p // chips
                s = seqs * (r % 2) + (w + turn) % 2
                there = (r // 2 * 2 + w // 2) * groups + s * chips + p % chips
                here = r * groups + p
                moves.append((there, here) if back else (here, there))
        return lax.ppermute(value, ("rep", "sq"), moves)

    def by_core(own, other, axis):
        return jnp.where(
            first,
            jnp.concatenate([own, other], axis=axis),
            jnp.concatenate([other, own], axis=axis),
        )

    def mine(value, axis, size):
        return lax.dynamic_slice_in_dim(value, core * size, size, axis)

    def yours(value, axis, size):
        return lax.dynamic_slice_in_dim(value, (1 - core) * size, size, axis)

    def over_pairs(value):
        if reps == 2:
            return value
        sets = [list(range(0, reps, 2)), list(range(1, reps, 2))]
        return lax.psum(value, "rep", axis_index_groups=sets)

    smem = pl.BlockSpec(memory_space=pltpu.SMEM)
    vmem = pl.BlockSpec(memory_space=pltpu.VMEM)

    def cost(microseconds):
        return pl.CostEstimate(
            flops=microseconds * 900_000_000,
            bytes_accessed=microseconds * 1_000_000,
            transcendentals=0,
        )

    limit = pltpu.CompilerParams(vmem_limit_bytes=56 * 1024 * 1024)
    spare = width - 3 * head_width
    query_at = core * half + (me % split) * sub
    inner = me % chips
    first_block = 2 * core * chips + inner
    parity = (me // chips) % 2
    place = jnp.stack(
        [
            core * half,
            query_at,
            group_at * group_heads,
            core * seqs,
            core,
            inner,
            first_block,
            parity,
        ]
    )
    place = place.astype(jnp.int32)
    shard_table = bucket_rows * heads
    marks = jnp.concatenate([segments, routes.reshape(seqs, rows)], axis=1)
    send = pl.pallas_call(
        partial(pack_kernel, split=split),
        name="pack",
        out_shape=jax.ShapeDtypeStruct((groups, part, width), bf16),
        in_specs=[smem] + [vmem] * 9,
        out_specs=vmem,
        scratch_shapes=[
            pltpu.VMEM((HEAD_GROUPS, part, 3 * head_width), f32),
            pltpu.VMEM((part, spare), f32),
        ],
        compiler_params=limit,
        cost_estimate=cost(3),
    )(
        place,
        marks,
        swap(marks),
        w_query,
        w_key,
        w_value,
        gain_one.reshape(1, shard),
        gain_two.reshape(1, shard),
        w_router.T,
        table,
    )
    def half_at(value, turn):
        return lax.dynamic_index_in_dim(value, (parity + turn) % 2, 0, keepdims=False)

    x_first, x_second = [to_tokens(half_at(inputs, turn), turn, False) for turn in range(2)]
    send, x_first, x_second = lax.optimization_barrier((send, x_first, x_second))
    x_tokens = jnp.where(
        parity == 0, jnp.stack([x_first, x_second]), jnp.stack([x_second, x_first])
    )
    x_parts = [x_tokens] + [plane(x_tokens, k, 0) for k in range(1, chips)]
    own = exchange(send)
    out_half = mine(w_out, 1, width // 2)
    out_send = jnp.broadcast_to(out_half[None], (groups, shard, width // 2))
    first, second = [to_tokens(half_at(cotangent, turn), turn, False) for turn in range(2)]
    own, out_send, place, x_parts, first, second = lax.optimization_barrier(
        (own, out_send, place, x_parts, first, second)
    )
    x_parts = x_parts + [swap(v) for v in x_parts]
    other, out_send = lax.optimization_barrier((swap(own), out_send))
    out_mine = exchange(out_send)
    queries_count = groups * sub
    tile = (LANES // rows) * sub
    sizes = dict(groups=groups, half=half, rows=rows, sub=sub, head_dim=head_dim)
    piece = jax.ShapeDtypeStruct((2, sub, head_width), bf16)
    (
        probs,
        queries,
        pair,
        normed_all,
        w_group,
        gain_one_full,
        gain_two_full,
        router_full,
        routes_all,
        *attended_parts,
    ) = pl.pallas_call(
        partial(forward_kernel, shard=shard, all_heads=heads, **sizes),
        name="attention_forward",
        out_shape=(
            jax.ShapeDtypeStruct((group_heads, queries_count, length), bf16),
            jax.ShapeDtypeStruct((queries_count, head_width), bf16),
            jax.ShapeDtypeStruct((length, 2 * head_width), bf16),
            jax.ShapeDtypeStruct((groups, rows, width), bf16),
            jax.ShapeDtypeStruct((width, 3 * head_width), bf16),
            jax.ShapeDtypeStruct((1, width), f32),
            jax.ShapeDtypeStruct((1, width), f32),
            jax.ShapeDtypeStruct((EXPERTS, width), f32),
            jax.ShapeDtypeStruct((groups, rows), f32),
        )
        + (piece,) * (2 * chips),
        in_specs=[smem] + [vmem] * (2 + 2 * chips),
        out_specs=[vmem] * (9 + 2 * chips),
        scratch_shapes=[
            pltpu.VMEM((groups, shard, 3 * head_width), f32),
            pltpu.VMEM((groups, rows, 3 * head_width), bf16),
            pltpu.VMEM((queries_count, length), f32),
            pltpu.VMEM((tile, 2 * length - LANES), f32),
            pltpu.VMEM((1, length), f32),
            pltpu.VMEM((queries_count, 1), f32),
            pltpu.VMEM((32, heads), f32),
            pltpu.VMEM((queries_count, head_width), bf16),
        ],
        compiler_params=limit,
        cost_estimate=cost(60),
    )(place, own, other, *x_parts)
    attended_parts, out_mine = lax.optimization_barrier((attended_parts, out_mine))
    back = plane_all(attended_parts)
    out_mine = out_mine.reshape(width, width // 2)
    out_yours = swap(out_mine)
    few = CAP
    pieces = dict(half=half, sub=sub, split=split, few=few)
    (
        buffer,
        attended,
        hidden,
        normed_two,
        router_probs,
        spread,
        cotangent_tokens,
        routes_tokens,
    ) = pl.pallas_call(
        partial(middle_kernel, share=share, **pieces),
        name="router_and_dispatch",
        out_shape=(
            jax.ShapeDtypeStruct((groups, 2 * few, width), bf16),
            jax.ShapeDtypeStruct((tokens, width), bf16),
            jax.ShapeDtypeStruct((tokens, width), f32),
            jax.ShapeDtypeStruct((tokens, width), bf16),
            jax.ShapeDtypeStruct((tokens, EXPERTS), f32),
            jax.ShapeDtypeStruct((tokens, EXPERTS * CAP), bf16),
            jax.ShapeDtypeStruct((seqs, rows, width), bf16),
            jax.ShapeDtypeStruct((tokens, 1), jnp.int32),
        ),
        in_specs=[smem] + [vmem] * (8 + 2 * chips),
        out_specs=[vmem] * 8,
        scratch_shapes=[
            pltpu.VMEM((seqs, rows, width), bf16),
            pltpu.VMEM((chips, 2, seqs, sub, head_width), bf16),
            pltpu.VMEM((rows, groups), f32),
        ],
        compiler_params=limit,
        cost_estimate=cost(5),
    )(
        place,
        x_tokens,
        out_mine,
        out_yours,
        gain_two_full,
        router_full,
        routes_all,
        first,
        second,
        *back,
    )
    arrived = exchange(buffer)
    expert_rows = groups * few
    units_low = jax.ShapeDtypeStruct((expert_rows, w_up.shape[1]), bf16)
    results, act, d_pre = pl.pallas_call(
        partial(expert_kernel, few=few),
        name="experts",
        out_shape=(
            jax.ShapeDtypeStruct((groups, 2 * few, width), bf16),
            units_low,
            units_low,
        ),
        in_specs=[vmem] * 3,
        out_specs=[vmem] * 3,
        compiler_params=limit,
        cost_estimate=cost(8),
    )(arrived, w_up, w_down)
    returned = exchange(results)
    received = arrived[:, :few].reshape(expert_rows, width)
    got = arrived[:, few:].reshape(expert_rows, width)
    up_local = dot(received, d_pre, ((0,), (0,))).astype(bf16)
    down_local = dot(act, got, ((0,), (0,))).astype(bf16)

    def both_reps(value):
        if reps == 2:
            return value.astype(f32) + swap(value).astype(f32)
        return lax.psum(value, "rep").astype(f32)

    returned, up_local, down_local = lax.optimization_barrier((returned, up_local, down_local))
    *d_parts, out_first, out_second, d_hidden, d_branch, router_grad, gain_two_grad = pl.pallas_call(
        partial(turn_kernel, share=share, **pieces),
        name="combine_and_turn",
        out_shape=[piece] * (2 * chips)
        + [
            jax.ShapeDtypeStruct((rows, width), bf16),
            jax.ShapeDtypeStruct((rows, width), bf16),
            jax.ShapeDtypeStruct((tokens, width), f32),
            jax.ShapeDtypeStruct((tokens, width), bf16),
            jax.ShapeDtypeStruct((EXPERTS, width), f32),
            jax.ShapeDtypeStruct((1, width), f32),
        ],
        in_specs=[smem] + [vmem] * 11,
        out_specs=[vmem] * (6 + 2 * chips),
        scratch_shapes=[
            pltpu.VMEM((seqs, rows, width), bf16),
            pltpu.VMEM((seqs, rows, width), bf16),
            pltpu.VMEM((chips, 2, seqs, sub, head_width), bf16),
        ],
        compiler_params=limit,
        cost_estimate=cost(5),
    )(
        place,
        returned,
        spread,
        hidden,
        normed_two,
        router_probs,
        routes_tokens,
        cotangent_tokens,
        gain_two_full,
        router_full,
        out_mine,
        out_yours,
    )
    grads = plane_all(d_parts)
    out_send = pl.pallas_call(
        partial(out_grad_kernel, groups=groups, shard=shard),
        name="out_grad",
        out_shape=jax.ShapeDtypeStruct((groups, part, width), bf16),
        in_specs=[smem] + [vmem] * 4,
        out_specs=vmem,
        scratch_shapes=[pltpu.VMEM((groups, shard, width), f32)],
        compiler_params=limit,
        cost_estimate=cost(3),
    )(place, attended, swap(attended), d_branch, swap(d_branch))
    grads, out_send = lax.optimization_barrier((grads, out_send))
    out_back = exchange(out_send)
    d_all, table_part = pl.pallas_call(
        partial(backward_kernel, **sizes),
        name="attention_backward",
        out_shape=(
            jax.ShapeDtypeStruct((groups, rows, 3 * head_width), bf16),
            jax.ShapeDtypeStruct((group_heads, groups * bucket_rows, LANES), f32),
        ),
        in_specs=[smem] + [vmem] * (3 + 2 * chips),
        out_specs=[vmem] * 2,
        scratch_shapes=[
            pltpu.VMEM((queries_count, length), f32),
            pltpu.VMEM((queries_count, length), bf16),
            pltpu.VMEM((tile, 2 * length - LANES), f32),
            pltpu.VMEM((2 * head_width, length), f32),
            pltpu.VMEM((queries_count, head_width), f32),
            pltpu.VMEM((queries_count, head_width), bf16),
        ],
        compiler_params=limit,
        cost_estimate=cost(1),
    )(place, probs, queries, pair, *grads)
    down_grad = both_reps(down_local)
    d_all, out_back, down_grad = lax.optimization_barrier((d_all, out_back, down_grad))
    d_all_other = swap(d_all)
    out_first = to_tokens(out_first, 0, True)
    out_second = to_tokens(out_second, 1, True)
    out_sum = jnp.sum(out_back.astype(f32), axis=0)
    out_sum = over_pairs(out_sum)
    out_other = swap(out_sum)
    d_normed_parts, d_sum, gain_one_part = pl.pallas_call(
        partial(rows_kernel, half=half),
        name="d_normed",
        out_shape=[
            jax.ShapeDtypeStruct((chips, groups // chips, half, width), bf16),
            jax.ShapeDtypeStruct((groups, rows, 3 * head_width), bf16),
            jax.ShapeDtypeStruct((1, width), f32),
        ],
        in_specs=[smem] + [vmem] * 5,
        out_specs=[vmem] * 3,
        compiler_params=limit,
        cost_estimate=cost(1),
    )(place, d_all, d_all_other, w_group, normed_all, gain_one_full)
    last = pl.pallas_call(
        partial(weight_kernel, shard=shard, all_heads=heads),
        name="weight_grads",
        out_shape=jax.ShapeDtypeStruct((groups, part, width), bf16),
        in_specs=[smem] + [vmem] * 6,
        out_specs=vmem,
        scratch_shapes=[
            pltpu.VMEM((groups, shard, 3 * head_width), f32),
            pltpu.VMEM((groups, part, spare), f32),
        ],
        compiler_params=limit,
        cost_estimate=cost(8),
    )(place, d_sum, normed_all, gain_one_part, gain_two_grad, router_grad, table_part)
    planes = [list(range(q, q + chips)) for q in range(0, groups, chips)]
    d_normed_parts = lax.all_to_all(
        d_normed_parts, "sq", 0, 0, axis_index_groups=planes, tiled=True
    )
    last, d_normed_parts, out_first, out_second = lax.optimization_barrier(
        (last, d_normed_parts, out_first, out_second)
    )
    final = exchange(last)
    d_keep, d_give = pl.pallas_call(
        total_kernel,
        name="d_normed_total",
        out_shape=[
            jax.ShapeDtypeStruct((seqs, half, width), f32),
            jax.ShapeDtypeStruct((seqs, half, width), bf16),
        ],
        in_specs=[smem, vmem],
        out_specs=[vmem] * 2,
        compiler_params=limit,
        cost_estimate=cost(1),
    )(place, d_normed_parts)
    grad_first, grad_second = pl.pallas_call(
        partial(token_kernel, half=half),
        name="token_grad",
        out_shape=[jax.ShapeDtypeStruct((rows, width), bf16)] * 2,
        in_specs=[smem] + [vmem] * 5,
        out_specs=[vmem] * 2,
        scratch_shapes=[pltpu.VMEM((seqs, rows, width), f32)] * 2,
        compiler_params=limit,
        cost_estimate=cost(2),
    )(place, x_tokens, d_hidden, gain_one_full, d_keep, swap(d_give))
    grad_first = to_tokens(grad_first, 0, True)
    grad_second = to_tokens(grad_second, 1, True)
    up_grad = both_reps(up_local)
    final, grad_first, grad_second, up_grad = lax.optimization_barrier(
        (final, grad_first, grad_second, up_grad)
    )
    four, four_low, small_sum = pl.pallas_call(
        partial(sum_kernel, seqs=seqs),
        name="sums",
        out_shape=(
            jax.ShapeDtypeStruct((3, part, width), f32),
            jax.ShapeDtypeStruct((3, part, width), bf16),
            jax.ShapeDtypeStruct((part, spare), f32),
        ),
        in_specs=[vmem],
        out_specs=[vmem] * 3,
        compiler_params=limit,
        cost_estimate=cost(2),
    )(final)
    if reps > 2:
        four, small_sum = over_pairs(four), over_pairs(small_sum)
        four_low = four.astype(bf16)
    (
        output,
        input_grad,
        query_grad,
        key_grad,
        value_grad,
        out_grad,
        table_grad,
        gain_one_grad,
        gain_two_grad,
        router_grad,
    ) = pl.pallas_call(
        input_kernel,
        name="input_grad",
        out_shape=(
            jax.ShapeDtypeStruct((seqs, rows, width), bf16),
            jax.ShapeDtypeStruct((seqs, rows, width), f32),
        )
        + (jax.ShapeDtypeStruct((shard, width), f32),) * 4
        + (
            jax.ShapeDtypeStruct((bucket_rows, heads), f32),
            jax.ShapeDtypeStruct((1, shard), f32),
            jax.ShapeDtypeStruct((1, shard), f32),
            jax.ShapeDtypeStruct((EXPERTS, shard), f32),
        ),
        in_specs=[smem] + [vmem] * 10,
        out_specs=[vmem] * 10,
        compiler_params=limit,
        cost_estimate=cost(2),
    )(
        place,
        grad_first,
        grad_second,
        out_first,
        out_second,
        four,
        swap(four_low),
        out_sum,
        out_other,
        small_sum,
        swap(small_sum),
    )
    return (
        output,
        input_grad,
        query_grad,
        key_grad,
        value_grad,
        out_grad,
        table_grad,
        gain_one_grad.reshape(shard),
        gain_two_grad.reshape(shard),
        router_grad.T,
        up_grad,
        down_grad,
    )


def solution(mesh):
    in_specs = (
        P("rep", "sq", None),
        P("sq", None),
        P("sq", None),
        P("sq", None),
        P("sq", None),
        P("sq", None),
        P("sq"),
        P("sq"),
        P("sq", None),
        P(None, "sq"),
        P("sq", None),
        P("rep", "sq", None),
        P("rep", "sq"),
        P("rep", "sq", None),
    )
    out_specs = (
        P("rep", "sq", None),
        P("rep", "sq", None),
        P("sq", None),
        P("sq", None),
        P("sq", None),
        P("sq", None),
        P("sq", None),
        P("sq"),
        P("sq"),
        P("sq", None),
        P(None, "sq"),
        P("sq", None),
    )
    return jax.shard_map(local, mesh=mesh, in_specs=in_specs, out_specs=out_specs, check_vma=False)
```
